256 devices in a mesh: sec: 4 (over x_lo, core), col: 64 (over y, x_hi, z).
Axes of the slice: x: 4 (x_hi: 2, x_lo: 2; x = x_hi * 2 + x_lo), y: 4, z: 8, core: 2. Of those that a mesh axis runs over, the one named last changes fastest.
Arguments:
- column_state: float32 [16384, 128], P('col'), may hold values from -6 to 6
- mixing_rate: float32 [128], replicated, may hold values from 0.05 to 0.2
- neighbours: int32 [4096, 4], P('col'), may hold values from 0 to 4095, as said below
- assignment: int32 [16384, 1], P('col'), may hold values from 0 to 191; in each aligned block of 256 rows (0 to 255, 256 to 511, ...) at most 2 rows name the same one
- substeps: int32 [16384], P('col'), may hold values from 1 to 4
- cloud_state: bfloat16 [4, 2, 58, 32, 8192], P('sec', None, None, None, 'col'), may hold values from -6 to 6
- level_map: float32 [58, 64], replicated, may hold values from -0.75 to 0.75
- saturation: float32 [58], replicated, may hold values from -0.5 to 0.5
Outputs:
- new_columns: float32 [16384, 128], P('col')
- new_cloud_state: bfloat16 [4, 2, 58, 32, 8192], P('sec', None, None, None, 'col')
The draws below stay inside these ranges and needn't reach their ends.
Inputs may be any that keep to these rules, and one draw needn't show every extreme that they name: `neighbours`: each neighbour lies within 64 elements of its own element in the order of elements that wraps around, and some lie exactly 64 away. `assignment`: in each aligned block of 256 columns no cloud device is named by more than 2 columns, and in some block one is named by exactly 2.
All inputs are finite; a program needn't handle non-finite values.
Results may differ from the reference program's by a relative error of at most 0.001.
Values sent between devices are 32-bit elements; how exact they have to be, the bound alone decides.
A program may use at most 64 MiB of HBM per device.

```python
import math
import jax
import jax.numpy as jnp
import numpy as np
from jax import lax

CH = 256
LEV = 64
FIELDS = 2
CZ = 58
CX = 32
MAX_SUB = 4
EH = 64
NELEM = 4096
NCOLS = 16384
CAP = 2
N_SEC = 4
N_COL = 64


def draw_neighbours(key, part):
    first_key, second_key = jax.random.split(jax.random.fold_in(key, 71))
    reach = jax.random.randint(first_key, (NELEM, 4), 1, EH + 1)
    orient = jax.random.randint(second_key, (NELEM, 4), 0, 2) * 2 - 1
    offset = reach * orient
    element = jnp.arange(NELEM, dtype=jnp.int32)
    corner = jnp.arange(4, dtype=jnp.int32)
    offset = jnp.where((element[:, None] % 64 == 0) & (corner[None, :] == 0), EH, offset)
    return jnp.mod(element[:, None] + offset, NELEM).astype(jnp.int32)


def set_ends(result, rng, least, high):
    dims = result.shape
    place = [jax.random.randint(jax.random.fold_in(rng, axis), (), 0, dims[axis]) for axis in range(len(dims))]
    result = result.at[tuple(place)].set(least)
    longest = dims.index(max(dims))
    place[longest] = (place[longest] + 1) % dims[longest]
    return result.at[tuple(place)].set(high)


def block_scale(key, shape, pieces, low, largest):
    level, own = 1.0, jax.random.fold_in(key, 6)
    for position, shards_of in pieces:
        heights = jnp.exp(jax.random.uniform(jax.random.fold_in(own, position), (shards_of,), jnp.float32, low / len(pieces), largest / len(pieces)))
        level = level * jnp.repeat(heights, shape[position] // shards_of).reshape([-1 if axis == position else 1 for axis in range(len(shape))])
    return level


def routed_block(own_key, own, number, rows, number_of, top, limit, lean):
    order = jax.random.permutation(own_key, number_of)
    heavy_load, usual = load_shares(number_of, rows * top, limit, lean, True), load_shares(number_of, rows * top, limit, lean, False)
    places = jnp.arange(number_of)

    def named(tallies, turn):
        used = int((tallies > 0).sum())
        fixed = max(1, used // 4)
        moved = fixed + (places - fixed + turn * (used - fixed)) % max(1, number_of - fixed)
        return jnp.zeros((number_of,), jnp.int32).at[order[jnp.where(places < fixed, places, moved)]].set(jnp.asarray(tallies, jnp.int32))

    tallies = jnp.where(number % 4 == 0, named(heavy_load, number // 4), named(usual, number - number // 4 - 1))
    mixed = jax.random.permutation(jax.random.fold_in(own, 3), number_of)
    donor, taker = mixed[0:number_of // 2 * 2:2], mixed[1:number_of // 2 * 2:2]
    slack = jnp.minimum(tallies[donor] - 1, limit - tallies[taker]) // 2
    slack = jnp.where((donor == order[0]) | (taker == order[0]) | (tallies[taker] == 0), 0, jnp.maximum(slack, 0))
    moved = jax.random.randint(jax.random.fold_in(own, 4), (number_of // 2,), 0, 1 << 20) % (slack + 1)
    tallies = tallies.at[donor].add(-moved).at[taker].add(moved)
    members = jnp.searchsorted(jnp.cumsum(tallies), jnp.arange(rows * top), side="right").astype(jnp.int32)
    listing = members.reshape(top, rows).T
    listing = listing[jax.random.permutation(jax.random.fold_in(own, 1), rows)]
    turn = jax.random.randint(jax.random.fold_in(own, 2), (rows, 1), 0, top)
    return jnp.take_along_axis(listing, (jnp.arange(top)[None, :] + turn) % top, axis=1)


def load_shares(amount, total, most, lean, full):
    loads = [(1 << 20) // math.isqrt(standing ** lean) + 1 for standing in range(1, amount + 1)]
    largest = most if full else min(most, max(-(-total // amount), total * loads[0] // sum(loads)))
    least = 1 if total - largest >= amount - 1 else 0
    given, spare = [largest] + [least] * (amount - 1), total - largest - least * (amount - 1)
    while spare > 0:
        candidates = [i for i in range(1, amount) if given[i] < largest] or [i for i in range(1, amount) if given[i] < most]
        mass, left = sum([loads[i] for i in candidates]), spare
        for i in candidates:
            extra = min(most - given[i], max(1, left * loads[i] // mass), spare)
            given[i] = given[i] + extra
            spare = spare - extra
    return np.array(given)


def gaussian(key, dims, deviation, most, shards=(), kind=jnp.bfloat16):
    factor_of = block_scale(key, dims, shards, -0.22, 0.18) if shards else 1.0
    result = jax.random.normal(key, dims, jnp.float32) * deviation * factor_of
    return jnp.minimum(jnp.maximum(result, -most), most).astype(kind)


def setup_inputs(seed: int = 0) -> dict:
    seeds = jax.random.split(jax.random.key(seed), 9)
    column_state = gaussian(seeds[0], (NCOLS, FIELDS * LEV), 1.0, 6.0, ((0, 64),), jnp.float32)
    mixing_rate = jnp.clip(jnp.exp(jax.random.uniform(seeds[1], (FIELDS * LEV,), jnp.float32, math.log(0.05), math.log(0.2))), 0.05, 0.2)
    neighbours = draw_neighbours(jax.random.fold_in(seeds[8], 71), 0)
    assignment_keys = jax.random.split(jax.random.fold_in(seeds[3], 1), NCOLS // CH)
    assignment_turns = jax.random.permutation(jax.random.fold_in(seeds[3], 3), NCOLS // CH)
    assignment = jax.vmap(lambda own, number: routed_block(jax.random.fold_in(seeds[3], 2), own, number, CH, (N_SEC - 1) * N_COL, 1, CAP, 2))(assignment_keys, assignment_turns).reshape((NCOLS, 1))
    substeps = set_ends(jax.random.randint(seeds[4], (NCOLS,), 1, 5), jax.random.fold_in(seeds[4], 1), 1, 4).astype(jnp.int32)
    cloud_state = gaussian(seeds[5], (N_SEC, FIELDS, CZ, CX, N_COL * N_COL * CAP), 1.0, 6.0, ((0, 4), (4, 64)))
    level_map = gaussian(seeds[6], (CZ, LEV), LEV ** -0.5, 0.75, (), jnp.float32)
    saturation = jnp.clip(jax.random.uniform(seeds[7], (CZ,), jnp.float32, -0.5, 0.5), -0.5, 0.5)
    return dict(column_state=column_state, mixing_rate=mixing_rate, neighbours=neighbours, assignment=assignment, substeps=substeps, cloud_state=cloud_state, level_map=level_map, saturation=saturation)


RELAX = 0.25
HORIZ = 0.12
VERTIC = 0.1
LATENT = 2.5
VMIX = 0.2
HIGH = lax.Precision.HIGHEST


def vertical_term(values, levels):
    shaped = values.reshape(values.shape[0], -1, levels)
    upper = jnp.concatenate([shaped[:, :, 1:], shaped[:, :, -1:]], axis=2)
    lower = jnp.concatenate([shaped[:, :, :1], shaped[:, :, :-1]], axis=2)
    return (upper + lower - 2.0 * shaped).reshape(values.shape)


def advance(columns, mixing_rate, element_means, near_ids, own_means, levels):
    spread = jnp.sum(element_means[near_ids], axis=1) - 4.0 * own_means
    return columns + mixing_rate[None, :] * jnp.repeat(spread, 4, axis=0) + VMIX * vertical_term(columns, levels)


def slot_ranks(targets, destinations):
    onehot = (targets[:, None] == jnp.arange(destinations, dtype=jnp.int32)[None, :]).astype(jnp.int32)
    running = jnp.cumsum(onehot, axis=0) - 1
    return jnp.sum(running * onehot, axis=1).astype(jnp.int32)


def cloud_substep(fields, target, saturation):
    mean_now = jnp.mean(fields, axis=2)
    fields = fields + RELAX * (target - mean_now)[:, :, None, :]
    across = jnp.roll(fields, 1, axis=2) + jnp.roll(fields, -1, axis=2) - 2.0 * fields
    upper = jnp.concatenate([fields[:, 1:], fields[:, -1:]], axis=1)
    lower = jnp.concatenate([fields[:, :1], fields[:, :-1]], axis=1)
    fields = fields + HORIZ * across + VERTIC * (upper + lower - 2.0 * fields)
    condensed = 0.5 * jnp.maximum(fields[1] - saturation[:, None, None], 0.0)
    return jnp.stack([fields[0] + LATENT * condensed, fields[1] - condensed])


def run_cloud(block, columns, counts, level_map, saturation, levels):
    shaped = columns.reshape(columns.shape[0], -1, levels)
    target = jnp.einsum("zl,sfl->fzs", level_map, shaped, precision=HIGH)
    start = block.astype(jnp.float32)
    fields = start
    for substep_index in range(MAX_SUB):
        stepped = cloud_substep(fields, target, saturation)
        fields = jnp.where((counts > substep_index)[None, None, None, :], stepped, fields)
    change = jnp.mean(fields, axis=2) - jnp.mean(start, axis=2)
    tendency = jnp.einsum("zl,fzs->sfl", level_map, change, precision=HIGH).reshape(columns.shape[0], -1)
    return fields.astype(jnp.bfloat16), tendency


def reference(column_state, mixing_rate, neighbours, assignment, substeps, cloud_state, level_map, saturation):
    levels = level_map.shape[1]
    width = column_state.shape[1]
    element_means = jnp.mean(column_state.reshape(-1, 4, width), axis=1)
    advanced = advance(column_state, mixing_rate, element_means, neighbours, element_means, levels)
    clouds = (N_SEC - 1) * N_COL
    per_device = N_COL * CAP
    targets = assignment[:, 0].astype(jnp.int32)
    ranks = jax.vmap(slot_ranks, in_axes=(0, None))(targets.reshape(N_COL, CH), clouds).reshape(-1)
    host_ids = jnp.arange(N_COL * CH, dtype=jnp.int32) // CH
    flat = (targets * per_device + host_ids * CAP + ranks).astype(jnp.int32)
    slot_columns = jnp.zeros((clouds * per_device, width), jnp.float32).at[flat].set(advanced)
    slot_counts = jnp.zeros((clouds * per_device,), jnp.int32).at[flat].set(substeps)
    zero_index = jnp.zeros((), jnp.int32)

    def one_block(index):
        sec_index = (index // N_COL + 1).astype(jnp.int32)
        col_index = (index % N_COL).astype(jnp.int32)
        block = lax.dynamic_slice(cloud_state, (sec_index, zero_index, zero_index, zero_index, (col_index * per_device).astype(jnp.int32)), (1,) + cloud_state.shape[1:4] + (per_device,))[0]
        block_columns = lax.dynamic_slice_in_dim(slot_columns, (index * per_device).astype(jnp.int32), per_device, 0)
        block_counts = lax.dynamic_slice_in_dim(slot_counts, (index * per_device).astype(jnp.int32), per_device, 0)
        return run_cloud(block, block_columns, block_counts, level_map, saturation, levels)

    new_blocks, tendencies = lax.map(one_block, jnp.arange(clouds, dtype=jnp.int32))
    shape_inner = cloud_state.shape[1:4]
    new_blocks = new_blocks.reshape((N_SEC - 1, N_COL) + shape_inner + (per_device,))
    new_blocks = jnp.transpose(new_blocks, (0, 2, 3, 4, 1, 5)).reshape((N_SEC - 1,) + shape_inner + (N_COL * per_device,))
    new_cloud_state = jnp.concatenate([cloud_state[:1], new_blocks], axis=0)
    summed = advanced + tendencies.reshape(-1, width)[flat]
    is_water = (jnp.arange(width) // levels == 1)[None, :]
    new_columns = jnp.where(is_water, jnp.maximum(summed, 0.0), summed)
    return new_columns, new_cloud_state
```

```python
import functools

import jax
import jax.numpy as jnp
from jax import lax
from jax.experimental import pallas as pl
from jax.experimental.pallas import tpu as pltpu
from jax.sharding import PartitionSpec as P

MAX_SUB = 4
RELAX = 0.25
HORIZ = 0.12
VERTIC = 0.1
LATENT = 2.5
VMIX = 0.2
MESH = pl.DeviceIdType.MESH
F32 = jnp.float32
BF16 = jnp.bfloat16
I32 = jnp.int32
NN = (((1,), (0,)), ((), ()))
NT = (((1,), (1,)), ((), ()))


def iota(shape, dim):
    return lax.broadcasted_iota(I32, shape, dim)


def halves(x):
    hi = x.astype(BF16)
    return hi, (x - hi.astype(F32)).astype(BF16)


def dot(a, b, dims=NN):
    return lax.dot_general(a, b, dims, preferred_element_type=F32)


def pick(exact, x, dims=NN):
    hi, lo = halves(x)
    return dot(exact, hi, dims) + dot(exact, lo, dims)


def dot3(x, y, dims=NN):
    xh, xl = halves(x)
    yh, yl = halves(y)
    return dot(xh, yh, dims) + (dot(xh, yl, dims) + dot(xl, yh, dims))


def kernel(
    sizes,
    cs_ref,
    rate_ref,
    nbr_ref,
    asg_ref,
    cnt_ref,
    cloud_ref,
    map_ref,
    sat_ref,
    out_ref,
    new_cloud_ref,
    block,
    plain,
    state,
    parts,
    shift_rows,
    square,
    means,
    halo,
    disp_send,
    disp_recv,
    tend_send,
    tends,
    adv_ref,
    local_sem,
    halo_send_sem,
    halo_recv_sem,
    disp_send_sem,
    disp_recv_sem,
    tend_send_sem,
    tend_recv_sem,
    group_send_sem,
    group_recv_sem,
):
    n_sec, n_col = sizes
    sec, col = lax.axis_index("sec"), lax.axis_index("col")
    rows, width = cs_ref.shape
    elements = rows // 4
    total = elements * n_col
    cap, slots = disp_send.shape[1], n_col * disp_send.shape[1]
    levels_c, levels_h = map_ref.shape
    left, right = lax.rem(col + n_col - 1, n_col), lax.rem(col + 1, n_col)
    is_cloud = sec > 0

    barrier = pltpu.get_barrier_semaphore()

    for step in range(1, n_sec):
        pl.semaphore_signal(
            barrier, inc=1, device_id=(lax.rem(sec + step, n_sec), col), device_id_type=MESH
        )

    @pl.when(is_cloud)
    def _():
        def greet(step, carry):
            pl.semaphore_signal(
                barrier, inc=1, device_id=(sec, lax.rem(col + step, n_col)), device_id_type=MESH
            )
            return carry

        lax.fori_loop(1, n_col, greet, 0)

    @pl.when(jnp.logical_not(is_cloud))
    def _():
        for other in (left, right):
            pl.semaphore_signal(barrier, inc=1, device_id=(sec, other), device_id_type=MESH)

    fetch = pltpu.make_async_copy(cloud_ref.at[0], block, local_sem.at[0])
    fetch.start()

    own = (
        cs_ref[pl.ds(0, elements, stride=4), :]
        + cs_ref[pl.ds(1, elements, stride=4), :]
        + cs_ref[pl.ds(2, elements, stride=4), :]
        + cs_ref[pl.ds(3, elements, stride=4), :]
    ) * 0.25
    means[...] = own

    @pl.when(is_cloud)
    def _():
        pl.semaphore_wait(barrier, n_sec - 1 + n_col - 1)

    @pl.when(jnp.logical_not(is_cloud))
    def _():
        pl.semaphore_wait(barrier, n_sec - 1 + 2)

    to_right = pltpu.make_async_remote_copy(
        src_ref=means, dst_ref=halo.at[0], send_sem=halo_send_sem.at[0], recv_sem=halo_recv_sem.at[0],
        device_id=(sec, right), device_id_type=MESH,
    )
    to_left = pltpu.make_async_remote_copy(
        src_ref=means, dst_ref=halo.at[1], send_sem=halo_send_sem.at[1], recv_sem=halo_recv_sem.at[1],
        device_id=(sec, left), device_id_type=MESH,
    )
    to_right.start()
    to_left.start()

    asg = asg_ref[...]
    asg_column = jnp.transpose(jnp.broadcast_to(asg.astype(F32), (128, rows)))[:, 0:1]
    same = (asg_column == asg.astype(F32)) & (iota((rows, rows), 0) < iota((rows, rows), 1))
    rank = jnp.max(jnp.where(same, 1.0, 0.0), axis=0, keepdims=True)
    slot = (asg * cap).astype(F32) + rank
    slot_column = jnp.transpose(jnp.broadcast_to(slot, (128, rows)))[:, 0:1]

    place = iota((3 * elements, elements), 0)
    place = jnp.where(
        place < elements, place, jnp.where(place < 2 * elements, place + elements, place - elements)
    )
    near = jnp.where(place == elements + iota((3 * elements, elements), 1), -4.0, 0.0)
    relative = jnp.bitwise_and(nbr_ref[...] - (col - 1) * elements, total - 1)
    for k in range(4):
        near = near + jnp.where(relative[k : k + 1, :] == place, 1.0, 0.0)
    near_t = near.astype(BF16)
    near_e = jnp.transpose(
        jnp.concatenate([near, jnp.zeros((3 * elements, 128 - elements), F32)], axis=1)
    )[:elements].astype(BF16)

    cs = cs_ref[...]
    lane = jnp.bitwise_and(iota((rows, width), 1), levels_h - 1)
    upper = jnp.where(lane == levels_h - 1, cs, pltpu.roll(cs, width - 1, axis=1))
    lower = jnp.where(lane == 0, cs, pltpu.roll(cs, 1, axis=1))
    base = cs + VMIX * (upper + lower - 2.0 * cs)
    rate = rate_ref[...]

    square[...] = jnp.zeros_like(square)
    square[0:levels_c, 0:levels_h] = map_ref[...]
    square[levels_h : levels_h + levels_c, levels_h : 2 * levels_h] = map_ref[...]

    @pl.when(is_cloud)
    def _():
        chosen = iota((slots, rows), 0) + (sec - 1) * slots == slot.astype(I32)
        chosen32 = jnp.where(chosen, 1.0, 0.0)
        chosen16 = chosen32.astype(BF16)
        counts = jnp.sum(chosen32 * cnt_ref[...].astype(F32), axis=1, keepdims=True)
        repeat = jnp.where(
            iota((elements, rows), 0) == lax.shift_right_logical(iota((elements, rows), 1), 2), 1.0, 0.0
        ).astype(BF16)
        by_element = dot(chosen16, repeat, NT).astype(BF16)
        reach = dot(by_element, near_t, NT).astype(BF16)
        known = pick(chosen16, base) + rate * pick(reach[:, 2 * elements :], own)
        reach = reach[:, : 2 * elements]

        to_right.wait_recv()
        to_left.wait_recv()
        outside = halo[...].reshape(2 * elements, width)
        sent = known + rate * pick(reach, outside)
        target = dot3(sent, square[...], NT)
        target = jnp.where(iota((slots, width), 1) == levels_c, counts, target)
        disp_send[...] = target.reshape(n_col, cap, width)

        def send(step, carry):
            other = lax.rem(col + step, n_col)
            pltpu.make_async_remote_copy(
                src_ref=disp_send.at[other], dst_ref=disp_recv.at[col],
                send_sem=disp_send_sem, recv_sem=disp_recv_sem,
                device_id=(sec, other), device_id_type=MESH,
            ).start()
            return carry

        lax.fori_loop(1, n_col, send, 0)
        pltpu.make_async_copy(disp_send.at[col], disp_recv.at[col], disp_recv_sem).start()

        fetch.wait()
        parts[...] = jnp.zeros_like(parts)

        for f in range(2):

            def widen(z, carry, f=f):
                x = block[f, z].astype(F32)
                plain[f, z] = x
                parts[f, z] = (x[0:8] + x[8:16]) + (x[16:24] + x[24:32])
                return carry

            lax.fori_loop(0, levels_c, widen, 0, unroll=2)

        def strided(f, z):
            return tuple(plain[f, z, pl.ds(k, 8, stride=4), :] for k in range(4))

        def packed(f, z):
            return tuple(state[f, z, pl.ds(8 * k, 8), :] for k in range(4))

        def stencil(here, below, above):
            west = (pltpu.roll(here[3], 1, axis=0),) + here[:3]
            east = here[1:] + (pltpu.roll(here[0], 7, axis=0),)
            return tuple(
                (1.0 - 2.0 * HORIZ - 2.0 * VERTIC) * here[k]
                + HORIZ * (east[k] + west[k])
                + VERTIC * (above[k] + below[k])
                for k in range(4)
            )

        for f in range(2):

            def first(z, carry, f=f):
                below, here = carry
                above = strided(f, jnp.minimum(z + 1, levels_c - 1))
                new = stencil(here, below, above)
                for k in range(4):
                    state[f, z, pl.ds(8 * k, 8), :] = new[k]
                return here, above

            edge = strided(f, 0)
            lax.fori_loop(0, levels_c, first, (edge, edge), unroll=2)

        columns_inv = 1.0 / plain.shape[2]
        start = [jnp.sum(parts[f], axis=1) * columns_inv for f in range(2)]
        level = iota((levels_h, slots), 0)

        def vertical(x):
            up = jnp.where(level == levels_c - 1, x, pltpu.roll(x, levels_h - 1, axis=0))
            low = jnp.where(level == 0, x, pltpu.roll(x, 1, axis=0))
            return VERTIC * (up + low - 2.0 * x)

        pltpu.make_async_copy(disp_recv, disp_recv, disp_recv_sem).wait()
        arrived = jnp.transpose(disp_recv[...].reshape(slots, width))
        counts = arrived[levels_c : levels_c + 1, :]
        goal = [arrived[f * levels_h : (f + 1) * levels_h] for f in range(2)]
        mean = list(start)

        def condense(a, f_shift, z, keep, old):
            half = 0.5 * sat_ref[z]
            new0, new1, drop = [], [], []
            for k in range(4):
                water = a[1][k] + f_shift[1]
                c = jnp.maximum(0.5 * water - half, 0.0)
                new1.append(jnp.where(keep, water - c, old[1][k]))
                new0.append(jnp.where(keep, (a[0][k] + f_shift[0]) + LATENT * c, old[0][k]))
                drop.append(c)
            parts[0, z] = (drop[0] + drop[1]) + (drop[2] + drop[3])
            return new0, new1

        for n in range(MAX_SUB):
            keep = counts > float(n)
            keep_tile = jnp.broadcast_to(counts, (8, slots)) > float(n)
            moved = []
            for f in range(2):
                d = RELAX * (goal[f] - mean[f])
                d = d + vertical(d)
                shift_rows[f] = d
                moved.append(mean[f] + vertical(mean[f]) + d)

            def shifts(z):
                return [
                    jnp.broadcast_to(shift_rows[f, pl.ds(z, 1), :], (8, slots)) for f in range(2)
                ]

            if n == 0:

                def finish(z, carry):
                    new = condense(
                        (packed(0, z), packed(1, z)), shifts(z), z, keep_tile,
                        (strided(0, z), strided(1, z)),
                    )
                    for f in range(2):
                        for k in range(4):
                            state[f, z, pl.ds(8 * k, 8), :] = new[f][k]
                    return carry

                lax.fori_loop(0, levels_c, finish, 0, unroll=2)
            else:

                def sweep(z, carry, last=n == MAX_SUB - 1):
                    below, here = carry
                    following = jnp.minimum(z + 1, levels_c - 1)
                    above = (packed(0, following), packed(1, following))
                    a = [stencil(here[f], below[f], above[f]) for f in range(2)]
                    new = condense(a, shifts(z), z, keep_tile, here)
                    for f in range(2):
                        for k in range(4):
                            if last:
                                plain[f, z, pl.ds(k, 8, stride=4), :] = new[f][k]
                            else:
                                state[f, z, pl.ds(8 * k, 8), :] = new[f][k]
                    return here, above

                edge = (packed(0, 0), packed(1, 0))
                lax.fori_loop(0, levels_c, sweep, (edge, edge), unroll=2)

            dried = jnp.sum(parts[0], axis=1) * columns_inv
            mean[0] = jnp.where(keep, moved[0] + LATENT * dried, mean[0])
            mean[1] = jnp.where(keep, moved[1] - dried, mean[1])

        change = jnp.concatenate(
            [jnp.where(level < levels_c, mean[f] - start[f], 0.0) for f in range(2)], axis=0
        )
        tendency = dot3(jnp.transpose(change), square[...])
        tend_send[...] = tendency.reshape(n_col, cap, width)

        def give(step, carry):
            other = lax.rem(col + step, n_col)
            pltpu.make_async_remote_copy(
                src_ref=tend_send.at[other], dst_ref=tends.at[sec - 1, col],
                send_sem=tend_send_sem, recv_sem=tend_recv_sem,
                device_id=(sec, other), device_id_type=MESH,
            ).start()
            return carry

        lax.fori_loop(1, n_col, give, 0)
        pltpu.make_async_copy(tend_send.at[col], tends.at[sec - 1, col], tend_recv_sem).start()

        for f in range(2):

            def narrow(z, carry, f=f):
                block[f, z] = plain[f, z].astype(BF16)
                return carry

            lax.fori_loop(0, levels_c, narrow, 0, unroll=2)

    @pl.when(jnp.logical_not(is_cloud))
    def _():
        to_right.wait_recv()
        to_left.wait_recv()
        fetch.wait()

    store = pltpu.make_async_copy(block, new_cloud_ref.at[0], local_sem.at[1])
    store.start()

    around = jnp.concatenate([halo[0], halo[1], own], axis=0)
    spread = rate * pick(near_e, around)
    adv_ref[...] = base
    for k in range(4):
        adv_ref[pl.ds(k, elements, stride=4), :] += spread
    member = jnp.where(
        slot_column == iota((rows, (n_sec - 1) * slots), 1).astype(F32), 1.0, 0.0
    ).astype(BF16)

    def passing(source, step):
        return pltpu.make_async_remote_copy(
            src_ref=tends.at[source], dst_ref=tends.at[source],
            send_sem=group_send_sem.at[step], recv_sem=group_recv_sem.at[source],
            device_id=(lax.rem(sec + step, n_sec), col), device_id_type=MESH,
        )

    @pl.when(is_cloud)
    def _():
        pltpu.make_async_copy(tends.at[sec - 1], tends.at[sec - 1], tend_recv_sem).wait()
        for step in range(1, n_sec):
            passing(sec - 1, step).start()

    for source in range(n_sec - 1):

        @pl.when(sec != source + 1)
        def _():
            passing(source, 1).wait_recv()

    gathered = tends[...].reshape((n_sec - 1) * slots, width)
    summed = adv_ref[...] + pick(member, gathered)
    out_ref[...] = jnp.where(
        iota((rows, width), 1) >= levels_h, jnp.maximum(summed, 0.0), summed
    )

    to_right.wait_send()
    to_left.wait_send()
    store.wait()

    @pl.when(is_cloud)
    def _():
        others = pl.ds(0, n_col - 1)
        pltpu.make_async_copy(disp_send.at[others], disp_send.at[others], disp_send_sem).wait()
        pltpu.make_async_copy(tend_send.at[others], tend_send.at[others], tend_send_sem).wait()
        for step in range(1, n_sec):
            passing(sec - 1, step).wait_send()


def body(
    column_state, mixing_rate, neighbours, assignment, substeps, cloud_state, level_map, saturation
):
    n_sec, n_col = lax.axis_size("sec"), lax.axis_size("col")
    rows, width = column_state.shape
    elements = rows // 4
    _, fields, levels_c, across, slots = cloud_state.shape
    cap, levels_h = slots // n_col, level_map.shape[1]
    vmem = pl.BlockSpec(memory_space=pltpu.VMEM)
    hbm = pl.BlockSpec(memory_space=pl.ANY)
    message = (n_col, cap, width)
    dma = pltpu.SemaphoreType.DMA
    return pl.pallas_call(
        functools.partial(kernel, (n_sec, n_col)),
        out_shape=(
            jax.ShapeDtypeStruct(column_state.shape, F32),
            jax.ShapeDtypeStruct(cloud_state.shape, BF16),
        ),
        in_specs=[vmem, vmem, vmem, vmem, vmem, hbm, vmem, pl.BlockSpec(memory_space=pltpu.SMEM)],
        out_specs=(vmem, hbm),
        scratch_shapes=[
            pltpu.VMEM((fields, levels_c, across, slots), BF16),
            pltpu.VMEM((fields, levels_c, across, slots), F32),
            pltpu.VMEM((fields, levels_c, across, slots), F32),
            pltpu.VMEM((fields, levels_h, 8, slots), F32),
            pltpu.VMEM((fields, levels_h, slots), F32),
            pltpu.VMEM((fields * levels_h, fields * levels_h), F32),
            pltpu.VMEM((elements, width), F32),
            pltpu.VMEM((2, elements, width), F32),
            pltpu.VMEM(message, F32),
            pltpu.VMEM(message, F32),
            pltpu.VMEM(message, F32),
            pltpu.VMEM((n_sec - 1,) + message, F32),
            pltpu.VMEM((rows, width), F32),
            dma((2,)),
            dma((2,)),
            dma((2,)),
            dma,
            dma,
            dma,
            dma,
            dma((n_sec,)),
            dma((n_sec - 1,)),
        ],
        compiler_params=pltpu.CompilerParams(
            collective_id=0, has_side_effects=True, vmem_limit_bytes=48 * 1024 * 1024
        ),
    )(
        column_state,
        mixing_rate.reshape(1, width),
        neighbours.T,
        assignment.reshape(1, rows),
        substeps.reshape(1, rows),
        cloud_state,
        level_map,
        saturation,
    )


def solution(mesh):
    in_specs = (
        P("col", None),
        P(),
        P("col", None),
        P("col", None),
        P("col"),
        P("sec", None, None, None, "col"),
        P(),
        P(),
    )
    out_specs = (P("col", None), P("sec", None, None, None, "col"))
    return jax.shard_map(body, mesh=mesh, in_specs=in_specs, out_specs=out_specs, check_vma=False)
```

```python
import functools

import jax
import jax.numpy as jnp
from jax import lax
from jax.experimental import pallas as pl
from jax.experimental.pallas import tpu as pltpu
from jax.sharding import PartitionSpec as P

MAX_SUB = 4
RELAX = 0.25
HORIZ = 0.12
VERTIC = 0.1
LATENT = 2.5
VMIX = 0.2
UNROLL = 29
CENTRE = 1.0 - 2.0 * HORIZ - 2.0 * VERTIC
MESH = pl.DeviceIdType.MESH
F32 = jnp.float32
BF16 = jnp.bfloat16
I32 = jnp.int32
NN = (((1,), (0,)), ((), ()))
NT = (((1,), (1,)), ((), ()))
ACROSS = ((2, 1), (1, 1), (3, 1), (2, 0), (0, 1), (1, 0), (3, 0), (0, 0))


def iota(shape, dim):
    return lax.broadcasted_iota(I32, shape, dim)


def halves(x):
    hi = x.astype(BF16)
    return hi, (x - hi.astype(F32)).astype(BF16)


def dot(a, b, dims=NN):
    return lax.dot_general(a, b, dims, preferred_element_type=F32)


def pick(exact, x, dims=NN):
    hi, lo = halves(x)
    return dot(exact, hi, dims) + dot(exact, lo, dims)


def dot3(x, y, dims=NN):
    xh, xl = halves(x)
    yh, yl = halves(y)
    return dot(xh, yh, dims) + (dot(xh, yl, dims) + dot(xl, yh, dims))


def for_others(col, visit):
    y, x, z = col // 16, lax.rem(col // 8, 2), lax.rem(col, 8)
    bases = [lax.rem(y + dy, 4) * 16 + lax.rem(x + dx, 2) * 8 for dy, dx in ACROSS]

    def ring(t, carry):
        half = (t + 1) // 2
        dz = 4 + half - 2 * half * lax.rem(t, 2)
        along = lax.rem(z + dz, 8)
        for base in bases:
            visit(base + along)
        return carry

    lax.fori_loop(0, 7, ring, 0)
    for base in bases[:-1]:
        visit(base + z)


def kernel(
    sizes,
    cs_hbm,
    rate_hbm,
    nbr_hbm,
    asg_hbm,
    cnt_hbm,
    cloud_hbm,
    map_hbm,
    sat_hbm,
    out_ref,
    block,
    cs_ref,
    rate_ref,
    nbr_ref,
    asg_ref,
    cnt_ref,
    map_ref,
    sat_ref,
    plain_energy,
    plain_water,
    energy_a,
    energy_b,
    water_a,
    water_b,
    drops,
    parts,
    limits,
    offsets,
    square,
    means,
    halo,
    disp_send,
    disp_recv,
    tend_send,
    tends,
    adv_ref,
    local_sem,
    halo_send_sem,
    halo_recv_sem,
    relay_sem,
    disp_send_sem,
    disp_recv_sem,
    tend_send_sem,
    tend_recv_sem,
    core_send_sem,
    core_recv_sem,
):
    n_sec, n_col = sizes
    sec, col = lax.axis_index("sec"), lax.axis_index("col")
    rows, width = cs_ref.shape
    elements = rows // 4
    total = elements * n_col
    cap, slots = disp_send.shape[1], n_col * disp_send.shape[1]
    levels_c, levels_h = map_ref.shape
    left, right = lax.rem(col + n_col - 1, n_col), lax.rem(col + 1, n_col)
    is_cloud = sec > 0
    plain = (plain_energy, plain_water)
    across = plain_water.shape[1]
    core = lax.rem(sec, 2)
    sibling = sec + 1 - 2 * core
    facing = lax.rem(sec + 2, n_sec)

    fetches = [
        pltpu.make_async_copy(src, dst, local_sem.at[i])
        for i, (src, dst) in enumerate(
            (
                (cs_hbm, cs_ref),
                (asg_hbm, asg_ref),
                (nbr_hbm, nbr_ref),
                (rate_hbm, rate_ref),
                (map_hbm, map_ref),
                (cnt_hbm, cnt_ref),
                (sat_hbm, sat_ref),
                (cloud_hbm, block),
            )
        )
    ]
    for fetch in fetches:
        fetch.start()

    barrier = pltpu.get_barrier_semaphore()

    def greet(device):
        pl.semaphore_signal(barrier, inc=1, device_id=device, device_id_type=MESH)

    greet((0, left))
    greet((0, right))

    @pl.when(is_cloud)
    def _():
        for_others(col, lambda other: greet((sec, other)))

    greet((sibling, col))

    @pl.when(sec != 2)
    def _():
        greet((facing, col))

    fetches[0].wait()
    own = (
        cs_ref[pl.ds(0, elements, stride=4), :]
        + cs_ref[pl.ds(1, elements, stride=4), :]
        + cs_ref[pl.ds(2, elements, stride=4), :]
        + cs_ref[pl.ds(3, elements, stride=4), :]
    ) * 0.25
    means[...] = own

    def sharing(section, side):
        return pltpu.make_async_remote_copy(
            src_ref=means, dst_ref=halo.at[side],
            send_sem=halo_send_sem.at[side, section // 2], recv_sem=halo_recv_sem.at[side],
            device_id=(section, (right, left)[side]), device_id_type=MESH,
        )

    def relay(side):
        return pltpu.make_async_remote_copy(
            src_ref=halo.at[side], dst_ref=halo.at[side],
            send_sem=relay_sem.at[side], recv_sem=halo_recv_sem.at[side],
            device_id=(sibling, col), device_id_type=MESH,
        )

    def halo_arrives():
        for side in range(2):
            relay(side).wait_recv()

            @pl.when(core == 0)
            def _():
                relay(side).start()

    @pl.when(jnp.logical_not(is_cloud))
    def _():
        pl.semaphore_wait(barrier, 2 * n_sec + 1)
        for section in (2, 0):
            for side in range(2):
                sharing(section, side).start()

    for fetch in fetches[1:7]:
        fetch.wait()

    asg = asg_ref[...]
    asg_column = jnp.transpose(jnp.broadcast_to(asg.astype(F32), (128, rows)))[:, 0:1]
    same = (asg_column == asg.astype(F32)) & (iota((rows, rows), 0) < iota((rows, rows), 1))
    rank = jnp.max(jnp.where(same, 1.0, 0.0), axis=0, keepdims=True)
    slot = (asg * cap).astype(F32) + rank

    place = iota((3 * elements, elements), 0)
    place = jnp.where(
        place < elements, place, jnp.where(place < 2 * elements, place + elements, place - elements)
    )
    near = jnp.where(place == elements + iota((3 * elements, elements), 1), -4.0, 0.0)
    relative = jnp.bitwise_and(nbr_ref[...] - (col - 1) * elements, total - 1)
    for k in range(4):
        near = near + jnp.where(relative[k : k + 1, :] == place, 1.0, 0.0)
    near_t = near.astype(BF16)

    cs = cs_ref[...]
    lane = jnp.bitwise_and(iota((rows, width), 1), levels_h - 1)
    upper = jnp.where(lane == levels_h - 1, cs, pltpu.roll(cs, width - 1, axis=1))
    lower = jnp.where(lane == 0, cs, pltpu.roll(cs, 1, axis=1))
    base = cs + VMIX * (upper + lower - 2.0 * cs)
    rate = rate_ref[...]

    square[...] = jnp.zeros_like(square)
    square[0:levels_c, 0:levels_h] = map_ref[...]
    square[levels_h : levels_h + levels_c, levels_h : 2 * levels_h] = map_ref[...]

    @pl.when(is_cloud)
    def _():
        chosen = iota((slots, rows), 0) + (sec - 1) * slots == slot.astype(I32)
        chosen32 = jnp.where(chosen, 1.0, 0.0)
        chosen16 = chosen32.astype(BF16)
        counts_out = jnp.sum(chosen32 * cnt_ref[...].astype(F32), axis=1, keepdims=True)
        repeat = jnp.where(
            iota((elements, rows), 0) == lax.shift_right_logical(iota((elements, rows), 1), 2), 1.0, 0.0
        ).astype(BF16)
        by_element = dot(chosen16, repeat, NT).astype(BF16)
        reach = dot(by_element, near_t, NT).astype(BF16)
        known = pick(chosen16, base) + rate * pick(reach[:, 2 * elements :], own)
        reach = reach[:, : 2 * elements]

        halo_arrives()
        outside = halo[...].reshape(2 * elements, width)
        sent = known + rate * pick(reach, outside)
        target = dot3(sent, square[...], NT)
        target = jnp.where(iota((slots, width), 1) == levels_c, counts_out, target)
        disp_send[...] = target.reshape(n_col, cap, width)

        pl.semaphore_wait(barrier, n_col + 1)
        def send(other):
            pltpu.make_async_remote_copy(
                src_ref=disp_send.at[other], dst_ref=disp_recv.at[col],
                send_sem=disp_send_sem, recv_sem=disp_recv_sem,
                device_id=(sec, other), device_id_type=MESH,
            ).start()

        for_others(col, send)
        pltpu.make_async_copy(disp_send.at[col], disp_recv.at[col], disp_recv_sem).start()

        fetches[7].wait()
        for f in range(2):
            parts[f, levels_c:] = jnp.zeros((levels_h - levels_c, 8, slots), F32)

            def widen(z, carry, f=f):
                x = block[0, f, z].astype(F32)
                plain[f][z] = x
                parts[f, z] = (x[0:8] + x[8:16]) + (x[16:24] + x[24:32])
                return carry

            lax.fori_loop(0, levels_c, widen, 0, unroll=UNROLL)

        def strided(ref, z):
            return tuple(ref[z, pl.ds(k, 8, stride=4), :] for k in range(4))

        def packed(ref, z):
            return tuple(ref[z, pl.ds(8 * k, 8), :] for k in range(4))

        def put_strided(ref, z, tiles):
            for k in range(4):
                ref[z, pl.ds(k, 8, stride=4), :] = tiles[k]

        def put_packed(ref, z, tiles):
            for k in range(4):
                ref[z, pl.ds(8 * k, 8), :] = tiles[k]

        def stencil(here, below, above, by_x, by_z):
            west = (pltpu.roll(here[3], 1, axis=0),) + here[:3]
            east = here[1:] + (pltpu.roll(here[0], 7, axis=0),)
            return tuple(
                here[k] + (by_x * (east[k] + west[k]) + by_z * (above[k] + below[k]))
                for k in range(4)
            )

        for f in range(2):

            def first(z, carry, f=f):
                below, here = carry
                above = strided(plain[f], jnp.minimum(z + 1, levels_c - 1))
                put_packed(
                    (energy_a, water_a)[f], z, stencil(here, below, above, HORIZ / CENTRE, VERTIC / CENTRE)
                )
                return here, above

            edge = strided(plain[f], 0)
            lax.fori_loop(0, levels_c, first, (edge, edge), unroll=UNROLL)

        columns_inv = 1.0 / across
        start = [jnp.sum(parts[f], axis=1) * columns_inv for f in range(2)]
        level = iota((levels_h, slots), 0)
        wet = jnp.concatenate([sat_ref[...], jnp.zeros((1, 128 - levels_c), F32)], axis=1)
        wet = jnp.transpose(jnp.broadcast_to(wet, (128, 128)))[:levels_h]

        def smoothed(x):
            up = jnp.where(level == levels_c - 1, x, pltpu.roll(x, levels_h - 1, axis=0))
            low = jnp.where(level == 0, x, pltpu.roll(x, 1, axis=0))
            return (1.0 - 2.0 * VERTIC) * x + VERTIC * (up + low)

        pltpu.make_async_copy(disp_recv, disp_recv, disp_recv_sem).wait()
        arrived = jnp.transpose(disp_recv[...].reshape(slots, width))
        counts = arrived[levels_c : levels_c + 1, :]
        counts8 = jnp.broadcast_to(counts, (8, slots))
        goal = [arrived[f * levels_h : (f + 1) * levels_h] for f in range(2)]
        mean = list(start)
        offset = [jnp.zeros((levels_h, slots), F32)] * 2

        for n in range(MAX_SUB):
            scale = CENTRE ** (n + 1)
            keep = counts > float(n)
            moved, shifted = [], []
            for f in range(2):
                d = RELAX * (goal[f] - mean[f])
                moved.append(smoothed(mean[f] + d))
                shifted.append(smoothed(offset[f] + d))
            limit = (0.5 / scale) * (wet - shifted[1])
            limits[...] = limit if n == 0 else jnp.where(keep, limit, 0.0)

            def condense(water, z, by_half):
                bound = jnp.broadcast_to(limits[pl.ds(z, 1), :], (8, slots))
                drop = [jnp.maximum(by_half * water[k] - bound, 0.0) for k in range(4)]
                parts[1, z] = (drop[0] + drop[1]) + (drop[2] + drop[3])
                return [water[k] - drop[k] for k in range(4)], drop

            if n == 0:

                def finish(z, carry):
                    new, drop = condense(packed(water_a, z), z, 0.5)
                    put_packed(water_b, z, new)
                    put_packed(drops.at[0], z, drop)
                    return carry

                lax.fori_loop(0, levels_c, finish, 0, unroll=UNROLL)
            else:
                going = jnp.where(counts8 > float(n), 1.0, 0.0)
                by_x, by_z, by_half = going * (HORIZ / CENTRE), going * (VERTIC / CENTRE), going * 0.5
                old, fresh = (water_b, water_a) if n % 2 else (water_a, water_b)

                def sweep(z, carry, n=n, old=old, fresh=fresh, by_x=by_x, by_z=by_z, by_half=by_half):
                    below, here = carry
                    above = packed(old, jnp.minimum(z + 1, levels_c - 1))
                    new, drop = condense(stencil(here, below, above, by_x, by_z), z, by_half)
                    if n == MAX_SUB - 1:
                        put_strided(plain_water, z, new)
                        put_strided(drops.at[n], z, drop)
                    else:
                        put_packed(fresh, z, new)
                        put_packed(drops.at[n], z, drop)
                    return here, above

                edge = packed(old, 0)
                lax.fori_loop(0, levels_c, sweep, (edge, edge), unroll=UNROLL)

            dried = jnp.sum(parts[1], axis=1) * (columns_inv * scale)
            mean[0] = jnp.where(keep, moved[0] + LATENT * dried, mean[0])
            mean[1] = jnp.where(keep, moved[1] - dried, mean[1])
            offset = [jnp.where(keep, shifted[f], offset[f]) for f in range(2)]

        change = jnp.concatenate(
            [jnp.where(level < levels_c, mean[f] - start[f], 0.0) for f in range(2)], axis=0
        )
        tendency = dot3(jnp.transpose(change), square[...])
        tend_send[...] = tendency.reshape(n_col, cap, width)

        def give(other, chip):
            pltpu.make_async_remote_copy(
                src_ref=tend_send.at[other], dst_ref=tends.at[sec - 1, col],
                send_sem=tend_send_sem.at[chip], recv_sem=tend_recv_sem.at[sec - 1],
                device_id=((sec, facing)[chip], other), device_id_type=MESH,
            ).start()

        def give_both(other):
            give(other, 1)
            give(other, 0)

        for_others(col, give_both)
        give(col, 1)
        pltpu.make_async_copy(tend_send.at[col], tends.at[sec - 1, col], tend_recv_sem.at[sec - 1]).start()

        for n in range(1, MAX_SUB):
            going = jnp.where(counts8 > float(n), 1.0, 0.0)
            by_x, by_z = going * (HORIZ / CENTRE), going * (VERTIC / CENTRE)

            old, fresh = (energy_a, energy_b) if n % 2 else (energy_b, energy_a)

            def warmed(z, n=n, old=old):
                energy, drop = packed(old, z), packed(drops.at[n - 1], z)
                return tuple(energy[k] + LATENT * drop[k] for k in range(4))

            def follow(z, carry, n=n, fresh=fresh, by_x=by_x, by_z=by_z, warmed=warmed):
                below, here = carry
                above = warmed(jnp.minimum(z + 1, levels_c - 1))
                new = stencil(here, below, above, by_x, by_z)
                if n == MAX_SUB - 1:
                    put_strided(plain_energy, z, new)
                else:
                    put_packed(fresh, z, new)
                return here, above

            edge = warmed(0)
            lax.fori_loop(0, levels_c, follow, (edge, edge), unroll=UNROLL)

        power = jnp.full((1, slots), CENTRE, F32)
        for n in range(1, MAX_SUB):
            power = jnp.where(counts > float(n), CENTRE ** (n + 1), power)
        used = jnp.broadcast_to(counts, (across, slots)) > 0.0
        power = jnp.broadcast_to(power, (across, slots))
        for f in range(2):
            offsets[f] = offset[f]

            def narrow(z, carry, f=f):
                x = plain[f][z]
                if f == 0:
                    x = x + LATENT * drops[MAX_SUB - 1, z]
                x = power * x + jnp.broadcast_to(offsets[f, pl.ds(z, 1), :], x.shape)
                block[0, f, z] = jnp.where(used, x, block[0, f, z].astype(F32)).astype(BF16)
                return carry

            lax.fori_loop(0, levels_c, narrow, 0, unroll=UNROLL)

    @pl.when(jnp.logical_not(is_cloud))
    def _():
        halo_arrives()
        fetches[7].wait()

    near_e = jnp.transpose(
        jnp.concatenate([near, jnp.zeros((3 * elements, 128 - elements), F32)], axis=1)
    )[:elements].astype(BF16)
    around = jnp.concatenate([halo[0], halo[1], own], axis=0)
    spread = rate * pick(near_e, around)
    adv_ref[...] = base
    for k in range(4):
        adv_ref[pl.ds(k, elements, stride=4), :] += spread
    slot_column = jnp.transpose(jnp.broadcast_to(slot, (128, rows)))[:, 0:1]
    member = jnp.where(
        slot_column == iota((rows, (n_sec - 1) * slots), 1).astype(F32), 1.0, 0.0
    ).astype(BF16)

    def heard(source):
        pltpu.make_async_copy(tends.at[source], tends.at[source], tend_recv_sem.at[source]).wait()

    def passing(source):
        return pltpu.make_async_remote_copy(
            src_ref=tends.at[source], dst_ref=tends.at[source],
            send_sem=core_send_sem.at[source], recv_sem=core_recv_sem.at[source],
            device_id=(sibling, col), device_id_type=MESH,
        )

    def gather(sources):
        for source in sources:
            found = tends[source].reshape(slots, width)
            adv_ref[...] += pick(member[:, source * slots : (source + 1) * slots], found)

    for mine, theirs in (((1,), (0, 2)), ((0, 2), (1,))):

        @pl.when(core == len(mine) - 1)
        def _():
            for source in mine:
                heard(source)
                passing(source).start()
            gather(mine)
            for source in theirs:
                passing(source).wait_recv()
            gather(theirs)

    summed = adv_ref[...]
    out_ref[...] = jnp.where(
        iota((rows, width), 1) >= levels_h, jnp.maximum(summed, 0.0), summed
    )

    @pl.when(jnp.logical_not(is_cloud))
    def _():
        for section in (2, 0):
            for side in range(2):
                sharing(section, side).wait_send()

    @pl.when(core == 0)
    def _():
        for side in range(2):
            relay(side).wait_send()

    for mine in ((1,), (0, 2)):

        @pl.when(core == len(mine) - 1)
        def _():
            for source in mine:
                passing(source).wait_send()

    @pl.when(is_cloud)
    def _():
        others = pl.ds(0, n_col - 1)
        pltpu.make_async_copy(disp_send.at[others], disp_send.at[others], disp_send_sem).wait()
        pltpu.make_async_copy(tend_send.at[others], tend_send.at[others], tend_send_sem.at[0]).wait()
        pltpu.make_async_copy(tend_send, tend_send, tend_send_sem.at[1]).wait()


def body(
    column_state, mixing_rate, neighbours, assignment, substeps, cloud_state, level_map, saturation
):
    n_sec, n_col = lax.axis_size("sec"), lax.axis_size("col")
    rows, width = column_state.shape
    elements = rows // 4
    _, fields, levels_c, across, slots = cloud_state.shape
    cap, levels_h = slots // n_col, level_map.shape[1]
    vmem = pl.BlockSpec(memory_space=pltpu.VMEM)
    hbm = pl.BlockSpec(memory_space=pltpu.HBM)
    message = (n_col, cap, width)
    dma = pltpu.SemaphoreType.DMA
    results = (
        jax.ShapeDtypeStruct(column_state.shape, F32),
        jax.ShapeDtypeStruct(cloud_state.shape, BF16),
    )
    operands = (
        column_state,
        mixing_rate.reshape(1, width),
        neighbours.T,
        assignment.reshape(1, rows),
        substeps.reshape(1, rows),
        cloud_state,
        level_map,
        saturation.reshape(1, levels_c),
    )
    return pl.pallas_call(
        functools.partial(kernel, (n_sec, n_col)),
        out_shape=tuple(pltpu.VMEM(r.shape, r.dtype) for r in results),
        in_specs=[hbm] * 8,
        out_specs=(vmem, vmem),
        scratch_shapes=[
            pltpu.VMEM((rows, width), F32),
            pltpu.VMEM((1, width), F32),
            pltpu.VMEM((4, elements), I32),
            pltpu.VMEM((1, rows), I32),
            pltpu.VMEM((1, rows), I32),
            pltpu.VMEM((levels_c, levels_h), F32),
            pltpu.VMEM((1, levels_c), F32),
            *[pltpu.VMEM((levels_c, across, slots), F32)] * 6,
            pltpu.VMEM((MAX_SUB, levels_c, across, slots), F32),
            pltpu.VMEM((fields, levels_h, 8, slots), F32),
            pltpu.VMEM((levels_h, slots), F32),
            pltpu.VMEM((fields, levels_h, slots), F32),
            pltpu.VMEM((fields * levels_h, fields * levels_h), F32),
            pltpu.VMEM((elements, width), F32),
            pltpu.VMEM((2, elements, width), F32),
            pltpu.VMEM(message, F32),
            pltpu.VMEM(message, F32),
            pltpu.VMEM(message, F32),
            pltpu.VMEM((n_sec - 1,) + message, F32),
            pltpu.VMEM((rows, width), F32),
            dma((8,)),
            dma((2, 2)),
            dma((2,)),
            dma((2,)),
            dma,
            dma,
            dma((2,)),
            dma((n_sec - 1,)),
            dma((n_sec - 1,)),
            dma((n_sec - 1,)),
        ],
        compiler_params=pltpu.CompilerParams(
            collective_id=0, has_side_effects=True, vmem_limit_bytes=48 * 1024 * 1024
        ),
    )(*(pltpu.with_memory_space_constraint(x, pltpu.HBM) for x in operands))


def solution(mesh):
    in_specs = (
        P("col", None),
        P(),
        P("col", None),
        P("col", None),
        P("col"),
        P("sec", None, None, None, "col"),
        P(),
        P(),
    )
    out_specs = (P("col", None), P("sec", None, None, None, "col"))
    return jax.shard_map(body, mesh=mesh, in_specs=in_specs, out_specs=out_specs, check_vma=False)
```

```python
import functools

import jax
import jax.numpy as jnp
from jax import lax
from jax.experimental import pallas as pl
from jax.experimental.pallas import tpu as pltpu
from jax.sharding import PartitionSpec as P

MAX_SUB = 4
RELAX = 0.25
HORIZ = 0.12
VERTIC = 0.1
LATENT = 2.5
VMIX = 0.2
UNROLL = 29
CENTRE = 1.0 - 2.0 * HORIZ - 2.0 * VERTIC
MESH = pl.DeviceIdType.MESH
F32 = jnp.float32
BF16 = jnp.bfloat16
I32 = jnp.int32
NN = (((1,), (0,)), ((), ()))
NT = (((1,), (1,)), ((), ()))
ACROSS = ((2, 1), (1, 1), (3, 1), (2, 0), (0, 1), (1, 0), (3, 0), (0, 0))


def iota(shape, dim):
    return lax.broadcasted_iota(I32, shape, dim)


def halves(x):
    hi = x.astype(BF16)
    return hi, (x - hi.astype(F32)).astype(BF16)


def dot(a, b, dims=NN):
    return lax.dot_general(a, b, dims, preferred_element_type=F32)


def pick(exact, x, dims=NN):
    hi, lo = halves(x)
    return dot(exact, hi, dims) + dot(exact, lo, dims)


def dot3(x, y, dims=NN):
    xh, xl = halves(x)
    yh, yl = halves(y)
    return dot(xh, yh, dims) + (dot(xh, yl, dims) + dot(xl, yh, dims))


def for_others(col, visit):
    y, x, z = col // 16, lax.rem(col // 8, 2), lax.rem(col, 8)
    bases = [lax.rem(y + dy, 4) * 16 + lax.rem(x + dx, 2) * 8 for dy, dx in ACROSS]

    def ring(t, carry):
        half = (t + 1) // 2
        dz = 4 + half - 2 * half * lax.rem(t, 2)
        along = lax.rem(z + dz, 8)
        for base in bases:
            visit(base + along)
        return carry

    lax.fori_loop(0, 7, ring, 0)
    for base in bases[:-1]:
        visit(base + z)


def kernel(
    sizes,
    cs_hbm,
    rate_hbm,
    nbr_hbm,
    asg_hbm,
    cnt_hbm,
    cloud_hbm,
    map_hbm,
    sat_hbm,
    out_ref,
    block,
    cs_ref,
    rate_ref,
    nbr_ref,
    asg_ref,
    cnt_ref,
    map_ref,
    sat_ref,
    plain_energy,
    plain_water,
    energy_a,
    energy_b,
    water_a,
    water_b,
    drops,
    parts,
    limits,
    offsets,
    square,
    pushed,
    given,
    beyond,
    disp_send,
    disp_recv,
    tend_send,
    tends,
    adv_ref,
    local_sem,
    push_send_sem,
    push_recv_sem,
    relay_sem,
    beyond_sem,
    disp_send_sem,
    disp_recv_sem,
    tend_send_sem,
    tend_recv_sem,
    core_send_sem,
    core_recv_sem,
):
    n_sec, n_col = sizes
    sec, col = lax.axis_index("sec"), lax.axis_index("col")
    rows, width = cs_ref.shape
    elements = rows // 4
    total = elements * n_col
    cap, slots = disp_send.shape[1], n_col * disp_send.shape[1]
    levels_c, levels_h = map_ref.shape
    left, right = lax.rem(col + n_col - 1, n_col), lax.rem(col + 1, n_col)
    is_cloud = sec > 0
    plain = (plain_energy, plain_water)
    across = plain_water.shape[1]
    core = lax.rem(sec, 2)
    sibling = sec + 1 - 2 * core
    facing = lax.rem(sec + 2, n_sec)

    fetches = [
        pltpu.make_async_copy(src, dst, local_sem.at[i])
        for i, (src, dst) in enumerate(
            (
                (cs_hbm, cs_ref),
                (asg_hbm, asg_ref),
                (nbr_hbm, nbr_ref),
                (rate_hbm, rate_ref),
                (map_hbm, map_ref),
                (cnt_hbm, cnt_ref),
                (sat_hbm, sat_ref),
                (cloud_hbm, block),
            )
        )
    ]
    for fetch in fetches:
        fetch.start()

    barrier = pltpu.get_barrier_semaphore()

    def greet(device):
        pl.semaphore_signal(barrier, inc=1, device_id=device, device_id_type=MESH)

    greet((0, left))

    @pl.when(is_cloud)
    def _():
        for_others(col, lambda other: greet((sec, other)))

    greet((sibling, col))

    @pl.when(sec != 2)
    def _():
        greet((facing, col))

    fetches[0].wait()
    own = (
        cs_ref[pl.ds(0, elements, stride=4), :]
        + cs_ref[pl.ds(1, elements, stride=4), :]
        + cs_ref[pl.ds(2, elements, stride=4), :]
        + cs_ref[pl.ds(3, elements, stride=4), :]
    ) * 0.25
    pushed[0:elements] = own
    fetches[1].wait()
    fetches[2].wait()

    asg = asg_ref[...]
    asg_column = jnp.transpose(jnp.broadcast_to(asg.astype(F32), (128, rows)))[:, 0:1]
    same = (asg_column == asg.astype(F32)) & (iota((rows, rows), 0) < iota((rows, rows), 1))
    rank = jnp.max(jnp.where(same, 1.0, 0.0), axis=0, keepdims=True)
    slot = (asg * cap).astype(F32) + rank

    pushed[elements : elements + 4, 0:elements] = nbr_ref[...].astype(F32)
    pushed[elements + 4 : elements + 5] = slot[:, :width]
    pushed[elements + 5 : elements + 6] = slot[:, width:]

    def push(section):
        return pltpu.make_async_remote_copy(
            src_ref=pushed, dst_ref=given,
            send_sem=push_send_sem.at[section - 1], recv_sem=push_recv_sem,
            device_id=(section, right), device_id_type=MESH,
        )

    relays = (sec == 1) | (sec == 2)
    relay = pltpu.make_async_remote_copy(
        src_ref=given, dst_ref=given, send_sem=relay_sem, recv_sem=push_recv_sem,
        device_id=(sibling, col), device_id_type=MESH,
    )

    def push_arrives():
        relay.wait_recv()

        @pl.when(relays)
        def _():
            relay.start()

    means = pushed.at[pl.ds(0, elements)]
    to_left = pltpu.make_async_remote_copy(
        src_ref=means, dst_ref=beyond, send_sem=beyond_sem.at[0], recv_sem=beyond_sem.at[1],
        device_id=(sec, left), device_id_type=MESH,
    )

    @pl.when(jnp.logical_not(is_cloud))
    def _():
        pl.semaphore_wait(barrier, n_sec + 1)
        for section in (2, 1):
            push(section).start()

    for fetch in fetches[3:7]:
        fetch.wait()

    place = iota((3 * elements, elements), 0)
    place = jnp.where(
        place < elements, place, jnp.where(place < 2 * elements, place + elements, place - elements)
    )
    near = jnp.where(place == elements + iota((3 * elements, elements), 1), -4.0, 0.0)
    relative = jnp.bitwise_and(nbr_ref[...] - (col - 1) * elements, total - 1)
    for k in range(4):
        near = near + jnp.where(relative[k : k + 1, :] == place, 1.0, 0.0)
    near_t = near.astype(BF16)

    cs = cs_ref[...]
    lane = jnp.bitwise_and(iota((rows, width), 1), levels_h - 1)
    upper = jnp.where(lane == levels_h - 1, cs, pltpu.roll(cs, width - 1, axis=1))
    lower = jnp.where(lane == 0, cs, pltpu.roll(cs, 1, axis=1))
    base = cs + VMIX * (upper + lower - 2.0 * cs)
    rate = rate_ref[...]

    square[...] = jnp.zeros_like(square)
    square[0:levels_c, 0:levels_h] = map_ref[...]
    square[levels_h : levels_h + levels_c, levels_h : 2 * levels_h] = map_ref[...]

    @pl.when(is_cloud)
    def _():
        chosen = iota((slots, rows), 0) + (sec - 1) * slots == slot.astype(I32)
        chosen32 = jnp.where(chosen, 1.0, 0.0)
        chosen16 = chosen32.astype(BF16)
        counts_out = jnp.sum(chosen32 * cnt_ref[...].astype(F32), axis=1, keepdims=True)
        repeat = jnp.where(
            iota((elements, rows), 0) == lax.shift_right_logical(iota((elements, rows), 1), 2), 1.0, 0.0
        ).astype(BF16)
        by_element = dot(chosen16, repeat, NT).astype(BF16)
        reach = dot(by_element, near_t, NT).astype(BF16)
        known = pick(chosen16, base) + rate * pick(reach[:, 2 * elements :], own)
        reach = reach[:, :elements]

        push_arrives()
        sent = known + rate * pick(reach, given[0:elements])
        target = dot3(sent, square[...], NT)
        target = jnp.where(iota((slots, width), 1) == levels_c, counts_out, target)
        disp_send[:, :, 0:width] = target.reshape(n_col, cap, width)
        slot_left = jnp.concatenate([given[elements + 4 : elements + 5], given[elements + 5 : elements + 6]], axis=1)
        chosen_left = jnp.where(
            iota((slots, rows), 0) + (sec - 1) * slots == slot_left.astype(I32), 1.0, 0.0
        ).astype(BF16)
        nbr_left = given[elements : elements + 4, 0:elements].astype(I32)
        here = iota((elements, elements), 0) + col * elements
        near_left = jnp.zeros((elements, elements), F32)
        for k in range(4):
            near_left = near_left + jnp.where(nbr_left[k : k + 1, :] == here, 1.0, 0.0)
        reach_left = dot(dot(chosen_left, repeat, NT).astype(BF16), near_left.astype(BF16), NT)
        extra = dot3(rate * pick(reach_left.astype(BF16), own), square[...], NT)
        disp_send[:, :, width:] = extra.reshape(n_col, cap, width)

        pl.semaphore_wait(barrier, n_col + 1)
        def send(other):
            pltpu.make_async_remote_copy(
                src_ref=disp_send.at[other], dst_ref=disp_recv.at[col],
                send_sem=disp_send_sem, recv_sem=disp_recv_sem,
                device_id=(sec, other), device_id_type=MESH,
            ).start()

        for_others(col, send)
        pltpu.make_async_copy(disp_send.at[col], disp_recv.at[col], disp_recv_sem).start()
        to_left.start()

        fetches[7].wait()
        for f in range(2):
            parts[f, levels_c:] = jnp.zeros((levels_h - levels_c, 8, slots), F32)

            def widen(z, carry, f=f):
                x = block[0, f, z].astype(F32)
                plain[f][z] = x
                parts[f, z] = (x[0:8] + x[8:16]) + (x[16:24] + x[24:32])
                return carry

            lax.fori_loop(0, levels_c, widen, 0, unroll=UNROLL)

        def strided(ref, z):
            return tuple(ref[z, pl.ds(k, 8, stride=4), :] for k in range(4))

        def packed(ref, z):
            return tuple(ref[z, pl.ds(8 * k, 8), :] for k in range(4))

        def put_strided(ref, z, tiles):
            for k in range(4):
                ref[z, pl.ds(k, 8, stride=4), :] = tiles[k]

        def put_packed(ref, z, tiles):
            for k in range(4):
                ref[z, pl.ds(8 * k, 8), :] = tiles[k]

        def stencil(here, below, above, by_x, by_z):
            west = (pltpu.roll(here[3], 1, axis=0),) + here[:3]
            east = here[1:] + (pltpu.roll(here[0], 7, axis=0),)
            return tuple(
                here[k] + (by_x * (east[k] + west[k]) + by_z * (above[k] + below[k]))
                for k in range(4)
            )

        for f in range(2):

            def first(z, carry, f=f):
                below, here = carry
                above = strided(plain[f], jnp.minimum(z + 1, levels_c - 1))
                put_packed(
                    (energy_a, water_a)[f], z, stencil(here, below, above, HORIZ / CENTRE, VERTIC / CENTRE)
                )
                return here, above

            edge = strided(plain[f], 0)
            lax.fori_loop(0, levels_c, first, (edge, edge), unroll=UNROLL)

        columns_inv = 1.0 / across
        start = [jnp.sum(parts[f], axis=1) * columns_inv for f in range(2)]
        level = iota((levels_h, slots), 0)
        wet = jnp.concatenate([sat_ref[...], jnp.zeros((1, 128 - levels_c), F32)], axis=1)
        wet = jnp.transpose(jnp.broadcast_to(wet, (128, 128)))[:levels_h]

        def smoothed(x):
            up = jnp.where(level == levels_c - 1, x, pltpu.roll(x, levels_h - 1, axis=0))
            low = jnp.where(level == 0, x, pltpu.roll(x, 1, axis=0))
            return (1.0 - 2.0 * VERTIC) * x + VERTIC * (up + low)

        pltpu.make_async_copy(disp_recv, disp_recv, disp_recv_sem).wait()
        later = disp_recv[:, :, width:].reshape(slots, width)
        arrived = jnp.transpose(
            disp_recv[:, :, 0:width].reshape(slots, width) + pltpu.roll(later, slots - cap, axis=0)
        )
        counts = arrived[levels_c : levels_c + 1, :]
        counts8 = jnp.broadcast_to(counts, (8, slots))
        goal = [arrived[f * levels_h : (f + 1) * levels_h] for f in range(2)]
        mean = list(start)
        offset = [jnp.zeros((levels_h, slots), F32)] * 2

        for n in range(MAX_SUB):
            scale = CENTRE ** (n + 1)
            keep = counts > float(n)
            moved, shifted = [], []
            for f in range(2):
                d = RELAX * (goal[f] - mean[f])
                moved.append(smoothed(mean[f] + d))
                shifted.append(smoothed(offset[f] + d))
            limit = (0.5 / scale) * (wet - shifted[1])
            limits[...] = limit if n == 0 else jnp.where(keep, limit, 0.0)

            def condense(water, z, by_half):
                bound = jnp.broadcast_to(limits[pl.ds(z, 1), :], (8, slots))
                drop = [jnp.maximum(by_half * water[k] - bound, 0.0) for k in range(4)]
                parts[1, z] = (drop[0] + drop[1]) + (drop[2] + drop[3])
                return [water[k] - drop[k] for k in range(4)], drop

            if n == 0:

                def finish(z, carry):
                    new, drop = condense(packed(water_a, z), z, 0.5)
                    put_packed(water_b, z, new)
                    put_packed(drops.at[0], z, drop)
                    return carry

                lax.fori_loop(0, levels_c, finish, 0, unroll=UNROLL)
            else:
                going = jnp.where(counts8 > float(n), 1.0, 0.0)
                by_x, by_z, by_half = going * (HORIZ / CENTRE), going * (VERTIC / CENTRE), going * 0.5
                old, fresh = (water_b, water_a) if n % 2 else (water_a, water_b)

                def sweep(z, carry, n=n, old=old, fresh=fresh, by_x=by_x, by_z=by_z, by_half=by_half):
                    below, here = carry
                    above = packed(old, jnp.minimum(z + 1, levels_c - 1))
                    new, drop = condense(stencil(here, below, above, by_x, by_z), z, by_half)
                    if n == MAX_SUB - 1:
                        put_strided(plain_water, z, new)
                        put_strided(drops.at[n], z, drop)
                    else:
                        put_packed(fresh, z, new)
                        put_packed(drops.at[n], z, drop)
                    return here, above

                edge = packed(old, 0)
                lax.fori_loop(0, levels_c, sweep, (edge, edge), unroll=UNROLL)

            dried = jnp.sum(parts[1], axis=1) * (columns_inv * scale)
            mean[0] = jnp.where(keep, moved[0] + LATENT * dried, mean[0])
            mean[1] = jnp.where(keep, moved[1] - dried, mean[1])
            offset = [jnp.where(keep, shifted[f], offset[f]) for f in range(2)]

        change = jnp.concatenate(
            [jnp.where(level < levels_c, mean[f] - start[f], 0.0) for f in range(2)], axis=0
        )
        tendency = dot3(jnp.transpose(change), square[...])
        tend_send[...] = tendency.reshape(n_col, cap, width)

        def give(other, chip):
            pltpu.make_async_remote_copy(
                src_ref=tend_send.at[other], dst_ref=tends.at[sec - 1, col],
                send_sem=tend_send_sem.at[chip], recv_sem=tend_recv_sem.at[sec - 1],
                device_id=((sec, facing)[chip], other), device_id_type=MESH,
            ).start()

        def give_both(other):
            give(other, 1)
            give(other, 0)

        for_others(col, give_both)
        give(col, 1)
        pltpu.make_async_copy(tend_send.at[col], tends.at[sec - 1, col], tend_recv_sem.at[sec - 1]).start()

        for n in range(1, MAX_SUB):
            going = jnp.where(counts8 > float(n), 1.0, 0.0)
            by_x, by_z = going * (HORIZ / CENTRE), going * (VERTIC / CENTRE)

            old, fresh = (energy_a, energy_b) if n % 2 else (energy_b, energy_a)

            def warmed(z, n=n, old=old):
                energy, drop = packed(old, z), packed(drops.at[n - 1], z)
                return tuple(energy[k] + LATENT * drop[k] for k in range(4))

            def follow(z, carry, n=n, fresh=fresh, by_x=by_x, by_z=by_z, warmed=warmed):
                below, here = carry
                above = warmed(jnp.minimum(z + 1, levels_c - 1))
                new = stencil(here, below, above, by_x, by_z)
                if n == MAX_SUB - 1:
                    put_strided(plain_energy, z, new)
                else:
                    put_packed(fresh, z, new)
                return here, above

            edge = warmed(0)
            lax.fori_loop(0, levels_c, follow, (edge, edge), unroll=UNROLL)

        power = jnp.full((1, slots), CENTRE, F32)
        for n in range(1, MAX_SUB):
            power = jnp.where(counts > float(n), CENTRE ** (n + 1), power)
        used = jnp.broadcast_to(counts, (across, slots)) > 0.0
        power = jnp.broadcast_to(power, (across, slots))
        for f in range(2):
            offsets[f] = offset[f]

            def narrow(z, carry, f=f):
                x = plain[f][z]
                if f == 0:
                    x = x + LATENT * drops[MAX_SUB - 1, z]
                x = power * x + jnp.broadcast_to(offsets[f, pl.ds(z, 1), :], x.shape)
                block[0, f, z] = jnp.where(used, x, block[0, f, z].astype(F32)).astype(BF16)
                return carry

            lax.fori_loop(0, levels_c, narrow, 0, unroll=UNROLL)

    @pl.when(jnp.logical_not(is_cloud))
    def _():
        push_arrives()
        to_left.start()
        fetches[7].wait()

    near_e = jnp.transpose(
        jnp.concatenate([near, jnp.zeros((3 * elements, 128 - elements), F32)], axis=1)
    )[:elements].astype(BF16)
    to_left.wait_recv()
    around = jnp.concatenate([given[0:elements], beyond[...], own], axis=0)
    spread = rate * pick(near_e, around)
    adv_ref[...] = base
    for k in range(4):
        adv_ref[pl.ds(k, elements, stride=4), :] += spread
    slot_column = jnp.transpose(jnp.broadcast_to(slot, (128, rows)))[:, 0:1]
    member = jnp.where(
        slot_column == iota((rows, (n_sec - 1) * slots), 1).astype(F32), 1.0, 0.0
    ).astype(BF16)

    def heard(source):
        pltpu.make_async_copy(tends.at[source], tends.at[source], tend_recv_sem.at[source]).wait()

    def passing(source):
        return pltpu.make_async_remote_copy(
            src_ref=tends.at[source], dst_ref=tends.at[source],
            send_sem=core_send_sem.at[source], recv_sem=core_recv_sem.at[source],
            device_id=(sibling, col), device_id_type=MESH,
        )

    def gather(sources):
        for source in sources:
            found = tends[source].reshape(slots, width)
            adv_ref[...] += pick(member[:, source * slots : (source + 1) * slots], found)

    for mine, theirs in (((1,), (0, 2)), ((0, 2), (1,))):

        @pl.when(core == len(mine) - 1)
        def _():
            for source in mine:
                heard(source)
                passing(source).start()
            gather(mine)
            for source in theirs:
                passing(source).wait_recv()
            gather(theirs)

    summed = adv_ref[...]
    out_ref[...] = jnp.where(
        iota((rows, width), 1) >= levels_h, jnp.maximum(summed, 0.0), summed
    )

    @pl.when(jnp.logical_not(is_cloud))
    def _():
        for section in (2, 1):
            push(section).wait_send()

    @pl.when(relays)
    def _():
        relay.wait_send()

    to_left.wait_send()

    for mine in ((1,), (0, 2)):

        @pl.when(core == len(mine) - 1)
        def _():
            for source in mine:
                passing(source).wait_send()

    @pl.when(is_cloud)
    def _():
        others = pl.ds(0, n_col - 1)
        pltpu.make_async_copy(disp_send.at[others], disp_send.at[others], disp_send_sem).wait()
        pltpu.make_async_copy(tend_send.at[others], tend_send.at[others], tend_send_sem.at[0]).wait()
        pltpu.make_async_copy(tend_send, tend_send, tend_send_sem.at[1]).wait()


def body(
    column_state, mixing_rate, neighbours, assignment, substeps, cloud_state, level_map, saturation
):
    n_sec, n_col = lax.axis_size("sec"), lax.axis_size("col")
    rows, width = column_state.shape
    elements = rows // 4
    _, fields, levels_c, across, slots = cloud_state.shape
    cap, levels_h = slots // n_col, level_map.shape[1]
    vmem = pl.BlockSpec(memory_space=pltpu.VMEM)
    hbm = pl.BlockSpec(memory_space=pltpu.HBM)
    message = (n_col, cap, width)
    dma = pltpu.SemaphoreType.DMA
    results = (
        jax.ShapeDtypeStruct(column_state.shape, F32),
        jax.ShapeDtypeStruct(cloud_state.shape, BF16),
    )
    operands = (
        column_state,
        mixing_rate.reshape(1, width),
        neighbours.T,
        assignment.reshape(1, rows),
        substeps.reshape(1, rows),
        cloud_state,
        level_map,
        saturation.reshape(1, levels_c),
    )
    return pl.pallas_call(
        functools.partial(kernel, (n_sec, n_col)),
        out_shape=tuple(pltpu.VMEM(r.shape, r.dtype) for r in results),
        in_specs=[hbm] * 8,
        out_specs=(vmem, vmem),
        scratch_shapes=[
            pltpu.VMEM((rows, width), F32),
            pltpu.VMEM((1, width), F32),
            pltpu.VMEM((4, elements), I32),
            pltpu.VMEM((1, rows), I32),
            pltpu.VMEM((1, rows), I32),
            pltpu.VMEM((levels_c, levels_h), F32),
            pltpu.VMEM((1, levels_c), F32),
            *[pltpu.VMEM((levels_c, across, slots), F32)] * 6,
            pltpu.VMEM((MAX_SUB, levels_c, across, slots), F32),
            pltpu.VMEM((fields, levels_h, 8, slots), F32),
            pltpu.VMEM((levels_h, slots), F32),
            pltpu.VMEM((fields, levels_h, slots), F32),
            pltpu.VMEM((fields * levels_h, fields * levels_h), F32),
            pltpu.VMEM((elements + 8, width), F32),
            pltpu.VMEM((elements + 8, width), F32),
            pltpu.VMEM((elements, width), F32),
            pltpu.VMEM((n_col, cap, 2 * width), F32),
            pltpu.VMEM((n_col, cap, 2 * width), F32),
            pltpu.VMEM(message, F32),
            pltpu.VMEM((n_sec - 1,) + message, F32),
            pltpu.VMEM((rows, width), F32),
            dma((8,)),
            dma((2,)),
            dma,
            dma,
            dma((2,)),
            dma,
            dma,
            dma((2,)),
            dma((n_sec - 1,)),
            dma((n_sec - 1,)),
            dma((n_sec - 1,)),
        ],
        compiler_params=pltpu.CompilerParams(
            collective_id=0, has_side_effects=True, vmem_limit_bytes=48 * 1024 * 1024
        ),
    )(*(pltpu.with_memory_space_constraint(x, pltpu.HBM) for x in operands))


def solution(mesh):
    in_specs = (
        P("col", None),
        P(),
        P("col", None),
        P("col", None),
        P("col"),
        P("sec", None, None, None, "col"),
        P(),
        P(),
    )
    out_specs = (P("col", None), P("sec", None, None, None, "col"))
    return jax.shard_map(body, mesh=mesh, in_specs=in_specs, out_specs=out_specs, check_vma=False)
```

```python
import functools

import jax
import jax.numpy as jnp
from jax import lax
from jax.experimental import pallas as pl
from jax.experimental.pallas import tpu as pltpu
from jax.sharding import PartitionSpec as P

MAX_SUB = 4
RELAX = 0.25
HORIZ = 0.12
VERTIC = 0.1
LATENT = 2.5
VMIX = 0.2
UNROLL = 29
CENTRE = 1.0 - 2.0 * HORIZ - 2.0 * VERTIC
MESH = pl.DeviceIdType.MESH
F32 = jnp.float32
BF16 = jnp.bfloat16
I32 = jnp.int32
NN = (((1,), (0,)), ((), ()))
NT = (((1,), (1,)), ((), ()))
ACROSS = ((2, 1), (1, 1), (3, 1), (2, 0), (0, 1), (1, 0), (3, 0), (0, 0))


def iota(shape, dim):
    return lax.broadcasted_iota(I32, shape, dim)


def halves(x):
    hi = x.astype(BF16)
    return hi, (x - hi.astype(F32)).astype(BF16)


def dot(a, b, dims=NN):
    return lax.dot_general(a, b, dims, preferred_element_type=F32)


def joined(lefts, rights, dims):
    (left_dims, right_dims), _ = dims
    return dot(
        jnp.concatenate(lefts, axis=left_dims[0]), jnp.concatenate(rights, axis=right_dims[0]), dims
    )


def pick(exact, x, dims=NN):
    hi, lo = halves(x)
    if exact.shape[1] % 128:
        return dot(exact, hi, dims) + dot(exact, lo, dims)
    return joined([exact, exact], [hi, lo], dims)


def dot3(x, y, dims=NN):
    xh, xl = halves(x)
    yh, yl = halves(y)
    return joined([xh, xh, xl], [yh, yl, yh], dims)


def for_others(col, visit):
    y, x, z = col // 16, lax.rem(col // 8, 2), lax.rem(col, 8)
    bases = [lax.rem(y + dy, 4) * 16 + lax.rem(x + dx, 2) * 8 for dy, dx in ACROSS]

    def ring(t, carry):
        half = (t + 1) // 2
        dz = 4 + half - 2 * half * lax.rem(t, 2)
        along = lax.rem(z + dz, 8)
        for base in bases:
            visit(base + along)
        return carry

    lax.fori_loop(0, 7, ring, 0)
    for base in bases[:-1]:
        visit(base + z)


def kernel(
    sizes,
    cs_hbm,
    rate_hbm,
    nbr_hbm,
    asg_hbm,
    cnt_hbm,
    cloud_hbm,
    map_hbm,
    sat_hbm,
    out_ref,
    block,
    cs_ref,
    rate_ref,
    nbr_ref,
    asg_ref,
    cnt_ref,
    map_ref,
    sat_ref,
    plain_energy,
    plain_water,
    energy_a,
    energy_b,
    water_a,
    water_b,
    parts,
    limits,
    offsets,
    square,
    pushed,
    given,
    beyond,
    disp_send,
    disp_recv,
    tend_send,
    tends,
    adv_ref,
    local_sem,
    push_send_sem,
    push_recv_sem,
    relay_sem,
    beyond_sem,
    disp_send_sem,
    disp_recv_sem,
    tend_send_sem,
    tend_recv_sem,
    core_send_sem,
    core_recv_sem,
):
    n_sec, n_col = sizes
    sec, col = lax.axis_index("sec"), lax.axis_index("col")
    rows, width = cs_ref.shape
    elements = rows // 4
    total = elements * n_col
    cap, slots = disp_send.shape[1], n_col * disp_send.shape[1]
    levels_c, levels_h = map_ref.shape
    left, right = lax.rem(col + n_col - 1, n_col), lax.rem(col + 1, n_col)
    is_cloud = sec > 0
    plain = (plain_energy, plain_water)
    across = plain_water.shape[1]
    core = lax.rem(sec, 2)
    sibling = sec + 1 - 2 * core
    facing = lax.rem(sec + 2, n_sec)

    fetches = [
        pltpu.make_async_copy(src, dst, local_sem.at[i])
        for i, (src, dst) in enumerate(
            (
                (asg_hbm, asg_ref),
                (nbr_hbm, nbr_ref),
                (cs_hbm, cs_ref),
                (rate_hbm, rate_ref),
                (map_hbm, map_ref),
                (cnt_hbm, cnt_ref),
                (sat_hbm, sat_ref),
                (cloud_hbm, block),
            )
        )
    ]
    for fetch in fetches:
        fetch.start()

    barrier = pltpu.get_barrier_semaphore()

    def greet(device):
        pl.semaphore_signal(barrier, inc=1, device_id=device, device_id_type=MESH)

    greet((0, left))

    @pl.when(is_cloud)
    def _():
        for_others(col, lambda other: greet((sec, other)))

    greet((sibling, col))

    @pl.when(sec != 2)
    def _():
        greet((facing, col))

    fetches[0].wait()
    fetches[1].wait()

    asg = asg_ref[...]
    asg_column = jnp.transpose(jnp.broadcast_to(asg.astype(F32), (128, rows)))[:, 0:1]
    same = (asg_column == asg.astype(F32)) & (iota((rows, rows), 0) < iota((rows, rows), 1))
    rank = jnp.max(jnp.where(same, 1.0, 0.0), axis=0, keepdims=True)
    slot = (asg * cap).astype(F32) + rank

    pushed[elements : elements + 4, 0:elements] = nbr_ref[...].astype(F32)
    pushed[elements + 4 : elements + 5] = slot[:, :width]
    pushed[elements + 5 : elements + 6] = slot[:, width:]

    fetches[2].wait()
    own = (
        cs_ref[pl.ds(0, elements, stride=4), :]
        + cs_ref[pl.ds(1, elements, stride=4), :]
        + cs_ref[pl.ds(2, elements, stride=4), :]
        + cs_ref[pl.ds(3, elements, stride=4), :]
    ) * 0.25
    pushed[0:elements] = own

    def push(section):
        return pltpu.make_async_remote_copy(
            src_ref=pushed, dst_ref=given,
            send_sem=push_send_sem.at[section - 1], recv_sem=push_recv_sem,
            device_id=(section, right), device_id_type=MESH,
        )

    relays = (sec == 1) | (sec == 2)
    relay = pltpu.make_async_remote_copy(
        src_ref=given, dst_ref=given, send_sem=relay_sem, recv_sem=push_recv_sem,
        device_id=(sibling, col), device_id_type=MESH,
    )

    def push_arrives():
        relay.wait_recv()

        @pl.when(relays)
        def _():
            relay.start()

    means = pushed.at[pl.ds(0, elements)]
    to_left = pltpu.make_async_remote_copy(
        src_ref=means, dst_ref=beyond, send_sem=beyond_sem.at[0], recv_sem=beyond_sem.at[1],
        device_id=(sec, left), device_id_type=MESH,
    )

    @pl.when(jnp.logical_not(is_cloud))
    def _():
        pl.semaphore_wait(barrier, n_sec + 1)
        for section in (2, 1):
            push(section).start()

    for fetch in fetches[3:7]:
        fetch.wait()

    place = iota((3 * elements, elements), 0)
    place = jnp.where(
        place < elements, place, jnp.where(place < 2 * elements, place + elements, place - elements)
    )
    near = jnp.where(place == elements + iota((3 * elements, elements), 1), -4.0, 0.0)
    relative = jnp.bitwise_and(nbr_ref[...] - (col - 1) * elements, total - 1)
    for k in range(4):
        near = near + jnp.where(relative[k : k + 1, :] == place, 1.0, 0.0)
    near_t = near.astype(BF16)

    cs = cs_ref[...]
    lane = jnp.bitwise_and(iota((rows, width), 1), levels_h - 1)
    upper = jnp.where(lane == levels_h - 1, cs, pltpu.roll(cs, width - 1, axis=1))
    lower = jnp.where(lane == 0, cs, pltpu.roll(cs, 1, axis=1))
    base = cs + VMIX * (upper + lower - 2.0 * cs)
    rate = rate_ref[...]

    square[...] = jnp.zeros_like(square)
    square[0:levels_c, 0:levels_h] = map_ref[...]
    square[levels_h : levels_h + levels_c, levels_h : 2 * levels_h] = map_ref[...]

    @pl.when(is_cloud)
    def _():
        chosen = iota((slots, rows), 0) + (sec - 1) * slots == slot.astype(I32)
        chosen32 = jnp.where(chosen, 1.0, 0.0)
        chosen16 = chosen32.astype(BF16)
        counts_out = jnp.sum(chosen32 * cnt_ref[...].astype(F32), axis=1, keepdims=True)
        repeat = jnp.where(
            iota((elements, rows), 0) == lax.shift_right_logical(iota((elements, rows), 1), 2), 1.0, 0.0
        ).astype(BF16)
        by_element = dot(chosen16, repeat, NT).astype(BF16)
        reach = dot(by_element, near_t, NT).astype(BF16)
        known = pick(chosen16, base) + rate * pick(reach[:, 2 * elements :], own)
        reach = reach[:, :elements]

        push_arrives()
        sent = known + rate * pick(reach, given[0:elements])
        slot_left = jnp.concatenate([given[elements + 4 : elements + 5], given[elements + 5 : elements + 6]], axis=1)
        chosen_left = jnp.where(
            iota((slots, rows), 0) + (sec - 1) * slots == slot_left.astype(I32), 1.0, 0.0
        ).astype(BF16)
        nbr_left = given[elements : elements + 4, 0:elements].astype(I32)
        here = iota((elements, elements), 0) + col * elements
        near_left = jnp.zeros((elements, elements), F32)
        for k in range(4):
            near_left = near_left + jnp.where(nbr_left[k : k + 1, :] == here, 1.0, 0.0)
        reach_left = dot(dot(chosen_left, repeat, NT).astype(BF16), near_left.astype(BF16), NT)
        extra = rate * pick(reach_left.astype(BF16), own)
        both = dot3(jnp.concatenate([sent, extra], axis=0), square[...], NT)
        target = jnp.where(iota((slots, width), 1) == levels_c, counts_out, both[:slots])
        disp_send[:, :, 0:width] = target.reshape(n_col, cap, width)
        disp_send[:, :, width:] = both[slots:].reshape(n_col, cap, width)

        pl.semaphore_wait(barrier, n_col + 1)
        def send(other):
            pltpu.make_async_remote_copy(
                src_ref=disp_send.at[other], dst_ref=disp_recv.at[col],
                send_sem=disp_send_sem, recv_sem=disp_recv_sem,
                device_id=(sec, other), device_id_type=MESH,
            ).start()

        for_others(col, send)
        pltpu.make_async_copy(disp_send.at[col], disp_recv.at[col], disp_recv_sem).start()
        to_left.start()

        fetches[7].wait()
        for f in range(2):
            parts[f, 8 * levels_c :] = jnp.zeros((8 * (levels_h - levels_c), slots), F32)

        def widen(z, carry):
            water = block[0, 1, z].astype(F32)
            for f, x in ((1, water), (0, block[0, 0, z].astype(F32) + LATENT * water)):
                plain[f][z] = x
                parts[f, pl.ds(8 * z, 8), :] = (x[0:8] + x[8:16]) + (x[16:24] + x[24:32])
            return carry

        lax.fori_loop(0, levels_c, widen, 0, unroll=UNROLL)

        def over_columns(f):
            return sum(parts[f, pl.ds(k, levels_h, stride=8), :] for k in range(8))

        def strided(ref, z):
            return tuple(ref[z, pl.ds(k, 8, stride=4), :] for k in range(4))

        def packed(ref, z):
            return tuple(ref[z, pl.ds(8 * k, 8), :] for k in range(4))

        def put_strided(ref, z, tiles):
            for k in range(4):
                ref[z, pl.ds(k, 8, stride=4), :] = tiles[k]

        def put_packed(ref, z, tiles):
            for k in range(4):
                ref[z, pl.ds(8 * k, 8), :] = tiles[k]

        def stencil(here, below, above, by_x, by_z):
            west = (pltpu.roll(here[3], 1, axis=0),) + here[:3]
            east = here[1:] + (pltpu.roll(here[0], 7, axis=0),)
            return tuple(
                here[k] + (by_x * (east[k] + west[k]) + by_z * (above[k] + below[k]))
                for k in range(4)
            )

        for f in range(2):

            def first(z, carry, f=f):
                below, here = carry
                above = strided(plain[f], jnp.minimum(z + 1, levels_c - 1))
                put_packed(
                    (energy_a, water_a)[f], z, stencil(here, below, above, HORIZ / CENTRE, VERTIC / CENTRE)
                )
                return here, above

            edge = strided(plain[f], 0)
            lax.fori_loop(0, levels_c, first, (edge, edge), unroll=UNROLL)

        columns_inv = 1.0 / across
        start = [over_columns(f) * columns_inv for f in range(2)]
        level = iota((levels_h, slots), 0)
        wet = jnp.concatenate([sat_ref[...], jnp.zeros((1, 128 - levels_c), F32)], axis=1)
        wet = jnp.transpose(jnp.broadcast_to(wet, (128, 128)))[:levels_h]

        def smoothed(x):
            up = jnp.where(level == levels_c - 1, x, pltpu.roll(x, levels_h - 1, axis=0))
            low = jnp.where(level == 0, x, pltpu.roll(x, 1, axis=0))
            return (1.0 - 2.0 * VERTIC) * x + VERTIC * (up + low)

        pltpu.make_async_copy(disp_recv, disp_recv, disp_recv_sem).wait()
        later = disp_recv[:, :, width:].reshape(slots, width)
        arrived = jnp.transpose(
            disp_recv[:, :, 0:width].reshape(slots, width) + pltpu.roll(later, slots - cap, axis=0)
        )
        counts = arrived[levels_c : levels_c + 1, :]
        counts8 = jnp.broadcast_to(counts, (8, slots))
        goal = [arrived[f * levels_h : (f + 1) * levels_h] for f in range(2)]
        goal[0] = goal[0] + LATENT * goal[1]
        mean = list(start)
        offset = [jnp.zeros((levels_h, slots), F32)] * 2

        for n in range(MAX_SUB):
            scale = CENTRE ** (n + 1)
            keep = counts > float(n)
            d = [RELAX * (goal[f] - mean[f]) for f in range(2)]
            moved = smoothed(mean[0] + d[0])
            shifted = [smoothed(offset[f] + d[f]) for f in range(2)]
            limit = (0.5 / scale) * (wet - shifted[1])
            limits[...] = limit if n == 0 else jnp.where(keep, limit, 0.0)

            def condense(water, z, by_half):
                bound = jnp.broadcast_to(limits[pl.ds(z, 1), :], (8, slots))
                new = [jnp.minimum(water[k], by_half * water[k] + bound) for k in range(4)]
                parts[1, pl.ds(8 * z, 8), :] = (new[0] + new[1]) + (new[2] + new[3])
                return new

            if n == 0:

                def finish(z, carry):
                    put_packed(water_b, z, condense(packed(water_a, z), z, 0.5))
                    return carry

                lax.fori_loop(0, levels_c, finish, 0, unroll=UNROLL)
            else:
                going = jnp.where(counts8 > float(n), 1.0, 0.0)
                by_x, by_z, by_half = going * (HORIZ / CENTRE), going * (VERTIC / CENTRE), 1.0 - going * 0.5
                old, fresh = (water_b, water_a) if n % 2 else (water_a, water_b)

                def sweep(z, carry, n=n, old=old, fresh=fresh, by_x=by_x, by_z=by_z, by_half=by_half):
                    below, here = carry
                    above = packed(old, jnp.minimum(z + 1, levels_c - 1))
                    new = condense(stencil(here, below, above, by_x, by_z), z, by_half)
                    if n == MAX_SUB - 1:
                        put_strided(plain_water, z, new)
                    else:
                        put_packed(fresh, z, new)
                    return here, above

                edge = packed(old, 0)
                lax.fori_loop(0, levels_c, sweep, (edge, edge), unroll=UNROLL)

            dried = over_columns(1) * (columns_inv * scale) + shifted[1]
            mean[0] = jnp.where(keep, moved, mean[0])
            mean[1] = jnp.where(keep, dried, mean[1])
            offset = [jnp.where(keep, shifted[f], offset[f]) for f in range(2)]

        gain = [jnp.where(level < levels_c, mean[f] - start[f], 0.0) for f in range(2)]
        change = jnp.concatenate([gain[0] - LATENT * gain[1], gain[1]], axis=0)
        tendency = dot3(jnp.transpose(change), square[...])
        tend_send[...] = tendency.reshape(n_col, cap, width)

        def give(other, chip):
            pltpu.make_async_remote_copy(
                src_ref=tend_send.at[other], dst_ref=tends.at[sec - 1, col],
                send_sem=tend_send_sem.at[chip], recv_sem=tend_recv_sem.at[sec - 1],
                device_id=((sec, facing)[chip], other), device_id_type=MESH,
            ).start()

        def give_both(other):
            give(other, 1)
            give(other, 0)

        for_others(col, give_both)
        give(col, 1)
        pltpu.make_async_copy(tend_send.at[col], tends.at[sec - 1, col], tend_recv_sem.at[sec - 1]).start()

        for n in range(1, MAX_SUB):
            going = jnp.where(counts8 > float(n), 1.0, 0.0)
            by_x, by_z = going * (HORIZ / CENTRE), going * (VERTIC / CENTRE)

            old, fresh = (energy_a, energy_b) if n % 2 else (energy_b, energy_a)

            def follow(z, carry, n=n, old=old, fresh=fresh, by_x=by_x, by_z=by_z):
                below, here = carry
                above = packed(old, jnp.minimum(z + 1, levels_c - 1))
                new = stencil(here, below, above, by_x, by_z)
                if n == MAX_SUB - 1:
                    put_strided(plain_energy, z, new)
                else:
                    put_packed(fresh, z, new)
                return here, above

            edge = packed(old, 0)
            lax.fori_loop(0, levels_c, follow, (edge, edge), unroll=UNROLL)

        power = jnp.full((1, slots), CENTRE, F32)
        for n in range(1, MAX_SUB):
            power = jnp.where(counts > float(n), CENTRE ** (n + 1), power)
        used = jnp.broadcast_to(counts, (across, slots)) > 0.0
        power = jnp.broadcast_to(power, (across, slots))
        for f in range(2):
            offsets[f] = offset[f]

        def narrow(z, carry):
            x = [
                power * plain[f][z] + jnp.broadcast_to(offsets[f, pl.ds(z, 1), :], power.shape)
                for f in range(2)
            ]
            x[0] = x[0] - LATENT * x[1]
            for f in range(2):
                block[0, f, z] = jnp.where(used, x[f], block[0, f, z].astype(F32)).astype(BF16)
            return carry

        lax.fori_loop(0, levels_c, narrow, 0, unroll=UNROLL)

    @pl.when(jnp.logical_not(is_cloud))
    def _():
        push_arrives()
        to_left.start()
        fetches[7].wait()

    near_e = jnp.transpose(
        jnp.concatenate([near, jnp.zeros((3 * elements, 128 - elements), F32)], axis=1)
    )[:elements].astype(BF16)
    to_left.wait_recv()
    around = jnp.concatenate([given[0:elements], beyond[...], own], axis=0)
    spread = rate * pick(near_e, around)
    adv_ref[...] = base
    for k in range(4):
        adv_ref[pl.ds(k, elements, stride=4), :] += spread
    slot_column = jnp.transpose(jnp.broadcast_to(slot, (128, rows)))[:, 0:1]
    member = jnp.where(
        slot_column == iota((rows, (n_sec - 1) * slots), 1).astype(F32), 1.0, 0.0
    ).astype(BF16)

    def heard(source):
        pltpu.make_async_copy(tends.at[source], tends.at[source], tend_recv_sem.at[source]).wait()

    def passing(source):
        return pltpu.make_async_remote_copy(
            src_ref=tends.at[source], dst_ref=tends.at[source],
            send_sem=core_send_sem.at[source], recv_sem=core_recv_sem.at[source],
            device_id=(sibling, col), device_id_type=MESH,
        )

    def gather(sources):
        found = [tends[source].reshape(slots, width) for source in sources]
        where = [member[:, source * slots : (source + 1) * slots] for source in sources]
        adv_ref[...] += pick(jnp.concatenate(where, axis=1), jnp.concatenate(found, axis=0))

    for mine, theirs in (((1,), (0, 2)), ((0, 2), (1,))):

        @pl.when(core == len(mine) - 1)
        def _():
            for source in mine:
                heard(source)
                passing(source).start()
            gather(mine)
            for source in theirs:
                passing(source).wait_recv()
            gather(theirs)

    summed = adv_ref[...]
    out_ref[...] = jnp.where(
        iota((rows, width), 1) >= levels_h, jnp.maximum(summed, 0.0), summed
    )

    @pl.when(jnp.logical_not(is_cloud))
    def _():
        for section in (2, 1):
            push(section).wait_send()

    @pl.when(relays)
    def _():
        relay.wait_send()

    to_left.wait_send()

    for mine in ((1,), (0, 2)):

        @pl.when(core == len(mine) - 1)
        def _():
            for source in mine:
                passing(source).wait_send()

    @pl.when(is_cloud)
    def _():
        others = pl.ds(0, n_col - 1)
        pltpu.make_async_copy(disp_send.at[others], disp_send.at[others], disp_send_sem).wait()
        pltpu.make_async_copy(tend_send.at[others], tend_send.at[others], tend_send_sem.at[0]).wait()
        pltpu.make_async_copy(tend_send, tend_send, tend_send_sem.at[1]).wait()


def body(
    column_state, mixing_rate, neighbours, assignment, substeps, cloud_state, level_map, saturation
):
    n_sec, n_col = lax.axis_size("sec"), lax.axis_size("col")
    rows, width = column_state.shape
    elements = rows // 4
    _, fields, levels_c, across, slots = cloud_state.shape
    cap, levels_h = slots // n_col, level_map.shape[1]
    vmem = pl.BlockSpec(memory_space=pltpu.VMEM)
    hbm = pl.BlockSpec(memory_space=pltpu.HBM)
    message = (n_col, cap, width)
    dma = pltpu.SemaphoreType.DMA
    results = (
        jax.ShapeDtypeStruct(column_state.shape, F32),
        jax.ShapeDtypeStruct(cloud_state.shape, BF16),
    )
    operands = (
        column_state,
        mixing_rate.reshape(1, width),
        neighbours.T,
        assignment.reshape(1, rows),
        substeps.reshape(1, rows),
        cloud_state,
        level_map,
        saturation.reshape(1, levels_c),
    )
    return pl.pallas_call(
        functools.partial(kernel, (n_sec, n_col)),
        out_shape=tuple(pltpu.VMEM(r.shape, r.dtype) for r in results),
        in_specs=[hbm] * 8,
        out_specs=(vmem, vmem),
        scratch_shapes=[
            pltpu.VMEM((rows, width), F32),
            pltpu.VMEM((1, width), F32),
            pltpu.VMEM((4, elements), I32),
            pltpu.VMEM((1, rows), I32),
            pltpu.VMEM((1, rows), I32),
            pltpu.VMEM((levels_c, levels_h), F32),
            pltpu.VMEM((1, levels_c), F32),
            *[pltpu.VMEM((levels_c, across, slots), F32)] * 6,
            pltpu.VMEM((fields, 8 * levels_h, slots), F32),
            pltpu.VMEM((levels_h, slots), F32),
            pltpu.VMEM((fields, levels_h, slots), F32),
            pltpu.VMEM((fields * levels_h, fields * levels_h), F32),
            pltpu.VMEM((elements + 8, width), F32),
            pltpu.VMEM((elements + 8, width), F32),
            pltpu.VMEM((elements, width), F32),
            pltpu.VMEM((n_col, cap, 2 * width), F32),
            pltpu.VMEM((n_col, cap, 2 * width), F32),
            pltpu.VMEM(message, F32),
            pltpu.VMEM((n_sec - 1,) + message, F32),
            pltpu.VMEM((rows, width), F32),
            dma((8,)),
            dma((2,)),
            dma,
            dma,
            dma((2,)),
            dma,
            dma,
            dma((2,)),
            dma((n_sec - 1,)),
            dma((n_sec - 1,)),
            dma((n_sec - 1,)),
        ],
        compiler_params=pltpu.CompilerParams(
            collective_id=0, has_side_effects=True, vmem_limit_bytes=48 * 1024 * 1024
        ),
    )(*(pltpu.with_memory_space_constraint(x, pltpu.HBM) for x in operands))


def solution(mesh):
    in_specs = (
        P("col", None),
        P(),
        P("col", None),
        P("col", None),
        P("col"),
        P("sec", None, None, None, "col"),
        P(),
        P(),
    )
    out_specs = (P("col", None), P("sec", None, None, None, "col"))
    return jax.shard_map(body, mesh=mesh, in_specs=in_specs, out_specs=out_specs, check_vma=False)
```

```python
import functools

import jax
import jax.numpy as jnp
from jax import lax
from jax.experimental import pallas as pl
from jax.experimental.pallas import tpu as pltpu
from jax.sharding import PartitionSpec as P

MAX_SUB = 4
RELAX = 0.25
HORIZ = 0.12
VERTIC = 0.1
LATENT = 2.5
VMIX = 0.2
UNROLL = 29
CENTRE = 1.0 - 2.0 * HORIZ - 2.0 * VERTIC
MESH = pl.DeviceIdType.MESH
F32 = jnp.float32
BF16 = jnp.bfloat16
I32 = jnp.int32
NN = (((1,), (0,)), ((), ()))
NT = (((1,), (1,)), ((), ()))
ACROSS = ((2, 1), (1, 1), (3, 1), (2, 0), (0, 1), (1, 0), (3, 0), (0, 0))


def iota(shape, dim):
    return lax.broadcasted_iota(I32, shape, dim)


def halves(x):
    hi = x.astype(BF16)
    return hi, (x - hi.astype(F32)).astype(BF16)


def dot(a, b, dims=NN):
    return lax.dot_general(a, b, dims, preferred_element_type=F32)


def joined(lefts, rights, dims):
    (left_dims, right_dims), _ = dims
    return dot(
        jnp.concatenate(lefts, axis=left_dims[0]), jnp.concatenate(rights, axis=right_dims[0]), dims
    )


def pick(exact, x, dims=NN):
    hi, lo = halves(x)
    if exact.shape[1] % 128:
        return dot(exact, hi, dims) + dot(exact, lo, dims)
    return joined([exact, exact], [hi, lo], dims)


def dot3(x, y, dims=NN):
    xh, xl = halves(x)
    yh, yl = halves(y)
    return joined([xh, xh, xl], [yh, yl, yh], dims)


def for_others(col, visit):
    y, x, z = col // 16, lax.rem(col // 8, 2), lax.rem(col, 8)
    bases = [lax.rem(y + dy, 4) * 16 + lax.rem(x + dx, 2) * 8 for dy, dx in ACROSS]

    def ring(t, carry):
        half = (t + 1) // 2
        dz = 4 + half - 2 * half * lax.rem(t, 2)
        along = lax.rem(z + dz, 8)
        for base in bases:
            visit(base + along)
        return carry

    lax.fori_loop(0, 7, ring, 0)
    for base in bases[:-1]:
        visit(base + z)


def kernel(
    sizes,
    cs_hbm,
    rate_hbm,
    nbr_hbm,
    asg_hbm,
    cnt_hbm,
    cloud_hbm,
    map_hbm,
    sat_hbm,
    out_ref,
    block,
    cs_ref,
    rate_ref,
    nbr_ref,
    asg_ref,
    cnt_ref,
    map_ref,
    sat_ref,
    plain_energy,
    plain_water,
    energy_a,
    energy_b,
    water_a,
    water_b,
    parts,
    limits,
    offsets,
    square,
    pushed,
    given,
    beyond,
    disp_send,
    disp_recv,
    tend_send,
    tends,
    adv_ref,
    local_sem,
    push_send_sem,
    push_recv_sem,
    relay_sem,
    beyond_sem,
    disp_send_sem,
    disp_recv_sem,
    tend_send_sem,
    tend_recv_sem,
    core_send_sem,
    core_recv_sem,
):
    n_sec, n_col = sizes
    sec, col = lax.axis_index("sec"), lax.axis_index("col")
    rows, width = cs_ref.shape
    elements = rows // 4
    total = elements * n_col
    cap, slots = disp_send.shape[1], n_col * disp_send.shape[1]
    levels_c, levels_h = map_ref.shape
    left, right = lax.rem(col + n_col - 1, n_col), lax.rem(col + 1, n_col)
    is_cloud = sec > 0
    plain = (plain_energy, plain_water)
    across = plain_water.shape[1]
    core = lax.rem(sec, 2)
    sibling = sec + 1 - 2 * core
    facing = lax.rem(sec + 2, n_sec)

    fetches = [
        pltpu.make_async_copy(src, dst, local_sem.at[i])
        for i, (src, dst) in enumerate(
            (
                (asg_hbm, asg_ref),
                (nbr_hbm, nbr_ref),
                (cs_hbm, cs_ref),
                (rate_hbm, rate_ref),
                (map_hbm, map_ref),
                (cnt_hbm, cnt_ref),
                (sat_hbm, sat_ref),
                (cloud_hbm, block),
            )
        )
    ]
    for fetch in fetches:
        fetch.start()

    barrier = pltpu.get_barrier_semaphore()

    def greet(device):
        pl.semaphore_signal(barrier, inc=1, device_id=device, device_id_type=MESH)

    greet((0, left))

    @pl.when(is_cloud)
    def _():
        for_others(col, lambda other: greet((sec, other)))

    greet((sibling, col))

    @pl.when(core == 1)
    def _():
        greet((facing, col))

    @pl.when(sec == 1)
    def _():
        greet((2, col))

    fetches[0].wait()
    fetches[1].wait()

    asg = asg_ref[...]
    asg_column = jnp.transpose(jnp.broadcast_to(asg.astype(F32), (128, rows)))[:, 0:1]
    same = (asg_column == asg.astype(F32)) & (iota((rows, rows), 0) < iota((rows, rows), 1))
    rank = jnp.max(jnp.where(same, 1.0, 0.0), axis=0, keepdims=True)
    slot = (asg * cap).astype(F32) + rank

    pushed[elements : elements + 4, 0:elements] = nbr_ref[...].astype(F32)
    pushed[elements + 4 : elements + 5] = slot[:, :width]
    pushed[elements + 5 : elements + 6] = slot[:, width:]

    fetches[2].wait()
    own = (
        cs_ref[pl.ds(0, elements, stride=4), :]
        + cs_ref[pl.ds(1, elements, stride=4), :]
        + cs_ref[pl.ds(2, elements, stride=4), :]
        + cs_ref[pl.ds(3, elements, stride=4), :]
    ) * 0.25
    pushed[0:elements] = own

    def push(section):
        return pltpu.make_async_remote_copy(
            src_ref=pushed, dst_ref=given,
            send_sem=push_send_sem.at[section - 1], recv_sem=push_recv_sem,
            device_id=(section, right), device_id_type=MESH,
        )

    relays = (sec == 1) | (sec == 2)
    relay = pltpu.make_async_remote_copy(
        src_ref=given, dst_ref=given, send_sem=relay_sem, recv_sem=push_recv_sem,
        device_id=(sibling, col), device_id_type=MESH,
    )

    def push_arrives():
        relay.wait_recv()

        @pl.when(relays)
        def _():
            relay.start()

    means = pushed.at[pl.ds(0, elements)]
    to_left = pltpu.make_async_remote_copy(
        src_ref=means, dst_ref=beyond, send_sem=beyond_sem.at[0], recv_sem=beyond_sem.at[1],
        device_id=(sec, left), device_id_type=MESH,
    )

    @pl.when(jnp.logical_not(is_cloud))
    def _():
        pl.semaphore_wait(barrier, n_sec + 1)
        for section in (2, 1):
            push(section).start()

    def give(other, chip):
        return pltpu.make_async_remote_copy(
            src_ref=tend_send.at[other], dst_ref=tends.at[sec - 1, col],
            send_sem=tend_send_sem.at[chip], recv_sem=tend_recv_sem.at[sec - 1],
            device_id=(2 * chip + 1, other), device_id_type=MESH,
        )

    for fetch in fetches[3:7]:
        fetch.wait()

    place = iota((3 * elements, elements), 0)
    place = jnp.where(
        place < elements, place, jnp.where(place < 2 * elements, place + elements, place - elements)
    )
    near = jnp.where(place == elements + iota((3 * elements, elements), 1), -4.0, 0.0)
    relative = jnp.bitwise_and(nbr_ref[...] - (col - 1) * elements, total - 1)
    for k in range(4):
        near = near + jnp.where(relative[k : k + 1, :] == place, 1.0, 0.0)
    near_t = near.astype(BF16)

    cs = cs_ref[...]
    lane = jnp.bitwise_and(iota((rows, width), 1), levels_h - 1)
    upper = jnp.where(lane == levels_h - 1, cs, pltpu.roll(cs, width - 1, axis=1))
    lower = jnp.where(lane == 0, cs, pltpu.roll(cs, 1, axis=1))
    base = cs + VMIX * (upper + lower - 2.0 * cs)
    rate = rate_ref[...]

    square[...] = jnp.zeros_like(square)
    square[0:levels_c, 0:levels_h] = map_ref[...]
    square[levels_h : levels_h + levels_c, levels_h : 2 * levels_h] = map_ref[...]

    @pl.when(is_cloud)
    def _():
        chosen = iota((slots, rows), 0) + (sec - 1) * slots == slot.astype(I32)
        chosen32 = jnp.where(chosen, 1.0, 0.0)
        chosen16 = chosen32.astype(BF16)
        counts_out = jnp.sum(chosen32 * cnt_ref[...].astype(F32), axis=1, keepdims=True)
        repeat = jnp.where(
            iota((elements, rows), 0) == lax.shift_right_logical(iota((elements, rows), 1), 2), 1.0, 0.0
        ).astype(BF16)
        by_element = dot(chosen16, repeat, NT).astype(BF16)
        reach = dot(by_element, near_t, NT).astype(BF16)
        known = pick(chosen16, base) + rate * pick(reach[:, 2 * elements :], own)
        reach = reach[:, :elements]

        push_arrives()
        sent = known + rate * pick(reach, given[0:elements])
        slot_left = jnp.concatenate([given[elements + 4 : elements + 5], given[elements + 5 : elements + 6]], axis=1)
        chosen_left = jnp.where(
            iota((slots, rows), 0) + (sec - 1) * slots == slot_left.astype(I32), 1.0, 0.0
        ).astype(BF16)
        nbr_left = given[elements : elements + 4, 0:elements].astype(I32)
        here = iota((elements, elements), 0) + col * elements
        near_left = jnp.zeros((elements, elements), F32)
        for k in range(4):
            near_left = near_left + jnp.where(nbr_left[k : k + 1, :] == here, 1.0, 0.0)
        reach_left = dot(dot(chosen_left, repeat, NT).astype(BF16), near_left.astype(BF16), NT)
        extra = rate * pick(reach_left.astype(BF16), own)
        both = dot3(jnp.concatenate([sent, extra], axis=0), square[...], NT)
        target = jnp.where(iota((slots, width), 1) == levels_c, counts_out, both[:slots])
        disp_send[:, :, 0:width] = target.reshape(n_col, cap, width)
        disp_send[:, :, width:] = both[slots:].reshape(n_col, cap, width)

        pl.semaphore_wait(barrier, n_col + 1)
        def send(other):
            pltpu.make_async_remote_copy(
                src_ref=disp_send.at[other], dst_ref=disp_recv.at[col],
                send_sem=disp_send_sem, recv_sem=disp_recv_sem,
                device_id=(sec, other), device_id_type=MESH,
            ).start()

        for_others(col, send)
        pltpu.make_async_copy(disp_send.at[col], disp_recv.at[col], disp_recv_sem).start()
        to_left.start()

        fetches[7].wait()
        for f in range(2):
            parts[f, 8 * levels_c :] = jnp.zeros((8 * (levels_h - levels_c), slots), F32)

        def widen(z, carry):
            water = block[0, 1, z].astype(F32)
            for f, x in ((1, water), (0, block[0, 0, z].astype(F32) + LATENT * water)):
                plain[f][z] = x
                parts[f, pl.ds(8 * z, 8), :] = (x[0:8] + x[8:16]) + (x[16:24] + x[24:32])
            return carry

        lax.fori_loop(0, levels_c, widen, 0, unroll=UNROLL)

        def over_columns(f):
            return sum(parts[f, pl.ds(k, levels_h, stride=8), :] for k in range(8))

        def strided(ref, z):
            return tuple(ref[z, pl.ds(k, 8, stride=4), :] for k in range(4))

        def packed(ref, z):
            return tuple(ref[z, pl.ds(8 * k, 8), :] for k in range(4))

        def put_strided(ref, z, tiles):
            for k in range(4):
                ref[z, pl.ds(k, 8, stride=4), :] = tiles[k]

        def put_packed(ref, z, tiles):
            for k in range(4):
                ref[z, pl.ds(8 * k, 8), :] = tiles[k]

        def stencil(here, below, above, by_x, by_z):
            west = (pltpu.roll(here[3], 1, axis=0),) + here[:3]
            east = here[1:] + (pltpu.roll(here[0], 7, axis=0),)
            return tuple(
                here[k] + (by_x * (east[k] + west[k]) + by_z * (above[k] + below[k]))
                for k in range(4)
            )

        for f in range(2):

            def first(z, carry, f=f):
                below, here = carry
                above = strided(plain[f], jnp.minimum(z + 1, levels_c - 1))
                put_packed(
                    (energy_a, water_a)[f], z, stencil(here, below, above, HORIZ / CENTRE, VERTIC / CENTRE)
                )
                return here, above

            edge = strided(plain[f], 0)
            lax.fori_loop(0, levels_c, first, (edge, edge), unroll=UNROLL)

        columns_inv = 1.0 / across
        start = [over_columns(f) * columns_inv for f in range(2)]
        level = iota((levels_h, slots), 0)
        wet = jnp.concatenate([sat_ref[...], jnp.zeros((1, 128 - levels_c), F32)], axis=1)
        wet = jnp.transpose(jnp.broadcast_to(wet, (128, 128)))[:levels_h]

        def smoothed(x):
            up = jnp.where(level == levels_c - 1, x, pltpu.roll(x, levels_h - 1, axis=0))
            low = jnp.where(level == 0, x, pltpu.roll(x, 1, axis=0))
            return (1.0 - 2.0 * VERTIC) * x + VERTIC * (up + low)

        pltpu.make_async_copy(disp_recv, disp_recv, disp_recv_sem).wait()
        later = disp_recv[:, :, width:].reshape(slots, width)
        arrived = jnp.transpose(
            disp_recv[:, :, 0:width].reshape(slots, width) + pltpu.roll(later, slots - cap, axis=0)
        )
        counts = arrived[levels_c : levels_c + 1, :]
        counts8 = jnp.broadcast_to(counts, (8, slots))
        goal = [arrived[f * levels_h : (f + 1) * levels_h] for f in range(2)]
        goal[0] = goal[0] + LATENT * goal[1]
        mean = list(start)
        offset = [jnp.zeros((levels_h, slots), F32)] * 2

        for n in range(MAX_SUB):
            scale = CENTRE ** (n + 1)
            keep = counts > float(n)
            d = [RELAX * (goal[f] - mean[f]) for f in range(2)]
            moved = smoothed(mean[0] + d[0])
            shifted = [smoothed(offset[f] + d[f]) for f in range(2)]
            limit = (0.5 / scale) * (wet - shifted[1])
            limits[...] = limit if n == 0 else jnp.where(keep, limit, 0.0)

            def condense(water, z, by_half):
                bound = jnp.broadcast_to(limits[pl.ds(z, 1), :], (8, slots))
                new = [jnp.minimum(water[k], by_half * water[k] + bound) for k in range(4)]
                parts[1, pl.ds(8 * z, 8), :] = (new[0] + new[1]) + (new[2] + new[3])
                return new

            if n == 0:

                def finish(z, carry):
                    put_packed(water_b, z, condense(packed(water_a, z), z, 0.5))
                    return carry

                lax.fori_loop(0, levels_c, finish, 0, unroll=UNROLL)
            else:
                going = jnp.where(counts8 > float(n), 1.0, 0.0)
                by_x, by_z, by_half = going * (HORIZ / CENTRE), going * (VERTIC / CENTRE), 1.0 - going * 0.5
                old, fresh = (water_b, water_a) if n % 2 else (water_a, water_b)

                def sweep(z, carry, n=n, old=old, fresh=fresh, by_x=by_x, by_z=by_z, by_half=by_half):
                    below, here = carry
                    above = packed(old, jnp.minimum(z + 1, levels_c - 1))
                    new = condense(stencil(here, below, above, by_x, by_z), z, by_half)
                    if n == MAX_SUB - 1:
                        put_strided(plain_water, z, new)
                    else:
                        put_packed(fresh, z, new)
                    return here, above

                edge = packed(old, 0)
                lax.fori_loop(0, levels_c, sweep, (edge, edge), unroll=UNROLL)

            dried = over_columns(1) * (columns_inv * scale) + shifted[1]
            mean[0] = jnp.where(keep, moved, mean[0])
            mean[1] = jnp.where(keep, dried, mean[1])
            offset = [jnp.where(keep, shifted[f], offset[f]) for f in range(2)]

        gain = [jnp.where(level < levels_c, mean[f] - start[f], 0.0) for f in range(2)]
        change = jnp.concatenate([gain[0] - LATENT * gain[1], gain[1]], axis=0)
        tendency = dot3(jnp.transpose(change), square[...])
        tend_send[...] = tendency.reshape(n_col, cap, width)

        def give_both(other):
            for chip in range(2):
                give(other, chip).start()

        for_others(col, give_both)
        for chip in range(2):

            @pl.when(sec != 2 * chip + 1)
            def _():
                give(col, chip).start()

        @pl.when(core == 1)
        def _():
            pltpu.make_async_copy(tend_send.at[col], tends.at[sec - 1, col], tend_recv_sem.at[sec - 1]).start()

        for n in range(1, MAX_SUB):
            going = jnp.where(counts8 > float(n), 1.0, 0.0)
            by_x, by_z = going * (HORIZ / CENTRE), going * (VERTIC / CENTRE)

            old, fresh = (energy_a, energy_b) if n % 2 else (energy_b, energy_a)

            def follow(z, carry, n=n, old=old, fresh=fresh, by_x=by_x, by_z=by_z):
                below, here = carry
                above = packed(old, jnp.minimum(z + 1, levels_c - 1))
                new = stencil(here, below, above, by_x, by_z)
                if n == MAX_SUB - 1:
                    put_strided(plain_energy, z, new)
                else:
                    put_packed(fresh, z, new)
                return here, above

            edge = packed(old, 0)
            lax.fori_loop(0, levels_c, follow, (edge, edge), unroll=UNROLL)

        power = jnp.full((1, slots), CENTRE, F32)
        for n in range(1, MAX_SUB):
            power = jnp.where(counts > float(n), CENTRE ** (n + 1), power)
        used = jnp.broadcast_to(counts, (across, slots)) > 0.0
        power = jnp.broadcast_to(power, (across, slots))
        for f in range(2):
            offsets[f] = offset[f]

        def narrow(z, carry):
            x = [
                power * plain[f][z] + jnp.broadcast_to(offsets[f, pl.ds(z, 1), :], power.shape)
                for f in range(2)
            ]
            x[0] = x[0] - LATENT * x[1]
            for f in range(2):
                block[0, f, z] = jnp.where(used, x[f], block[0, f, z].astype(F32)).astype(BF16)
            return carry

        lax.fori_loop(0, levels_c, narrow, 0, unroll=UNROLL)

    @pl.when(jnp.logical_not(is_cloud))
    def _():
        push_arrives()
        to_left.start()
        fetches[7].wait()

    near_e = jnp.transpose(
        jnp.concatenate([near, jnp.zeros((3 * elements, 128 - elements), F32)], axis=1)
    )[:elements].astype(BF16)
    to_left.wait_recv()
    around = jnp.concatenate([given[0:elements], beyond[...], own], axis=0)
    spread = rate * pick(near_e, around)
    adv_ref[...] = base
    for k in range(4):
        adv_ref[pl.ds(k, elements, stride=4), :] += spread
    slot_column = jnp.transpose(jnp.broadcast_to(slot, (128, rows)))[:, 0:1]
    member = jnp.where(
        slot_column == iota((rows, (n_sec - 1) * slots), 1).astype(F32), 1.0, 0.0
    ).astype(BF16)

    def heard(source):
        pltpu.make_async_copy(tends.at[source], tends.at[source], tend_recv_sem.at[source]).wait()

    def passing(source):
        return pltpu.make_async_remote_copy(
            src_ref=tends.at[source], dst_ref=tends.at[source],
            send_sem=core_send_sem.at[source], recv_sem=core_recv_sem.at[source],
            device_id=(sibling, col), device_id_type=MESH,
        )

    @pl.when(core == 1)
    def _():
        for source in range(n_sec - 1):
            heard(source)
            passing(source).start()

    @pl.when(core == 0)
    def _():
        for source in range(n_sec - 1):
            passing(source).wait_recv()

    gathered = tends[...].reshape((n_sec - 1) * slots, width)
    summed = adv_ref[...] + pick(member, gathered)
    out_ref[...] = jnp.where(
        iota((rows, width), 1) >= levels_h, jnp.maximum(summed, 0.0), summed
    )

    @pl.when(jnp.logical_not(is_cloud))
    def _():
        for section in (2, 1):
            push(section).wait_send()

    @pl.when(relays)
    def _():
        relay.wait_send()

    to_left.wait_send()

    @pl.when(core == 1)
    def _():
        for source in range(n_sec - 1):
            passing(source).wait_send()

    @pl.when(is_cloud)
    def _():
        others = pl.ds(0, n_col - 1)
        pltpu.make_async_copy(disp_send.at[others], disp_send.at[others], disp_send_sem).wait()
        for chip in range(2):
            pltpu.make_async_copy(tend_send.at[others], tend_send.at[others], tend_send_sem.at[chip]).wait()

            @pl.when(sec != 2 * chip + 1)
            def _():
                give(col, chip).wait_send()


def body(
    column_state, mixing_rate, neighbours, assignment, substeps, cloud_state, level_map, saturation
):
    n_sec, n_col = lax.axis_size("sec"), lax.axis_size("col")
    rows, width = column_state.shape
    elements = rows // 4
    _, fields, levels_c, across, slots = cloud_state.shape
    cap, levels_h = slots // n_col, level_map.shape[1]
    vmem = pl.BlockSpec(memory_space=pltpu.VMEM)
    hbm = pl.BlockSpec(memory_space=pltpu.HBM)
    message = (n_col, cap, width)
    dma = pltpu.SemaphoreType.DMA
    results = (
        jax.ShapeDtypeStruct(column_state.shape, F32),
        jax.ShapeDtypeStruct(cloud_state.shape, BF16),
    )
    operands = (
        column_state,
        mixing_rate.reshape(1, width),
        neighbours.T,
        assignment.reshape(1, rows),
        substeps.reshape(1, rows),
        cloud_state,
        level_map,
        saturation.reshape(1, levels_c),
    )
    return pl.pallas_call(
        functools.partial(kernel, (n_sec, n_col)),
        out_shape=tuple(pltpu.VMEM(r.shape, r.dtype) for r in results),
        in_specs=[hbm] * 8,
        out_specs=(vmem, vmem),
        scratch_shapes=[
            pltpu.VMEM((rows, width), F32),
            pltpu.VMEM((1, width), F32),
            pltpu.VMEM((4, elements), I32),
            pltpu.VMEM((1, rows), I32),
            pltpu.VMEM((1, rows), I32),
            pltpu.VMEM((levels_c, levels_h), F32),
            pltpu.VMEM((1, levels_c), F32),
            *[pltpu.VMEM((levels_c, across, slots), F32)] * 6,
            pltpu.VMEM((fields, 8 * levels_h, slots), F32),
            pltpu.VMEM((levels_h, slots), F32),
            pltpu.VMEM((fields, levels_h, slots), F32),
            pltpu.VMEM((fields * levels_h, fields * levels_h), F32),
            pltpu.VMEM((elements + 8, width), F32),
            pltpu.VMEM((elements + 8, width), F32),
            pltpu.VMEM((elements, width), F32),
            pltpu.VMEM((n_col, cap, 2 * width), F32),
            pltpu.VMEM((n_col, cap, 2 * width), F32),
            pltpu.VMEM(message, F32),
            pltpu.VMEM((n_sec - 1,) + message, F32),
            pltpu.VMEM((rows, width), F32),
            dma((8,)),
            dma((2,)),
            dma,
            dma,
            dma((2,)),
            dma,
            dma,
            dma((2,)),
            dma((n_sec - 1,)),
            dma((n_sec - 1,)),
            dma((n_sec - 1,)),
        ],
        compiler_params=pltpu.CompilerParams(
            collective_id=0, has_side_effects=True, vmem_limit_bytes=48 * 1024 * 1024
        ),
    )(*(pltpu.with_memory_space_constraint(x, pltpu.HBM) for x in operands))


def solution(mesh):
    in_specs = (
        P("col", None),
        P(),
        P("col", None),
        P("col", None),
        P("col"),
        P("sec", None, None, None, "col"),
        P(),
        P(),
    )
    out_specs = (P("col", None), P("sec", None, None, None, "col"))
    return jax.shard_map(body, mesh=mesh, in_specs=in_specs, out_specs=out_specs, check_vma=False)
```

```python
import functools

import jax
import jax.numpy as jnp
from jax import lax
from jax.experimental import pallas as pl
from jax.experimental.pallas import tpu as pltpu
from jax.sharding import PartitionSpec as P

MAX_SUB = 4
RELAX = 0.25
HORIZ = 0.12
VERTIC = 0.1
LATENT = 2.5
VMIX = 0.2
UNROLL = 29
CENTRE = 1.0 - 2.0 * HORIZ - 2.0 * VERTIC
MESH = pl.DeviceIdType.MESH
F32 = jnp.float32
BF16 = jnp.bfloat16
I32 = jnp.int32
NN = (((1,), (0,)), ((), ()))
NT = (((1,), (1,)), ((), ()))
ACROSS = ((2, 1), (1, 1), (3, 1), (2, 0), (0, 1), (1, 0), (3, 0), (0, 0))


def iota(shape, dim):
    return lax.broadcasted_iota(I32, shape, dim)


def halves(x):
    hi = x.astype(BF16)
    return hi, (x - hi.astype(F32)).astype(BF16)


def dot(a, b, dims=NN):
    return lax.dot_general(a, b, dims, preferred_element_type=F32)


def joined(lefts, rights, dims):
    (left_dims, right_dims), _ = dims
    return dot(
        jnp.concatenate(lefts, axis=left_dims[0]), jnp.concatenate(rights, axis=right_dims[0]), dims
    )


def pick(exact, x, dims=NN):
    hi, lo = halves(x)
    if exact.shape[1] % 128:
        return dot(exact, hi, dims) + dot(exact, lo, dims)
    return joined([exact, exact], [hi, lo], dims)


def dot3(x, y, dims=NN):
    xh, xl = halves(x)
    yh, yl = halves(y)
    return joined([xh, xh, xl], [yh, yl, yh], dims)


def for_others(col, visit):
    y, x, z = col // 16, lax.rem(col // 8, 2), lax.rem(col, 8)
    bases = [lax.rem(y + dy, 4) * 16 + lax.rem(x + dx, 2) * 8 for dy, dx in ACROSS]

    def ring(t, carry):
        half = (t + 1) // 2
        dz = 4 + half - 2 * half * lax.rem(t, 2)
        along = lax.rem(z + dz, 8)
        for base in bases:
            visit(base + along)
        return carry

    lax.fori_loop(0, 7, ring, 0)
    for base in bases[:-1]:
        visit(base + z)


def kernel(
    sizes,
    cs_hbm,
    rate_hbm,
    nbr_hbm,
    asg_hbm,
    cnt_hbm,
    cloud_hbm,
    map_hbm,
    sat_hbm,
    out_ref,
    block,
    cs_ref,
    rate_ref,
    nbr_ref,
    asg_ref,
    cnt_ref,
    map_ref,
    sat_ref,
    plain_energy,
    plain_water,
    energy_a,
    energy_b,
    water_a,
    water_b,
    parts,
    limits,
    offsets,
    square,
    pushed,
    given,
    beyond,
    disp_send,
    disp_recv,
    tend_send,
    tends,
    adv_ref,
    local_sem,
    push_send_sem,
    push_recv_sem,
    relay_sem,
    beyond_sem,
    disp_send_sem,
    disp_recv_sem,
    tend_send_sem,
    tend_recv_sem,
    core_send_sem,
    core_recv_sem,
):
    n_sec, n_col = sizes
    sec, col = lax.axis_index("sec"), lax.axis_index("col")
    rows, width = cs_ref.shape
    elements = rows // 4
    total = elements * n_col
    cap, slots = disp_send.shape[1], n_col * disp_send.shape[1]
    levels_c, levels_h = map_ref.shape
    left, right = lax.rem(col + n_col - 1, n_col), lax.rem(col + 1, n_col)
    is_cloud = sec > 0
    plain = (plain_energy, plain_water)
    across = plain_water.shape[1]
    core = lax.rem(sec, 2)
    sibling = sec + 1 - 2 * core
    facing = lax.rem(sec + 2, n_sec)

    fetches = [
        pltpu.make_async_copy(src, dst, local_sem.at[i])
        for i, (src, dst) in enumerate(
            (
                (asg_hbm, asg_ref),
                (nbr_hbm, nbr_ref),
                (cs_hbm, cs_ref),
                (rate_hbm, rate_ref),
                (map_hbm, map_ref),
                (cnt_hbm, cnt_ref),
                (sat_hbm, sat_ref),
                (cloud_hbm, block),
            )
        )
    ]
    for fetch in fetches:
        fetch.start()

    barrier = pltpu.get_barrier_semaphore()

    def greet(device):
        pl.semaphore_signal(barrier, inc=1, device_id=device, device_id_type=MESH)

    greet((0, left))

    @pl.when(is_cloud)
    def _():
        for_others(col, lambda other: greet((sec, other)))

    greet((sibling, col))

    @pl.when(core == 1)
    def _():
        greet((facing, col))

    @pl.when(sec == 1)
    def _():
        greet((2, col))

    fetches[0].wait()
    fetches[1].wait()

    asg = asg_ref[...]
    asg_column = jnp.transpose(jnp.broadcast_to(asg.astype(F32), (128, rows)))[:, 0:1]
    same = (asg_column == asg.astype(F32)) & (iota((rows, rows), 0) < iota((rows, rows), 1))
    rank = jnp.max(jnp.where(same, 1.0, 0.0), axis=0, keepdims=True)
    slot = (asg * cap).astype(F32) + rank

    pushed[elements : elements + 4, 0:elements] = nbr_ref[...].astype(F32)
    pushed[elements + 4 : elements + 5] = slot[:, :width]
    pushed[elements + 5 : elements + 6] = slot[:, width:]

    fetches[2].wait()
    own = (
        cs_ref[pl.ds(0, elements, stride=4), :]
        + cs_ref[pl.ds(1, elements, stride=4), :]
        + cs_ref[pl.ds(2, elements, stride=4), :]
        + cs_ref[pl.ds(3, elements, stride=4), :]
    ) * 0.25
    pushed[0:elements] = own

    def push(section):
        return pltpu.make_async_remote_copy(
            src_ref=pushed, dst_ref=given,
            send_sem=push_send_sem.at[section - 1], recv_sem=push_recv_sem,
            device_id=(section, right), device_id_type=MESH,
        )

    relays = (sec == 1) | (sec == 2)
    relay = pltpu.make_async_remote_copy(
        src_ref=given, dst_ref=given, send_sem=relay_sem, recv_sem=push_recv_sem,
        device_id=(sibling, col), device_id_type=MESH,
    )

    def push_arrives():
        relay.wait_recv()

        @pl.when(relays)
        def _():
            relay.start()

    means = pushed.at[pl.ds(0, elements)]
    to_left = pltpu.make_async_remote_copy(
        src_ref=means, dst_ref=beyond, send_sem=beyond_sem.at[0], recv_sem=beyond_sem.at[1],
        device_id=(sec, left), device_id_type=MESH,
    )

    @pl.when(jnp.logical_not(is_cloud))
    def _():
        pl.semaphore_wait(barrier, n_sec + 1)
        for section in (2, 1):
            push(section).start()

    def give(other, chip):
        return pltpu.make_async_remote_copy(
            src_ref=tend_send.at[other], dst_ref=tends.at[sec - 1, col],
            send_sem=tend_send_sem.at[chip], recv_sem=tend_recv_sem.at[sec - 1],
            device_id=(2 * chip + 1, other), device_id_type=MESH,
        )

    for fetch in fetches[3:7]:
        fetch.wait()

    place = iota((3 * elements, elements), 0)
    place = jnp.where(
        place < elements, place, jnp.where(place < 2 * elements, place + elements, place - elements)
    )
    near = jnp.where(place == elements + iota((3 * elements, elements), 1), -4.0, 0.0)
    relative = jnp.bitwise_and(nbr_ref[...] - (col - 1) * elements, total - 1)
    for k in range(4):
        near = near + jnp.where(relative[k : k + 1, :] == place, 1.0, 0.0)
    near_t = near.astype(BF16)

    cs = cs_ref[...]
    lane = jnp.bitwise_and(iota((rows, width), 1), levels_h - 1)
    upper = jnp.where(lane == levels_h - 1, cs, pltpu.roll(cs, width - 1, axis=1))
    lower = jnp.where(lane == 0, cs, pltpu.roll(cs, 1, axis=1))
    base = cs + VMIX * (upper + lower - 2.0 * cs)
    rate = rate_ref[...]

    square[...] = jnp.zeros_like(square)
    square[0:levels_c, 0:levels_h] = map_ref[...]
    square[levels_h : levels_h + levels_c, levels_h : 2 * levels_h] = map_ref[...]

    @pl.when(is_cloud)
    def _():
        chosen = iota((slots, rows), 0) + (sec - 1) * slots == slot.astype(I32)
        chosen32 = jnp.where(chosen, 1.0, 0.0)
        chosen16 = chosen32.astype(BF16)
        counts_out = jnp.sum(chosen32 * cnt_ref[...].astype(F32), axis=1, keepdims=True)
        repeat = jnp.where(
            iota((elements, rows), 0) == lax.shift_right_logical(iota((elements, rows), 1), 2), 1.0, 0.0
        ).astype(BF16)
        by_element = dot(chosen16, repeat, NT).astype(BF16)
        reach = dot(by_element, near_t, NT).astype(BF16)
        known = pick(chosen16, base) + rate * pick(reach[:, 2 * elements :], own)
        reach = reach[:, :elements]

        push_arrives()
        sent = known + rate * pick(reach, given[0:elements])
        slot_left = jnp.concatenate([given[elements + 4 : elements + 5], given[elements + 5 : elements + 6]], axis=1)
        chosen_left = jnp.where(
            iota((slots, rows), 0) + (sec - 1) * slots == slot_left.astype(I32), 1.0, 0.0
        ).astype(BF16)
        nbr_left = given[elements : elements + 4, 0:elements].astype(I32)
        here = iota((elements, elements), 0) + col * elements
        near_left = jnp.zeros((elements, elements), F32)
        for k in range(4):
            near_left = near_left + jnp.where(nbr_left[k : k + 1, :] == here, 1.0, 0.0)
        reach_left = dot(dot(chosen_left, repeat, NT).astype(BF16), near_left.astype(BF16), NT)
        extra = rate * pick(reach_left.astype(BF16), own)
        both = dot3(jnp.concatenate([sent, extra], axis=0), square[...], NT)
        target = jnp.where(iota((slots, width), 1) == levels_c, counts_out, both[:slots])
        disp_send[:, :, 0:width] = target.reshape(n_col, cap, width)
        disp_send[:, :, width:] = both[slots:].reshape(n_col, cap, width)

        pl.semaphore_wait(barrier, n_col + 1)
        def send(other):
            pltpu.make_async_remote_copy(
                src_ref=disp_send.at[other], dst_ref=disp_recv.at[col],
                send_sem=disp_send_sem, recv_sem=disp_recv_sem,
                device_id=(sec, other), device_id_type=MESH,
            ).start()

        for_others(col, send)
        pltpu.make_async_copy(disp_send.at[col], disp_recv.at[col], disp_recv_sem).start()
        to_left.start()

        fetches[7].wait()
        for f in range(2):
            parts[f, 8 * levels_c :] = jnp.zeros((8 * (levels_h - levels_c), slots), F32)

        def widen(z, carry):
            water = block[0, 1, z].astype(F32)
            for f, x in ((1, water), (0, block[0, 0, z].astype(F32) + LATENT * water)):
                plain[f][z] = x
                parts[f, pl.ds(8 * z, 8), :] = (x[0:8] + x[8:16]) + (x[16:24] + x[24:32])
            return carry

        lax.fori_loop(0, levels_c, widen, 0, unroll=UNROLL)

        def over_columns(f):
            return sum(parts[f, pl.ds(k, levels_h, stride=8), :] for k in range(8))

        def strided(ref, z):
            return tuple(ref[z, pl.ds(k, 8, stride=4), :] for k in range(4))

        def packed(ref, z):
            return tuple(ref[z, pl.ds(8 * k, 8), :] for k in range(4))

        def put_strided(ref, z, tiles):
            for k in range(4):
                ref[z, pl.ds(k, 8, stride=4), :] = tiles[k]

        def put_packed(ref, z, tiles):
            for k in range(4):
                ref[z, pl.ds(8 * k, 8), :] = tiles[k]

        def stencil(here, below, above, by_x, by_z):
            west = (pltpu.roll(here[3], 1, axis=0),) + here[:3]
            east = here[1:] + (pltpu.roll(here[0], 7, axis=0),)
            return tuple(
                here[k] + (by_x * (east[k] + west[k]) + by_z * (above[k] + below[k]))
                for k in range(4)
            )

        for f in range(2):

            def first(z, carry, f=f):
                below, here = carry
                above = strided(plain[f], jnp.minimum(z + 1, levels_c - 1))
                put_packed(
                    (energy_a, water_a)[f], z, stencil(here, below, above, HORIZ / CENTRE, VERTIC / CENTRE)
                )
                return here, above

            edge = strided(plain[f], 0)
            lax.fori_loop(0, levels_c, first, (edge, edge), unroll=UNROLL)

        columns_inv = 1.0 / across
        start = [over_columns(f) * columns_inv for f in range(2)]
        level = iota((levels_h, slots), 0)
        wet = jnp.concatenate([sat_ref[...], jnp.zeros((1, 128 - levels_c), F32)], axis=1)
        wet = jnp.transpose(jnp.broadcast_to(wet, (128, 128)))[:levels_h]

        def smoothed(x):
            up = jnp.where(level == levels_c - 1, x, pltpu.roll(x, levels_h - 1, axis=0))
            low = jnp.where(level == 0, x, pltpu.roll(x, 1, axis=0))
            return (1.0 - 2.0 * VERTIC) * x + VERTIC * (up + low)

        pltpu.make_async_copy(disp_recv, disp_recv, disp_recv_sem).wait()
        later = disp_recv[:, :, width:].reshape(slots, width)
        arrived = jnp.transpose(
            disp_recv[:, :, 0:width].reshape(slots, width) + pltpu.roll(later, slots - cap, axis=0)
        )
        counts = arrived[levels_c : levels_c + 1, :]
        counts8 = jnp.broadcast_to(counts, (8, slots))
        goal = [arrived[f * levels_h : (f + 1) * levels_h] for f in range(2)]
        goal[0] = goal[0] + LATENT * goal[1]
        mean = list(start)
        offset = [jnp.zeros((levels_h, slots), F32)] * 2

        for n in range(MAX_SUB):
            scale = CENTRE ** (n + 1)
            keep = counts > float(n)
            d = [RELAX * (goal[f] - mean[f]) for f in range(2)]
            moved = smoothed(mean[0] + d[0])
            shifted = [smoothed(offset[f] + d[f]) for f in range(2)]
            limit = (0.5 / scale) * (wet - shifted[1])
            limits[...] = limit if n == 0 else jnp.where(keep, limit, 0.0)

            def condense(water, z, by_half):
                bound = jnp.broadcast_to(limits[pl.ds(z, 1), :], (8, slots))
                new = [jnp.minimum(water[k], by_half * water[k] + bound) for k in range(4)]
                parts[1, pl.ds(8 * z, 8), :] = (new[0] + new[1]) + (new[2] + new[3])
                return new

            if n == 0:

                def finish(z, carry):
                    put_packed(water_b, z, condense(packed(water_a, z), z, 0.5))
                    return carry

                lax.fori_loop(0, levels_c, finish, 0, unroll=UNROLL)
            else:
                going = jnp.where(counts8 > float(n), 1.0, 0.0)
                by_x, by_z, by_half = going * (HORIZ / CENTRE), going * (VERTIC / CENTRE), 1.0 - going * 0.5
                old, fresh = (water_b, water_a) if n % 2 else (water_a, water_b)

                def sweep(z, carry, n=n, old=old, fresh=fresh, by_x=by_x, by_z=by_z, by_half=by_half):
                    below, here = carry
                    above = packed(old, jnp.minimum(z + 1, levels_c - 1))
                    new = condense(stencil(here, below, above, by_x, by_z), z, by_half)
                    if n == MAX_SUB - 1:
                        put_strided(plain_water, z, new)
                    else:
                        put_packed(fresh, z, new)
                    return here, above

                edge = packed(old, 0)
                lax.fori_loop(0, levels_c, sweep, (edge, edge), unroll=UNROLL)

            dried = over_columns(1) * (columns_inv * scale) + shifted[1]
            mean[0] = jnp.where(keep, moved, mean[0])
            mean[1] = jnp.where(keep, dried, mean[1])
            offset = [jnp.where(keep, shifted[f], offset[f]) for f in range(2)]

        gain = [jnp.where(level < levels_c, mean[f] - start[f], 0.0) for f in range(2)]
        change = jnp.concatenate([gain[0] - LATENT * gain[1], gain[1]], axis=0)
        tendency = dot3(jnp.transpose(change), square[...])
        tend_send[...] = tendency.reshape(n_col, cap, width)

        def give_both(other):
            for chip in range(2):
                give(other, chip).start()

        for_others(col, give_both)
        for chip in range(2):

            @pl.when(sec != 2 * chip + 1)
            def _():
                give(col, chip).start()

        @pl.when(core == 1)
        def _():
            pltpu.make_async_copy(tend_send.at[col], tends.at[sec - 1, col], tend_recv_sem.at[sec - 1]).start()

        for n in range(1, MAX_SUB):
            going = jnp.where(counts8 > float(n), 1.0, 0.0)
            by_x, by_z = going * (HORIZ / CENTRE), going * (VERTIC / CENTRE)

            old, fresh = (energy_a, energy_b) if n % 2 else (energy_b, energy_a)

            def follow(z, carry, n=n, old=old, fresh=fresh, by_x=by_x, by_z=by_z):
                below, here = carry
                above = packed(old, jnp.minimum(z + 1, levels_c - 1))
                new = stencil(here, below, above, by_x, by_z)
                if n == MAX_SUB - 1:
                    put_strided(plain_energy, z, new)
                else:
                    put_packed(fresh, z, new)
                return here, above

            edge = packed(old, 0)
            lax.fori_loop(0, levels_c, follow, (edge, edge), unroll=UNROLL)

        power = jnp.full((1, slots), CENTRE, F32)
        for n in range(1, MAX_SUB):
            power = jnp.where(counts > float(n), CENTRE ** (n + 1), power)
        used = jnp.broadcast_to(counts, (across, slots)) > 0.0
        power = jnp.broadcast_to(power, (across, slots))
        for f in range(2):
            offsets[f] = offset[f]

        def narrow(z, carry):
            x = [
                power * plain[f][z] + jnp.broadcast_to(offsets[f, pl.ds(z, 1), :], power.shape)
                for f in range(2)
            ]
            x[0] = x[0] - LATENT * x[1]
            for f in range(2):
                block[0, f, z] = jnp.where(used, x[f], block[0, f, z].astype(F32)).astype(BF16)
            return carry

        lax.fori_loop(0, levels_c, narrow, 0, unroll=UNROLL)

    @pl.when(jnp.logical_not(is_cloud))
    def _():
        push_arrives()
        to_left.start()
        fetches[7].wait()

    near_e = jnp.transpose(
        jnp.concatenate([near, jnp.zeros((3 * elements, 128 - elements), F32)], axis=1)
    )[:elements].astype(BF16)
    to_left.wait_recv()
    around = jnp.concatenate([given[0:elements], beyond[...], own], axis=0)
    spread = rate * pick(near_e, around)
    adv_ref[...] = base
    for k in range(4):
        adv_ref[pl.ds(k, elements, stride=4), :] += spread
    slot_column = jnp.transpose(jnp.broadcast_to(slot, (128, rows)))[:, 0:1]
    member = jnp.where(
        slot_column == iota((rows, (n_sec - 1) * slots), 1).astype(F32), 1.0, 0.0
    ).astype(BF16)

    def heard(source):
        pltpu.make_async_copy(tends.at[source], tends.at[source], tend_recv_sem.at[source]).wait()

    def passing(source):
        return pltpu.make_async_remote_copy(
            src_ref=tends.at[source], dst_ref=tends.at[source],
            send_sem=core_send_sem.at[source], recv_sem=core_recv_sem.at[source],
            device_id=(sibling, col), device_id_type=MESH,
        )

    @pl.when(core == 1)
    def _():
        for source in range(n_sec - 1):
            heard(source)
            passing(source).start()

    @pl.when(core == 0)
    def _():
        for source in range(n_sec - 1):
            passing(source).wait_recv()

    gathered = tends[...].reshape((n_sec - 1) * slots, width)
    summed = adv_ref[...] + pick(member, gathered)
    out_ref[...] = jnp.where(
        iota((rows, width), 1) >= levels_h, jnp.maximum(summed, 0.0), summed
    )

    @pl.when(jnp.logical_not(is_cloud))
    def _():
        for section in (2, 1):
            push(section).wait_send()

    @pl.when(relays)
    def _():
        relay.wait_send()

    to_left.wait_send()

    @pl.when(core == 1)
    def _():
        for source in range(n_sec - 1):
            passing(source).wait_send()

    @pl.when(is_cloud)
    def _():
        others = pl.ds(0, n_col - 1)
        pltpu.make_async_copy(disp_send.at[others], disp_send.at[others], disp_send_sem).wait()
        for chip in range(2):
            pltpu.make_async_copy(tend_send.at[others], tend_send.at[others], tend_send_sem.at[chip]).wait()

            @pl.when(sec != 2 * chip + 1)
            def _():
                give(col, chip).wait_send()


def write(columns, cloud, columns_out, cloud_out, sem):
    copies = [
        pltpu.make_async_copy(cloud, cloud_out, sem.at[0]),
        pltpu.make_async_copy(columns, columns_out, sem.at[1]),
    ]
    for copy in copies:
        copy.start()
    for copy in copies:
        copy.wait()


def body(
    column_state, mixing_rate, neighbours, assignment, substeps, cloud_state, level_map, saturation
):
    n_sec, n_col = lax.axis_size("sec"), lax.axis_size("col")
    rows, width = column_state.shape
    elements = rows // 4
    _, fields, levels_c, across, slots = cloud_state.shape
    cap, levels_h = slots // n_col, level_map.shape[1]
    vmem = pl.BlockSpec(memory_space=pltpu.VMEM)
    hbm = pl.BlockSpec(memory_space=pltpu.HBM)
    message = (n_col, cap, width)
    dma = pltpu.SemaphoreType.DMA
    results = (
        jax.ShapeDtypeStruct(column_state.shape, F32),
        jax.ShapeDtypeStruct(cloud_state.shape, BF16),
    )
    operands = (
        column_state,
        mixing_rate.reshape(1, width),
        neighbours.T,
        assignment.reshape(1, rows),
        substeps.reshape(1, rows),
        cloud_state,
        level_map,
        saturation.reshape(1, levels_c),
    )
    columns, cloud = pl.pallas_call(
        functools.partial(kernel, (n_sec, n_col)),
        out_shape=tuple(pltpu.VMEM(r.shape, r.dtype) for r in results),
        in_specs=[hbm] * 8,
        out_specs=(vmem, vmem),
        scratch_shapes=[
            pltpu.VMEM((rows, width), F32),
            pltpu.VMEM((1, width), F32),
            pltpu.VMEM((4, elements), I32),
            pltpu.VMEM((1, rows), I32),
            pltpu.VMEM((1, rows), I32),
            pltpu.VMEM((levels_c, levels_h), F32),
            pltpu.VMEM((1, levels_c), F32),
            *[pltpu.VMEM((levels_c, across, slots), F32)] * 6,
            pltpu.VMEM((fields, 8 * levels_h, slots), F32),
            pltpu.VMEM((levels_h, slots), F32),
            pltpu.VMEM((fields, levels_h, slots), F32),
            pltpu.VMEM((fields * levels_h, fields * levels_h), F32),
            pltpu.VMEM((elements + 8, width), F32),
            pltpu.VMEM((elements + 8, width), F32),
            pltpu.VMEM((elements, width), F32),
            pltpu.VMEM((n_col, cap, 2 * width), F32),
            pltpu.VMEM((n_col, cap, 2 * width), F32),
            pltpu.VMEM(message, F32),
            pltpu.VMEM((n_sec - 1,) + message, F32),
            pltpu.VMEM((rows, width), F32),
            dma((8,)),
            dma((2,)),
            dma,
            dma,
            dma((2,)),
            dma,
            dma,
            dma((2,)),
            dma((n_sec - 1,)),
            dma((n_sec - 1,)),
            dma((n_sec - 1,)),
        ],
        compiler_params=pltpu.CompilerParams(
            collective_id=0, has_side_effects=True, vmem_limit_bytes=48 * 1024 * 1024
        ),
    )(*(pltpu.with_memory_space_constraint(x, pltpu.HBM) for x in operands))
    anywhere = pl.BlockSpec(memory_space=pl.ANY)
    return pl.pallas_call(
        write,
        out_shape=results,
        in_specs=[anywhere, anywhere],
        out_specs=(anywhere, anywhere),
        scratch_shapes=[dma((2,))],
        compiler_params=pltpu.CompilerParams(vmem_limit_bytes=1024 * 1024),
    )(columns, cloud)


def solution(mesh):
    in_specs = (
        P("col", None),
        P(),
        P("col", None),
        P("col", None),
        P("col"),
        P("sec", None, None, None, "col"),
        P(),
        P(),
    )
    out_specs = (P("col", None), P("sec", None, None, None, "col"))
    return jax.shard_map(body, mesh=mesh, in_specs=in_specs, out_specs=out_specs, check_vma=False)
```

```python
import functools

import jax
import jax.numpy as jnp
from jax import lax
from jax.experimental import pallas as pl
from jax.experimental.pallas import tpu as pltpu
from jax.sharding import PartitionSpec as P

MAX_SUB = 4
RELAX = 0.25
HORIZ = 0.12
VERTIC = 0.1
LATENT = 2.5
VMIX = 0.2
UNROLL = 29
CENTRE = 1.0 - 2.0 * HORIZ - 2.0 * VERTIC
MESH = pl.DeviceIdType.MESH
F32 = jnp.float32
BF16 = jnp.bfloat16
I32 = jnp.int32
NN = (((1,), (0,)), ((), ()))
NT = (((1,), (1,)), ((), ()))
ACROSS = ((2, 1), (1, 1), (3, 1), (2, 0), (0, 1), (1, 0), (3, 0), (0, 0))


def iota(shape, dim):
    return lax.broadcasted_iota(I32, shape, dim)


def halves(x):
    hi = x.astype(BF16)
    return hi, (x - hi.astype(F32)).astype(BF16)


def dot(a, b, dims=NN):
    return lax.dot_general(a, b, dims, preferred_element_type=F32)


def joined(lefts, rights, dims):
    (left_dims, right_dims), _ = dims
    return dot(
        jnp.concatenate(lefts, axis=left_dims[0]), jnp.concatenate(rights, axis=right_dims[0]), dims
    )


def pick(exact, x, dims=NN):
    hi, lo = halves(x)
    if exact.shape[1] % 128:
        return dot(exact, hi, dims) + dot(exact, lo, dims)
    return joined([exact, exact], [hi, lo], dims)


def dot3(x, y, dims=NN):
    xh, xl = halves(x)
    yh, yl = halves(y)
    return joined([xh, xh, xl], [yh, yl, yh], dims)


def for_others(col, visit):
    y, x, z = col // 16, lax.rem(col // 8, 2), lax.rem(col, 8)
    bases = [lax.rem(y + dy, 4) * 16 + lax.rem(x + dx, 2) * 8 for dy, dx in ACROSS]

    def ring(t, carry):
        half = (t + 1) // 2
        dz = 4 + half - 2 * half * lax.rem(t, 2)
        along = lax.rem(z + dz, 8)
        for base in bases:
            visit(base + along)
        return carry

    lax.fori_loop(0, 7, ring, 0)
    for base in bases[:-1]:
        visit(base + z)


def kernel(
    sizes,
    cs_hbm,
    rate_hbm,
    nbr_hbm,
    asg_hbm,
    cnt_hbm,
    cloud_hbm,
    map_hbm,
    sat_hbm,
    out_ref,
    block,
    cs_ref,
    rate_ref,
    nbr_ref,
    asg_ref,
    cnt_ref,
    map_ref,
    sat_ref,
    plain_energy,
    plain_water,
    energy_a,
    energy_b,
    water_a,
    water_b,
    parts,
    limits,
    offsets,
    square,
    pushed,
    given,
    beyond,
    disp_send,
    disp_recv,
    tend_send,
    tends,
    adv_ref,
    local_sem,
    push_send_sem,
    push_recv_sem,
    relay_sem,
    beyond_sem,
    disp_send_sem,
    disp_recv_sem,
    tend_send_sem,
    tend_recv_sem,
    core_send_sem,
    core_recv_sem,
):
    n_sec, n_col = sizes
    sec, col = lax.axis_index("sec"), lax.axis_index("col")
    rows, width = cs_ref.shape
    elements = rows // 4
    total = elements * n_col
    cap, slots = disp_send.shape[1], n_col * disp_send.shape[1]
    levels_c, levels_h = map_ref.shape
    left, right = lax.rem(col + n_col - 1, n_col), lax.rem(col + 1, n_col)
    is_cloud = sec > 0
    plain = (plain_energy, plain_water)
    across = plain_water.shape[1]
    core = lax.rem(sec, 2)
    sibling = sec + 1 - 2 * core
    facing = lax.rem(sec + 2, n_sec)

    fetches = [
        pltpu.make_async_copy(src, dst, local_sem.at[i])
        for i, (src, dst) in enumerate(
            (
                (asg_hbm, asg_ref),
                (nbr_hbm, nbr_ref),
                (cs_hbm, cs_ref),
                (rate_hbm, rate_ref),
                (map_hbm, map_ref),
                (cnt_hbm, cnt_ref),
                (sat_hbm, sat_ref),
                (cloud_hbm, block),
            )
        )
    ]
    for fetch in fetches:
        fetch.start()

    barrier = pltpu.get_barrier_semaphore()

    def greet(device):
        pl.semaphore_signal(barrier, inc=1, device_id=device, device_id_type=MESH)

    greet((0, left))

    @pl.when(is_cloud)
    def _():
        for_others(col, lambda other: greet((sec, other)))

    greet((sibling, col))

    @pl.when(core == 1)
    def _():
        greet((facing, col))

    @pl.when(sec == 1)
    def _():
        greet((2, col))

    fetches[0].wait()
    fetches[1].wait()

    asg = asg_ref[...]
    asg_column = jnp.transpose(jnp.broadcast_to(asg.astype(F32), (128, rows)))[:, 0:1]
    same = (asg_column == asg.astype(F32)) & (iota((rows, rows), 0) < iota((rows, rows), 1))
    rank = jnp.max(jnp.where(same, 1.0, 0.0), axis=0, keepdims=True)
    slot = (asg * cap).astype(F32) + rank

    pushed[elements : elements + 4, 0:elements] = nbr_ref[...].astype(F32)
    pushed[elements + 4 : elements + 5] = slot[:, :width]
    pushed[elements + 5 : elements + 6] = slot[:, width:]

    fetches[2].wait()
    own = (
        cs_ref[pl.ds(0, elements, stride=4), :]
        + cs_ref[pl.ds(1, elements, stride=4), :]
        + cs_ref[pl.ds(2, elements, stride=4), :]
        + cs_ref[pl.ds(3, elements, stride=4), :]
    ) * 0.25
    pushed[0:elements] = own

    def push(section):
        return pltpu.make_async_remote_copy(
            src_ref=pushed, dst_ref=given,
            send_sem=push_send_sem.at[section - 1], recv_sem=push_recv_sem,
            device_id=(section, right), device_id_type=MESH,
        )

    relays = (sec == 1) | (sec == 2)
    relay = pltpu.make_async_remote_copy(
        src_ref=given, dst_ref=given, send_sem=relay_sem, recv_sem=push_recv_sem,
        device_id=(sibling, col), device_id_type=MESH,
    )

    def push_arrives():
        relay.wait_recv()

        @pl.when(relays)
        def _():
            relay.start()

    means = pushed.at[pl.ds(0, elements)]
    to_left = pltpu.make_async_remote_copy(
        src_ref=means, dst_ref=beyond, send_sem=beyond_sem.at[0], recv_sem=beyond_sem.at[1],
        device_id=(sec, left), device_id_type=MESH,
    )

    @pl.when(jnp.logical_not(is_cloud))
    def _():
        pl.semaphore_wait(barrier, n_sec + 1)
        for section in (2, 1):
            push(section).start()

    def give(other, chip):
        return pltpu.make_async_remote_copy(
            src_ref=tend_send.at[other], dst_ref=tends.at[sec - 1, col],
            send_sem=tend_send_sem.at[chip], recv_sem=tend_recv_sem.at[sec - 1],
            device_id=(2 * chip + 1, other), device_id_type=MESH,
        )

    for fetch in fetches[3:7]:
        fetch.wait()

    place = iota((3 * elements, elements), 0)
    place = jnp.where(
        place < elements, place, jnp.where(place < 2 * elements, place + elements, place - elements)
    )
    near = jnp.where(place == elements + iota((3 * elements, elements), 1), -4.0, 0.0)
    relative = jnp.bitwise_and(nbr_ref[...] - (col - 1) * elements, total - 1)
    for k in range(4):
        near = near + jnp.where(relative[k : k + 1, :] == place, 1.0, 0.0)
    near_t = near.astype(BF16)

    cs = cs_ref[...]
    lane = jnp.bitwise_and(iota((rows, width), 1), levels_h - 1)
    upper = jnp.where(lane == levels_h - 1, cs, pltpu.roll(cs, width - 1, axis=1))
    lower = jnp.where(lane == 0, cs, pltpu.roll(cs, 1, axis=1))
    base = cs + VMIX * (upper + lower - 2.0 * cs)
    rate = rate_ref[...]

    square[...] = jnp.zeros_like(square)
    square[0:levels_c, 0:levels_h] = map_ref[...]
    square[levels_h : levels_h + levels_c, levels_h : 2 * levels_h] = map_ref[...]

    @pl.when(is_cloud)
    def _():
        chosen = iota((slots, rows), 0) + (sec - 1) * slots == slot.astype(I32)
        chosen32 = jnp.where(chosen, 1.0, 0.0)
        chosen16 = chosen32.astype(BF16)
        counts_out = jnp.sum(chosen32 * cnt_ref[...].astype(F32), axis=1, keepdims=True)
        repeat = jnp.where(
            iota((elements, rows), 0) == lax.shift_right_logical(iota((elements, rows), 1), 2), 1.0, 0.0
        ).astype(BF16)
        by_element = dot(chosen16, repeat, NT).astype(BF16)
        reach = dot(by_element, near_t, NT).astype(BF16)
        known = pick(chosen16, base) + rate * pick(reach[:, 2 * elements :], own)
        reach = reach[:, :elements]

        push_arrives()
        sent = known + rate * pick(reach, given[0:elements])
        slot_left = jnp.concatenate([given[elements + 4 : elements + 5], given[elements + 5 : elements + 6]], axis=1)
        chosen_left = jnp.where(
            iota((slots, rows), 0) + (sec - 1) * slots == slot_left.astype(I32), 1.0, 0.0
        ).astype(BF16)
        nbr_left = given[elements : elements + 4, 0:elements].astype(I32)
        here = iota((elements, elements), 0) + col * elements
        near_left = jnp.zeros((elements, elements), F32)
        for k in range(4):
            near_left = near_left + jnp.where(nbr_left[k : k + 1, :] == here, 1.0, 0.0)
        reach_left = dot(dot(chosen_left, repeat, NT).astype(BF16), near_left.astype(BF16), NT)
        extra = rate * pick(reach_left.astype(BF16), own)
        both = dot3(jnp.concatenate([sent, extra], axis=0), square[...], NT)
        target = jnp.where(iota((slots, width), 1) == levels_c, counts_out, both[:slots])
        disp_send[:, :, 0:width] = target.reshape(n_col, cap, width)
        disp_send[:, :, width:] = both[slots:].reshape(n_col, cap, width)

        pl.semaphore_wait(barrier, n_col + 1)
        def send(other):
            pltpu.make_async_remote_copy(
                src_ref=disp_send.at[other], dst_ref=disp_recv.at[col],
                send_sem=disp_send_sem, recv_sem=disp_recv_sem,
                device_id=(sec, other), device_id_type=MESH,
            ).start()

        for_others(col, send)
        pltpu.make_async_copy(disp_send.at[col], disp_recv.at[col], disp_recv_sem).start()
        to_left.start()

        fetches[7].wait()
        for f in range(2):
            parts[f, 8 * levels_c :] = jnp.zeros((8 * (levels_h - levels_c), slots), F32)

        def widen(z, carry):
            water = block[0, 1, z].astype(F32)
            for f, x in ((1, water), (0, block[0, 0, z].astype(F32) + LATENT * water)):
                plain[f][z] = x
                parts[f, pl.ds(8 * z, 8), :] = (x[0:8] + x[8:16]) + (x[16:24] + x[24:32])
            return carry

        lax.fori_loop(0, levels_c, widen, 0, unroll=UNROLL)

        def over_columns(f):
            return sum(parts[f, pl.ds(k, levels_h, stride=8), :] for k in range(8))

        def strided(ref, z):
            return tuple(ref[z, pl.ds(k, 8, stride=4), :] for k in range(4))

        def packed(ref, z):
            return tuple(ref[z, pl.ds(8 * k, 8), :] for k in range(4))

        def put_strided(ref, z, tiles):
            for k in range(4):
                ref[z, pl.ds(k, 8, stride=4), :] = tiles[k]

        def put_packed(ref, z, tiles):
            for k in range(4):
                ref[z, pl.ds(8 * k, 8), :] = tiles[k]

        def stencil(here, below, above, by_x, by_z):
            west = (pltpu.roll(here[3], 1, axis=0),) + here[:3]
            east = here[1:] + (pltpu.roll(here[0], 7, axis=0),)
            return tuple(
                here[k] + (by_x * (east[k] + west[k]) + by_z * (above[k] + below[k]))
                for k in range(4)
            )

        for f in range(2):

            def first(z, carry, f=f):
                below, here = carry
                above = strided(plain[f], jnp.minimum(z + 1, levels_c - 1))
                put_packed(
                    (energy_a, water_a)[f], z, stencil(here, below, above, HORIZ / CENTRE, VERTIC / CENTRE)
                )
                return here, above

            edge = strided(plain[f], 0)
            lax.fori_loop(0, levels_c, first, (edge, edge), unroll=UNROLL)

        columns_inv = 1.0 / across
        start = [over_columns(f) * columns_inv for f in range(2)]
        level = iota((levels_h, slots), 0)
        wet = jnp.concatenate([sat_ref[...], jnp.zeros((1, 128 - levels_c), F32)], axis=1)
        wet = jnp.transpose(jnp.broadcast_to(wet, (128, 128)))[:levels_h]

        def smoothed(x):
            up = jnp.where(level == levels_c - 1, x, pltpu.roll(x, levels_h - 1, axis=0))
            low = jnp.where(level == 0, x, pltpu.roll(x, 1, axis=0))
            return (1.0 - 2.0 * VERTIC) * x + VERTIC * (up + low)

        pltpu.make_async_copy(disp_recv, disp_recv, disp_recv_sem).wait()
        later = disp_recv[:, :, width:].reshape(slots, width)
        arrived = jnp.transpose(
            disp_recv[:, :, 0:width].reshape(slots, width) + pltpu.roll(later, slots - cap, axis=0)
        )
        counts = arrived[levels_c : levels_c + 1, :]
        counts8 = jnp.broadcast_to(counts, (8, slots))
        goal = [arrived[f * levels_h : (f + 1) * levels_h] for f in range(2)]
        goal[0] = goal[0] + LATENT * goal[1]
        mean = list(start)
        offset = [jnp.zeros((levels_h, slots), F32)] * 2

        for n in range(MAX_SUB):
            scale = CENTRE ** (n + 1)
            keep = counts > float(n)
            d = [RELAX * (goal[f] - mean[f]) for f in range(2)]
            moved = smoothed(mean[0] + d[0])
            shifted = [smoothed(offset[f] + d[f]) for f in range(2)]
            limit = (0.5 / scale) * (wet - shifted[1])
            limits[...] = limit if n == 0 else jnp.where(keep, limit, 0.0)

            def condense(water, z, by_half):
                bound = jnp.broadcast_to(limits[pl.ds(z, 1), :], (8, slots))
                new = [jnp.minimum(water[k], by_half * water[k] + bound) for k in range(4)]
                parts[1, pl.ds(8 * z, 8), :] = (new[0] + new[1]) + (new[2] + new[3])
                return new

            if n == 0:

                def finish(z, carry):
                    put_packed(water_b, z, condense(packed(water_a, z), z, 0.5))
                    return carry

                lax.fori_loop(0, levels_c, finish, 0, unroll=UNROLL)
            else:
                going = jnp.where(counts8 > float(n), 1.0, 0.0)
                by_x, by_z, by_half = going * (HORIZ / CENTRE), going * (VERTIC / CENTRE), 1.0 - going * 0.5
                old, fresh = (water_b, water_a) if n % 2 else (water_a, water_b)

                def sweep(z, carry, n=n, old=old, fresh=fresh, by_x=by_x, by_z=by_z, by_half=by_half):
                    below, here = carry
                    above = packed(old, jnp.minimum(z + 1, levels_c - 1))
                    new = condense(stencil(here, below, above, by_x, by_z), z, by_half)
                    if n == MAX_SUB - 1:
                        put_strided(plain_water, z, new)
                    else:
                        put_packed(fresh, z, new)
                    return here, above

                edge = packed(old, 0)
                lax.fori_loop(0, levels_c, sweep, (edge, edge), unroll=UNROLL)

            dried = over_columns(1) * (columns_inv * scale) + shifted[1]
            mean[0] = jnp.where(keep, moved, mean[0])
            mean[1] = jnp.where(keep, dried, mean[1])
            offset = [jnp.where(keep, shifted[f], offset[f]) for f in range(2)]

        gain = [jnp.where(level < levels_c, mean[f] - start[f], 0.0) for f in range(2)]
        change = jnp.concatenate([gain[0] - LATENT * gain[1], gain[1]], axis=0)
        tendency = dot3(jnp.transpose(change), square[...])
        tend_send[...] = tendency.reshape(n_col, cap, width)

        for chip in range(2):
            for_others(col, lambda other, chip=chip: give(other, chip).start())

            @pl.when(sec != 2 * chip + 1)
            def _():
                give(col, chip).start()

        @pl.when(core == 1)
        def _():
            pltpu.make_async_copy(tend_send.at[col], tends.at[sec - 1, col], tend_recv_sem.at[sec - 1]).start()

        for n in range(1, MAX_SUB):
            going = jnp.where(counts8 > float(n), 1.0, 0.0)
            by_x, by_z = going * (HORIZ / CENTRE), going * (VERTIC / CENTRE)

            old, fresh = (energy_a, energy_b) if n % 2 else (energy_b, energy_a)

            def follow(z, carry, n=n, old=old, fresh=fresh, by_x=by_x, by_z=by_z):
                below, here = carry
                above = packed(old, jnp.minimum(z + 1, levels_c - 1))
                new = stencil(here, below, above, by_x, by_z)
                if n == MAX_SUB - 1:
                    put_strided(plain_energy, z, new)
                else:
                    put_packed(fresh, z, new)
                return here, above

            edge = packed(old, 0)
            lax.fori_loop(0, levels_c, follow, (edge, edge), unroll=UNROLL)

        power = jnp.full((1, slots), CENTRE, F32)
        for n in range(1, MAX_SUB):
            power = jnp.where(counts > float(n), CENTRE ** (n + 1), power)
        used = jnp.broadcast_to(counts, (across, slots)) > 0.0
        power = jnp.broadcast_to(power, (across, slots))
        for f in range(2):
            offsets[f] = offset[f]

        def narrow(z, carry):
            x = [
                power * plain[f][z] + jnp.broadcast_to(offsets[f, pl.ds(z, 1), :], power.shape)
                for f in range(2)
            ]
            x[0] = x[0] - LATENT * x[1]
            for f in range(2):
                block[0, f, z] = jnp.where(used, x[f], block[0, f, z].astype(F32)).astype(BF16)
            return carry

        lax.fori_loop(0, levels_c, narrow, 0, unroll=UNROLL)

    @pl.when(jnp.logical_not(is_cloud))
    def _():
        push_arrives()
        to_left.start()
        fetches[7].wait()

    near_e = jnp.transpose(
        jnp.concatenate([near, jnp.zeros((3 * elements, 128 - elements), F32)], axis=1)
    )[:elements].astype(BF16)
    to_left.wait_recv()
    around = jnp.concatenate([given[0:elements], beyond[...], own], axis=0)
    spread = rate * pick(near_e, around)
    adv_ref[...] = base
    for k in range(4):
        adv_ref[pl.ds(k, elements, stride=4), :] += spread
    slot_column = jnp.transpose(jnp.broadcast_to(slot, (128, rows)))[:, 0:1]
    member = jnp.where(
        slot_column == iota((rows, (n_sec - 1) * slots), 1).astype(F32), 1.0, 0.0
    ).astype(BF16)

    def heard(source):
        pltpu.make_async_copy(tends.at[source], tends.at[source], tend_recv_sem.at[source]).wait()

    def passing(source):
        return pltpu.make_async_remote_copy(
            src_ref=tends.at[source], dst_ref=tends.at[source],
            send_sem=core_send_sem.at[source], recv_sem=core_recv_sem.at[source],
            device_id=(sibling, col), device_id_type=MESH,
        )

    @pl.when(core == 1)
    def _():
        for source in range(n_sec - 1):
            heard(source)
            passing(source).start()
        adv_ref[...] += pick(member, tends[...].reshape((n_sec - 1) * slots, width))

    @pl.when(core == 0)
    def _():
        for source in range(n_sec - 1):
            passing(source).wait_recv()
            found = tends[source].reshape(slots, width)
            adv_ref[...] += pick(member[:, source * slots : (source + 1) * slots], found)

    summed = adv_ref[...]
    out_ref[...] = jnp.where(
        iota((rows, width), 1) >= levels_h, jnp.maximum(summed, 0.0), summed
    )

    @pl.when(jnp.logical_not(is_cloud))
    def _():
        for section in (2, 1):
            push(section).wait_send()

    @pl.when(relays)
    def _():
        relay.wait_send()

    to_left.wait_send()

    @pl.when(core == 1)
    def _():
        for source in range(n_sec - 1):
            passing(source).wait_send()

    @pl.when(is_cloud)
    def _():
        others = pl.ds(0, n_col - 1)
        pltpu.make_async_copy(disp_send.at[others], disp_send.at[others], disp_send_sem).wait()
        for chip in range(2):
            pltpu.make_async_copy(tend_send.at[others], tend_send.at[others], tend_send_sem.at[chip]).wait()

            @pl.when(sec != 2 * chip + 1)
            def _():
                give(col, chip).wait_send()


def write(columns, cloud, columns_out, cloud_out, sem):
    copies = [
        pltpu.make_async_copy(cloud, cloud_out, sem.at[0]),
        pltpu.make_async_copy(columns, columns_out, sem.at[1]),
    ]
    for copy in copies:
        copy.start()
    for copy in copies:
        copy.wait()


def body(
    column_state, mixing_rate, neighbours, assignment, substeps, cloud_state, level_map, saturation
):
    n_sec, n_col = lax.axis_size("sec"), lax.axis_size("col")
    rows, width = column_state.shape
    elements = rows // 4
    _, fields, levels_c, across, slots = cloud_state.shape
    cap, levels_h = slots // n_col, level_map.shape[1]
    vmem = pl.BlockSpec(memory_space=pltpu.VMEM)
    hbm = pl.BlockSpec(memory_space=pltpu.HBM)
    message = (n_col, cap, width)
    dma = pltpu.SemaphoreType.DMA
    results = (
        jax.ShapeDtypeStruct(column_state.shape, F32),
        jax.ShapeDtypeStruct(cloud_state.shape, BF16),
    )
    operands = (
        column_state,
        mixing_rate.reshape(1, width),
        neighbours.T,
        assignment.reshape(1, rows),
        substeps.reshape(1, rows),
        cloud_state,
        level_map,
        saturation.reshape(1, levels_c),
    )
    columns, cloud = pl.pallas_call(
        functools.partial(kernel, (n_sec, n_col)),
        out_shape=tuple(pltpu.VMEM(r.shape, r.dtype) for r in results),
        in_specs=[hbm] * 8,
        out_specs=(vmem, vmem),
        scratch_shapes=[
            pltpu.VMEM((rows, width), F32),
            pltpu.VMEM((1, width), F32),
            pltpu.VMEM((4, elements), I32),
            pltpu.VMEM((1, rows), I32),
            pltpu.VMEM((1, rows), I32),
            pltpu.VMEM((levels_c, levels_h), F32),
            pltpu.VMEM((1, levels_c), F32),
            *[pltpu.VMEM((levels_c, across, slots), F32)] * 6,
            pltpu.VMEM((fields, 8 * levels_h, slots), F32),
            pltpu.VMEM((levels_h, slots), F32),
            pltpu.VMEM((fields, levels_h, slots), F32),
            pltpu.VMEM((fields * levels_h, fields * levels_h), F32),
            pltpu.VMEM((elements + 8, width), F32),
            pltpu.VMEM((elements + 8, width), F32),
            pltpu.VMEM((elements, width), F32),
            pltpu.VMEM((n_col, cap, 2 * width), F32),
            pltpu.VMEM((n_col, cap, 2 * width), F32),
            pltpu.VMEM(message, F32),
            pltpu.VMEM((n_sec - 1,) + message, F32),
            pltpu.VMEM((rows, width), F32),
            dma((8,)),
            dma((2,)),
            dma,
            dma,
            dma((2,)),
            dma,
            dma,
            dma((2,)),
            dma((n_sec - 1,)),
            dma((n_sec - 1,)),
            dma((n_sec - 1,)),
        ],
        compiler_params=pltpu.CompilerParams(
            collective_id=0, has_side_effects=True, vmem_limit_bytes=48 * 1024 * 1024
        ),
    )(*(pltpu.with_memory_space_constraint(x, pltpu.HBM) for x in operands))
    anywhere = pl.BlockSpec(memory_space=pl.ANY)
    return pl.pallas_call(
        write,
        out_shape=results,
        in_specs=[anywhere, anywhere],
        out_specs=(anywhere, anywhere),
        scratch_shapes=[dma((2,))],
        compiler_params=pltpu.CompilerParams(vmem_limit_bytes=1024 * 1024),
    )(columns, cloud)


def solution(mesh):
    in_specs = (
        P("col", None),
        P(),
        P("col", None),
        P("col", None),
        P("col"),
        P("sec", None, None, None, "col"),
        P(),
        P(),
    )
    out_specs = (P("col", None), P("sec", None, None, None, "col"))
    return jax.shard_map(body, mesh=mesh, in_specs=in_specs, out_specs=out_specs, check_vma=False)
```

```python
import functools

import jax
import jax.numpy as jnp
from jax import lax
from jax.experimental import pallas as pl
from jax.experimental.pallas import tpu as pltpu
from jax.sharding import PartitionSpec as P

MAX_SUB = 4
RELAX = 0.25
HORIZ = 0.12
VERTIC = 0.1
LATENT = 2.5
VMIX = 0.2
UNROLL = 29
CENTRE = 1.0 - 2.0 * HORIZ - 2.0 * VERTIC
MESH = pl.DeviceIdType.MESH
F32 = jnp.float32
BF16 = jnp.bfloat16
I32 = jnp.int32
NN = (((1,), (0,)), ((), ()))
NT = (((1,), (1,)), ((), ()))
ACROSS = ((2, 1), (1, 1), (3, 1), (2, 0), (0, 1), (1, 0), (3, 0), (0, 0))


def iota(shape, dim):
    return lax.broadcasted_iota(I32, shape, dim)


def halves(x):
    hi = x.astype(BF16)
    return hi, (x - hi.astype(F32)).astype(BF16)


def dot(a, b, dims=NN):
    return lax.dot_general(a, b, dims, preferred_element_type=F32)


def joined(lefts, rights, dims):
    (left_dims, right_dims), _ = dims
    return dot(
        jnp.concatenate(lefts, axis=left_dims[0]), jnp.concatenate(rights, axis=right_dims[0]), dims
    )


def pick(exact, x, dims=NN):
    hi, lo = halves(x)
    if exact.shape[1] % 128:
        return dot(exact, hi, dims) + dot(exact, lo, dims)
    return joined([exact, exact], [hi, lo], dims)


def dot3(x, y, dims=NN):
    xh, xl = halves(x)
    yh, yl = halves(y)
    return joined([xh, xh, xl], [yh, yl, yh], dims)


def for_others(col, visit):
    y, x, z = col // 16, lax.rem(col // 8, 2), lax.rem(col, 8)
    bases = [lax.rem(y + dy, 4) * 16 + lax.rem(x + dx, 2) * 8 for dy, dx in ACROSS]

    def ring(t, carry):
        half = (t + 1) // 2
        dz = 4 + half - 2 * half * lax.rem(t, 2)
        along = lax.rem(z + dz, 8)
        for base in bases:
            visit(base + along)
        return carry

    lax.fori_loop(0, 7, ring, 0)
    for base in bases[:-1]:
        visit(base + z)


def kernel(
    sizes,
    cs_hbm,
    rate_hbm,
    nbr_hbm,
    asg_hbm,
    cnt_hbm,
    cloud_hbm,
    map_hbm,
    sat_hbm,
    out_ref,
    block,
    cs_ref,
    rate_ref,
    nbr_ref,
    asg_ref,
    cnt_ref,
    map_ref,
    sat_ref,
    plain_energy,
    plain_water,
    energy_a,
    energy_b,
    water_a,
    water_b,
    parts,
    limits,
    offsets,
    square,
    pushed,
    given,
    beyond,
    disp_send,
    disp_recv,
    tend_send,
    tends,
    adv_ref,
    local_sem,
    push_send_sem,
    push_recv_sem,
    relay_sem,
    beyond_sem,
    disp_send_sem,
    disp_recv_sem,
    tend_send_sem,
    tend_recv_sem,
    core_send_sem,
    core_recv_sem,
):
    n_sec, n_col = sizes
    sec, col = lax.axis_index("sec"), lax.axis_index("col")
    rows, width = cs_ref.shape
    elements = rows // 4
    total = elements * n_col
    cap, slots = disp_send.shape[1], n_col * disp_send.shape[1]
    levels_c, levels_h = map_ref.shape
    left, right = lax.rem(col + n_col - 1, n_col), lax.rem(col + 1, n_col)
    is_cloud = sec > 0
    plain = (plain_energy, plain_water)
    across = plain_water.shape[1]
    core = lax.rem(sec, 2)
    sibling = sec + 1 - 2 * core
    facing = lax.rem(sec + 2, n_sec)

    fetches = [
        pltpu.make_async_copy(src, dst, local_sem.at[i])
        for i, (src, dst) in enumerate(
            (
                (asg_hbm, asg_ref),
                (nbr_hbm, nbr_ref),
                (cs_hbm, cs_ref),
                (rate_hbm, rate_ref),
                (map_hbm, map_ref),
                (cnt_hbm, cnt_ref),
                (sat_hbm, sat_ref),
                (cloud_hbm, block),
            )
        )
    ]
    for fetch in fetches:
        fetch.start()

    barrier = pltpu.get_barrier_semaphore()

    def greet(device):
        pl.semaphore_signal(barrier, inc=1, device_id=device, device_id_type=MESH)

    greet((0, left))

    @pl.when(is_cloud)
    def _():
        for_others(col, lambda other: greet((sec, other)))

    greet((sibling, col))

    @pl.when(core == 1)
    def _():
        greet((facing, col))

    @pl.when(sec == 1)
    def _():
        greet((2, col))

    fetches[0].wait()
    fetches[1].wait()

    asg = asg_ref[...]
    asg_column = jnp.transpose(jnp.broadcast_to(asg.astype(F32), (128, rows)))[:, 0:1]
    same = (asg_column == asg.astype(F32)) & (iota((rows, rows), 0) < iota((rows, rows), 1))
    rank = jnp.max(jnp.where(same, 1.0, 0.0), axis=0, keepdims=True)
    slot = (asg * cap).astype(F32) + rank

    pushed[elements : elements + 4, 0:elements] = nbr_ref[...].astype(F32)
    pushed[elements + 4 : elements + 5] = slot[:, :width]
    pushed[elements + 5 : elements + 6] = slot[:, width:]

    fetches[2].wait()
    own = (
        cs_ref[pl.ds(0, elements, stride=4), :]
        + cs_ref[pl.ds(1, elements, stride=4), :]
        + cs_ref[pl.ds(2, elements, stride=4), :]
        + cs_ref[pl.ds(3, elements, stride=4), :]
    ) * 0.25
    pushed[0:elements] = own

    def push(section):
        return pltpu.make_async_remote_copy(
            src_ref=pushed, dst_ref=given,
            send_sem=push_send_sem.at[section - 1], recv_sem=push_recv_sem,
            device_id=(section, right), device_id_type=MESH,
        )

    relays = (sec == 1) | (sec == 2)
    relay = pltpu.make_async_remote_copy(
        src_ref=given, dst_ref=given, send_sem=relay_sem, recv_sem=push_recv_sem,
        device_id=(sibling, col), device_id_type=MESH,
    )

    def push_arrives():
        relay.wait_recv()

        @pl.when(relays)
        def _():
            relay.start()

    means = pushed.at[pl.ds(0, elements)]
    to_left = pltpu.make_async_remote_copy(
        src_ref=means, dst_ref=beyond, send_sem=beyond_sem.at[0], recv_sem=beyond_sem.at[1],
        device_id=(sec, left), device_id_type=MESH,
    )

    @pl.when(jnp.logical_not(is_cloud))
    def _():
        pl.semaphore_wait(barrier, n_sec + 1)
        for section in (2, 1):
            push(section).start()

    def give(other, chip):
        return pltpu.make_async_remote_copy(
            src_ref=tend_send.at[other], dst_ref=tends.at[sec - 1, col],
            send_sem=tend_send_sem.at[chip], recv_sem=tend_recv_sem.at[sec - 1],
            device_id=(2 * chip + 1, other), device_id_type=MESH,
        )

    for fetch in fetches[3:7]:
        fetch.wait()

    place = iota((3 * elements, elements), 0)
    place = jnp.where(
        place < elements, place, jnp.where(place < 2 * elements, place + elements, place - elements)
    )
    near = jnp.where(place == elements + iota((3 * elements, elements), 1), -4.0, 0.0)
    relative = jnp.bitwise_and(nbr_ref[...] - (col - 1) * elements, total - 1)
    for k in range(4):
        near = near + jnp.where(relative[k : k + 1, :] == place, 1.0, 0.0)
    near_t = near.astype(BF16)

    cs = cs_ref[...]
    lane = jnp.bitwise_and(iota((rows, width), 1), levels_h - 1)
    upper = jnp.where(lane == levels_h - 1, cs, pltpu.roll(cs, width - 1, axis=1))
    lower = jnp.where(lane == 0, cs, pltpu.roll(cs, 1, axis=1))
    base = cs + VMIX * (upper + lower - 2.0 * cs)
    rate = rate_ref[...]

    square[...] = jnp.zeros_like(square)
    square[0:levels_c, 0:levels_h] = map_ref[...]
    square[levels_h : levels_h + levels_c, levels_h : 2 * levels_h] = map_ref[...]

    @pl.when(is_cloud)
    def _():
        chosen = iota((slots, rows), 0) + (sec - 1) * slots == slot.astype(I32)
        chosen32 = jnp.where(chosen, 1.0, 0.0)
        chosen16 = chosen32.astype(BF16)
        counts_out = jnp.sum(chosen32 * cnt_ref[...].astype(F32), axis=1, keepdims=True)
        repeat = jnp.where(
            iota((elements, rows), 0) == lax.shift_right_logical(iota((elements, rows), 1), 2), 1.0, 0.0
        ).astype(BF16)
        by_element = dot(chosen16, repeat, NT).astype(BF16)
        reach = dot(by_element, near_t, NT).astype(BF16)
        known = pick(chosen16, base) + rate * pick(reach[:, 2 * elements :], own)
        reach = reach[:, :elements]
        mapped = dot3(rate * own, square[...], NT)

        push_arrives()
        sent = known + rate * pick(reach, given[0:elements])
        slot_left = jnp.concatenate([given[elements + 4 : elements + 5], given[elements + 5 : elements + 6]], axis=1)
        chosen_left = jnp.where(
            iota((slots, rows), 0) + (sec - 1) * slots == slot_left.astype(I32), 1.0, 0.0
        ).astype(BF16)
        nbr_left = given[elements : elements + 4, 0:elements].astype(I32)
        here = iota((elements, elements), 0) + col * elements
        near_left = jnp.zeros((elements, elements), F32)
        for k in range(4):
            near_left = near_left + jnp.where(nbr_left[k : k + 1, :] == here, 1.0, 0.0)
        reach_left = dot(dot(chosen_left, repeat, NT).astype(BF16), near_left.astype(BF16), NT)
        extra = pick(reach_left.astype(BF16), mapped)
        target = dot3(sent, square[...], NT)
        target = jnp.where(iota((slots, width), 1) == levels_c, counts_out, target)
        disp_send[:, :, 0:width] = target.reshape(n_col, cap, width)
        disp_send[:, :, width:] = extra.reshape(n_col, cap, width)

        pl.semaphore_wait(barrier, n_col + 1)
        def send(other):
            pltpu.make_async_remote_copy(
                src_ref=disp_send.at[other], dst_ref=disp_recv.at[col],
                send_sem=disp_send_sem, recv_sem=disp_recv_sem,
                device_id=(sec, other), device_id_type=MESH,
            ).start()

        for_others(col, send)
        pltpu.make_async_copy(disp_send.at[col], disp_recv.at[col], disp_recv_sem).start()
        to_left.start()

        fetches[7].wait()
        for f in range(2):
            parts[f, 8 * levels_c :] = jnp.zeros((8 * (levels_h - levels_c), slots), F32)

        def widen(z, carry):
            water = block[0, 1, z].astype(F32)
            for f, x in ((1, water), (0, block[0, 0, z].astype(F32) + LATENT * water)):
                plain[f][z] = x
                parts[f, pl.ds(8 * z, 8), :] = (x[0:8] + x[8:16]) + (x[16:24] + x[24:32])
            return carry

        lax.fori_loop(0, levels_c, widen, 0, unroll=UNROLL)

        def over_columns(f):
            return sum(parts[f, pl.ds(k, levels_h, stride=8), :] for k in range(8))

        def strided(ref, z):
            return tuple(ref[z, pl.ds(k, 8, stride=4), :] for k in range(4))

        def packed(ref, z):
            return tuple(ref[z, pl.ds(8 * k, 8), :] for k in range(4))

        def put_strided(ref, z, tiles):
            for k in range(4):
                ref[z, pl.ds(k, 8, stride=4), :] = tiles[k]

        def put_packed(ref, z, tiles):
            for k in range(4):
                ref[z, pl.ds(8 * k, 8), :] = tiles[k]

        def stencil(here, below, above, by_x, by_z):
            west = (pltpu.roll(here[3], 1, axis=0),) + here[:3]
            east = here[1:] + (pltpu.roll(here[0], 7, axis=0),)
            return tuple(
                here[k] + (by_x * (east[k] + west[k]) + by_z * (above[k] + below[k]))
                for k in range(4)
            )

        for f in range(2):

            def first(z, carry, f=f):
                below, here = carry
                above = strided(plain[f], jnp.minimum(z + 1, levels_c - 1))
                put_packed(
                    (energy_a, water_a)[f], z, stencil(here, below, above, HORIZ / CENTRE, VERTIC / CENTRE)
                )
                return here, above

            edge = strided(plain[f], 0)
            lax.fori_loop(0, levels_c, first, (edge, edge), unroll=UNROLL)

        columns_inv = 1.0 / across
        start = [over_columns(f) * columns_inv for f in range(2)]
        level = iota((levels_h, slots), 0)
        wet = jnp.concatenate([sat_ref[...], jnp.zeros((1, 128 - levels_c), F32)], axis=1)
        wet = jnp.transpose(jnp.broadcast_to(wet, (128, 128)))[:levels_h]

        def smoothed(x):
            up = jnp.where(level == levels_c - 1, x, pltpu.roll(x, levels_h - 1, axis=0))
            low = jnp.where(level == 0, x, pltpu.roll(x, 1, axis=0))
            return (1.0 - 2.0 * VERTIC) * x + VERTIC * (up + low)

        untouched = [start[0]]
        for _ in range(MAX_SUB):
            untouched.append(smoothed(untouched[-1]))

        pltpu.make_async_copy(disp_recv, disp_recv, disp_recv_sem).wait()
        later = disp_recv[:, :, width:].reshape(slots, width)
        arrived = jnp.transpose(
            disp_recv[:, :, 0:width].reshape(slots, width) + pltpu.roll(later, slots - cap, axis=0)
        )
        counts = arrived[levels_c : levels_c + 1, :]
        counts8 = jnp.broadcast_to(counts, (8, slots))
        goal = [arrived[f * levels_h : (f + 1) * levels_h] for f in range(2)]
        goal[0] = goal[0] + LATENT * goal[1]
        mean = list(start)
        offset = [jnp.zeros((levels_h, slots), F32)] * 2

        for n in range(MAX_SUB):
            scale = CENTRE ** (n + 1)
            keep = counts > float(n)
            d = [RELAX * (goal[f] - mean[f]) for f in range(2)]
            shifted = [smoothed(offset[f] + d[f]) for f in range(2)]
            limit = (0.5 / scale) * (wet - shifted[1])
            limits[...] = limit if n == 0 else jnp.where(keep, limit, 0.0)

            def condense(water, z, by_half):
                bound = jnp.broadcast_to(limits[pl.ds(z, 1), :], (8, slots))
                new = [jnp.minimum(water[k], by_half * water[k] + bound) for k in range(4)]
                parts[1, pl.ds(8 * z, 8), :] = (new[0] + new[1]) + (new[2] + new[3])
                return new

            if n == 0:

                def finish(z, carry):
                    put_packed(water_b, z, condense(packed(water_a, z), z, 0.5))
                    return carry

                lax.fori_loop(0, levels_c, finish, 0, unroll=UNROLL)
            else:
                going = jnp.where(counts8 > float(n), 1.0, 0.0)
                by_x, by_z, by_half = going * (HORIZ / CENTRE), going * (VERTIC / CENTRE), 1.0 - going * 0.5
                old, fresh = (water_b, water_a) if n % 2 else (water_a, water_b)

                def sweep(z, carry, n=n, old=old, fresh=fresh, by_x=by_x, by_z=by_z, by_half=by_half):
                    below, here = carry
                    above = packed(old, jnp.minimum(z + 1, levels_c - 1))
                    new = condense(stencil(here, below, above, by_x, by_z), z, by_half)
                    if n == MAX_SUB - 1:
                        put_strided(plain_water, z, new)
                    else:
                        put_packed(fresh, z, new)
                    return here, above

                edge = packed(old, 0)
                lax.fori_loop(0, levels_c, sweep, (edge, edge), unroll=UNROLL)

            dried = over_columns(1) * (columns_inv * scale) + shifted[1]
            mean[0] = jnp.where(keep, untouched[n + 1] + shifted[0], mean[0])
            mean[1] = jnp.where(keep, dried, mean[1])
            offset = [jnp.where(keep, shifted[f], offset[f]) for f in range(2)]

        gain = [jnp.where(level < levels_c, mean[f] - start[f], 0.0) for f in range(2)]
        change = jnp.concatenate([gain[0] - LATENT * gain[1], gain[1]], axis=0)
        tendency = dot3(jnp.transpose(change), square[...])
        tend_send[...] = tendency.reshape(n_col, cap, width)

        for chip in range(2):
            for_others(col, lambda other, chip=chip: give(other, chip).start())

            @pl.when(sec != 2 * chip + 1)
            def _():
                give(col, chip).start()

        @pl.when(core == 1)
        def _():
            pltpu.make_async_copy(tend_send.at[col], tends.at[sec - 1, col], tend_recv_sem.at[sec - 1]).start()

        for n in range(1, MAX_SUB):
            going = jnp.where(counts8 > float(n), 1.0, 0.0)
            by_x, by_z = going * (HORIZ / CENTRE), going * (VERTIC / CENTRE)

            old, fresh = (energy_a, energy_b) if n % 2 else (energy_b, energy_a)

            def follow(z, carry, n=n, old=old, fresh=fresh, by_x=by_x, by_z=by_z):
                below, here = carry
                above = packed(old, jnp.minimum(z + 1, levels_c - 1))
                new = stencil(here, below, above, by_x, by_z)
                if n == MAX_SUB - 1:
                    put_strided(plain_energy, z, new)
                else:
                    put_packed(fresh, z, new)
                return here, above

            edge = packed(old, 0)
            lax.fori_loop(0, levels_c, follow, (edge, edge), unroll=UNROLL)

        power = jnp.full((1, slots), CENTRE, F32)
        for n in range(1, MAX_SUB):
            power = jnp.where(counts > float(n), CENTRE ** (n + 1), power)
        used = jnp.broadcast_to(counts, (across, slots)) > 0.0
        power = jnp.broadcast_to(power, (across, slots))
        for f in range(2):
            offsets[f] = offset[f]

        def narrow(z, carry):
            x = [
                power * plain[f][z] + jnp.broadcast_to(offsets[f, pl.ds(z, 1), :], power.shape)
                for f in range(2)
            ]
            x[0] = x[0] - LATENT * x[1]
            for f in range(2):
                block[0, f, z] = jnp.where(used, x[f], block[0, f, z].astype(F32)).astype(BF16)
            return carry

        lax.fori_loop(0, levels_c, narrow, 0, unroll=UNROLL)

    @pl.when(jnp.logical_not(is_cloud))
    def _():
        push_arrives()
        to_left.start()
        fetches[7].wait()

    near_e = jnp.transpose(
        jnp.concatenate([near, jnp.zeros((3 * elements, 128 - elements), F32)], axis=1)
    )[:elements].astype(BF16)
    to_left.wait_recv()
    around = jnp.concatenate([given[0:elements], beyond[...], own], axis=0)
    spread = rate * pick(near_e, around)
    adv_ref[...] = base
    for k in range(4):
        adv_ref[pl.ds(k, elements, stride=4), :] += spread
    slot_column = jnp.transpose(jnp.broadcast_to(slot, (128, rows)))[:, 0:1]
    member = jnp.where(
        slot_column == iota((rows, (n_sec - 1) * slots), 1).astype(F32), 1.0, 0.0
    ).astype(BF16)

    def heard(source):
        pltpu.make_async_copy(tends.at[source], tends.at[source], tend_recv_sem.at[source]).wait()

    def passing(source):
        return pltpu.make_async_remote_copy(
            src_ref=tends.at[source], dst_ref=tends.at[source],
            send_sem=core_send_sem.at[source], recv_sem=core_recv_sem.at[source],
            device_id=(sibling, col), device_id_type=MESH,
        )

    @pl.when(core == 1)
    def _():
        for source in range(n_sec - 1):
            heard(source)
            passing(source).start()
        adv_ref[...] += pick(member, tends[...].reshape((n_sec - 1) * slots, width))

    @pl.when(core == 0)
    def _():
        for source in range(n_sec - 1):
            passing(source).wait_recv()
            found = tends[source].reshape(slots, width)
            adv_ref[...] += pick(member[:, source * slots : (source + 1) * slots], found)

    summed = adv_ref[...]
    out_ref[...] = jnp.where(
        iota((rows, width), 1) >= levels_h, jnp.maximum(summed, 0.0), summed
    )

    @pl.when(jnp.logical_not(is_cloud))
    def _():
        for section in (2, 1):
            push(section).wait_send()

    @pl.when(relays)
    def _():
        relay.wait_send()

    to_left.wait_send()

    @pl.when(core == 1)
    def _():
        for source in range(n_sec - 1):
            passing(source).wait_send()

    @pl.when(is_cloud)
    def _():
        others = pl.ds(0, n_col - 1)
        pltpu.make_async_copy(disp_send.at[others], disp_send.at[others], disp_send_sem).wait()
        for chip in range(2):
            pltpu.make_async_copy(tend_send.at[others], tend_send.at[others], tend_send_sem.at[chip]).wait()

            @pl.when(sec != 2 * chip + 1)
            def _():
                give(col, chip).wait_send()


def write(columns, cloud, columns_out, cloud_out, sem):
    copies = [
        pltpu.make_async_copy(cloud, cloud_out, sem.at[0]),
        pltpu.make_async_copy(columns, columns_out, sem.at[1]),
    ]
    for copy in copies:
        copy.start()
    for copy in copies:
        copy.wait()


def body(
    column_state, mixing_rate, neighbours, assignment, substeps, cloud_state, level_map, saturation
):
    n_sec, n_col = lax.axis_size("sec"), lax.axis_size("col")
    rows, width = column_state.shape
    elements = rows // 4
    _, fields, levels_c, across, slots = cloud_state.shape
    cap, levels_h = slots // n_col, level_map.shape[1]
    vmem = pl.BlockSpec(memory_space=pltpu.VMEM)
    hbm = pl.BlockSpec(memory_space=pltpu.HBM)
    message = (n_col, cap, width)
    dma = pltpu.SemaphoreType.DMA
    results = (
        jax.ShapeDtypeStruct(column_state.shape, F32),
        jax.ShapeDtypeStruct(cloud_state.shape, BF16),
    )
    operands = (
        column_state,
        mixing_rate.reshape(1, width),
        neighbours.T,
        assignment.reshape(1, rows),
        substeps.reshape(1, rows),
        cloud_state,
        level_map,
        saturation.reshape(1, levels_c),
    )
    columns, cloud = pl.pallas_call(
        functools.partial(kernel, (n_sec, n_col)),
        out_shape=tuple(pltpu.VMEM(r.shape, r.dtype) for r in results),
        in_specs=[hbm] * 8,
        out_specs=(vmem, vmem),
        scratch_shapes=[
            pltpu.VMEM((rows, width), F32),
            pltpu.VMEM((1, width), F32),
            pltpu.VMEM((4, elements), I32),
            pltpu.VMEM((1, rows), I32),
            pltpu.VMEM((1, rows), I32),
            pltpu.VMEM((levels_c, levels_h), F32),
            pltpu.VMEM((1, levels_c), F32),
            *[pltpu.VMEM((levels_c, across, slots), F32)] * 6,
            pltpu.VMEM((fields, 8 * levels_h, slots), F32),
            pltpu.VMEM((levels_h, slots), F32),
            pltpu.VMEM((fields, levels_h, slots), F32),
            pltpu.VMEM((fields * levels_h, fields * levels_h), F32),
            pltpu.VMEM((elements + 8, width), F32),
            pltpu.VMEM((elements + 8, width), F32),
            pltpu.VMEM((elements, width), F32),
            pltpu.VMEM((n_col, cap, 2 * width), F32),
            pltpu.VMEM((n_col, cap, 2 * width), F32),
            pltpu.VMEM(message, F32),
            pltpu.VMEM((n_sec - 1,) + message, F32),
            pltpu.VMEM((rows, width), F32),
            dma((8,)),
            dma((2,)),
            dma,
            dma,
            dma((2,)),
            dma,
            dma,
            dma((2,)),
            dma((n_sec - 1,)),
            dma((n_sec - 1,)),
            dma((n_sec - 1,)),
        ],
        compiler_params=pltpu.CompilerParams(
            collective_id=0, has_side_effects=True, vmem_limit_bytes=48 * 1024 * 1024
        ),
    )(*(pltpu.with_memory_space_constraint(x, pltpu.HBM) for x in operands))
    anywhere = pl.BlockSpec(memory_space=pl.ANY)
    return pl.pallas_call(
        write,
        out_shape=results,
        in_specs=[anywhere, anywhere],
        out_specs=(anywhere, anywhere),
        scratch_shapes=[dma((2,))],
        compiler_params=pltpu.CompilerParams(vmem_limit_bytes=1024 * 1024),
    )(columns, cloud)


def solution(mesh):
    in_specs = (
        P("col", None),
        P(),
        P("col", None),
        P("col", None),
        P("col"),
        P("sec", None, None, None, "col"),
        P(),
        P(),
    )
    out_specs = (P("col", None), P("sec", None, None, None, "col"))
    return jax.shard_map(body, mesh=mesh, in_specs=in_specs, out_specs=out_specs, check_vma=False)
```

```python
import functools

import jax
import jax.numpy as jnp
from jax import lax
from jax.experimental import pallas as pl
from jax.experimental.pallas import tpu as pltpu
from jax.sharding import PartitionSpec as P

MAX_SUB = 4
RELAX = 0.25
HORIZ = 0.12
VERTIC = 0.1
LATENT = 2.5
VMIX = 0.2
UNROLL = 29
CENTRE = 1.0 - 2.0 * HORIZ - 2.0 * VERTIC
MESH = pl.DeviceIdType.MESH
F32 = jnp.float32
BF16 = jnp.bfloat16
I32 = jnp.int32
NN = (((1,), (0,)), ((), ()))
NT = (((1,), (1,)), ((), ()))
ACROSS = ((2, 1), (1, 1), (3, 1), (2, 0), (0, 1), (1, 0), (3, 0), (0, 0))


def iota(shape, dim):
    return lax.broadcasted_iota(I32, shape, dim)


def halves(x):
    hi = x.astype(BF16)
    return hi, (x - hi.astype(F32)).astype(BF16)


def dot(a, b, dims=NN):
    return lax.dot_general(a, b, dims, preferred_element_type=F32)


def joined(lefts, rights, dims):
    (left_dims, right_dims), _ = dims
    return dot(
        jnp.concatenate(lefts, axis=left_dims[0]), jnp.concatenate(rights, axis=right_dims[0]), dims
    )


def pick(exact, x, dims=NN):
    hi, lo = halves(x)
    if exact.shape[1] % 128:
        return dot(exact, hi, dims) + dot(exact, lo, dims)
    return joined([exact, exact], [hi, lo], dims)


def dot3(x, y, dims=NN):
    xh, xl = halves(x)
    yh, yl = halves(y)
    return joined([xh, xh, xl], [yh, yl, yh], dims)


def for_others(col, visit):
    y, x, z = col // 16, lax.rem(col // 8, 2), lax.rem(col, 8)
    bases = [lax.rem(y + dy, 4) * 16 + lax.rem(x + dx, 2) * 8 for dy, dx in ACROSS]

    def ring(t, carry):
        half = (t + 1) // 2
        dz = 4 + half - 2 * half * lax.rem(t, 2)
        along = lax.rem(z + dz, 8)
        for base in bases:
            visit(base + along)
        return carry

    lax.fori_loop(0, 7, ring, 0)
    for base in bases[:-1]:
        visit(base + z)


def kernel(
    sizes,
    cs_hbm,
    rate_hbm,
    nbr_hbm,
    asg_hbm,
    cnt_hbm,
    cloud_hbm,
    map_hbm,
    sat_hbm,
    out_ref,
    block,
    cs_ref,
    rate_ref,
    nbr_ref,
    asg_ref,
    cnt_ref,
    map_ref,
    sat_ref,
    plain_energy,
    plain_water,
    energy_a,
    energy_b,
    water_a,
    water_b,
    parts,
    limits,
    offsets,
    square,
    pushed,
    given,
    beyond,
    disp_send,
    disp_recv,
    tend_send,
    tends,
    adv_ref,
    local_sem,
    push_send_sem,
    push_recv_sem,
    relay_sem,
    beyond_sem,
    disp_send_sem,
    disp_recv_sem,
    tend_send_sem,
    tend_recv_sem,
    core_send_sem,
    core_recv_sem,
):
    n_sec, n_col = sizes
    sec, col = lax.axis_index("sec"), lax.axis_index("col")
    rows, width = cs_ref.shape
    elements = rows // 4
    total = elements * n_col
    cap, slots = disp_send.shape[1], n_col * disp_send.shape[1]
    levels_c, levels_h = map_ref.shape
    left, right = lax.rem(col + n_col - 1, n_col), lax.rem(col + 1, n_col)
    is_cloud = sec > 0
    plain = (plain_energy, plain_water)
    across = plain_water.shape[1]
    core = lax.rem(sec, 2)
    sibling = sec + 1 - 2 * core
    facing = lax.rem(sec + 2, n_sec)

    fetches = [
        pltpu.make_async_copy(src, dst, local_sem.at[i])
        for i, (src, dst) in enumerate(
            (
                (asg_hbm, asg_ref),
                (nbr_hbm, nbr_ref),
                (cs_hbm, cs_ref),
                (rate_hbm, rate_ref),
                (map_hbm, map_ref),
                (cnt_hbm, cnt_ref),
                (sat_hbm, sat_ref),
                (cloud_hbm, block),
            )
        )
    ]
    for fetch in fetches:
        fetch.start()

    barrier = pltpu.get_barrier_semaphore()

    def greet(device):
        pl.semaphore_signal(barrier, inc=1, device_id=device, device_id_type=MESH)

    greet((0, left))

    @pl.when(is_cloud)
    def _():
        for_others(col, lambda other: greet((sec, other)))

    greet((sibling, col))

    @pl.when(core == 1)
    def _():
        greet((facing, col))

    @pl.when(sec == 1)
    def _():
        greet((2, col))

    fetches[0].wait()
    fetches[1].wait()

    asg = asg_ref[...]
    asg_column = jnp.transpose(jnp.broadcast_to(asg.astype(F32), (128, rows)))[:, 0:1]
    same = (asg_column == asg.astype(F32)) & (iota((rows, rows), 0) < iota((rows, rows), 1))
    rank = jnp.max(jnp.where(same, 1.0, 0.0), axis=0, keepdims=True)
    slot = (asg * cap).astype(F32) + rank

    pushed[elements : elements + 4, 0:elements] = nbr_ref[...].astype(F32)
    pushed[elements + 4 : elements + 5] = slot[:, :width]
    pushed[elements + 5 : elements + 6] = slot[:, width:]

    fetches[2].wait()
    own = (
        cs_ref[pl.ds(0, elements, stride=4), :]
        + cs_ref[pl.ds(1, elements, stride=4), :]
        + cs_ref[pl.ds(2, elements, stride=4), :]
        + cs_ref[pl.ds(3, elements, stride=4), :]
    ) * 0.25
    pushed[0:elements] = own

    def push(section):
        return pltpu.make_async_remote_copy(
            src_ref=pushed, dst_ref=given,
            send_sem=push_send_sem.at[section - 1], recv_sem=push_recv_sem,
            device_id=(section, right), device_id_type=MESH,
        )

    relays = sec == 1
    relay = pltpu.make_async_remote_copy(
        src_ref=given, dst_ref=given, send_sem=relay_sem, recv_sem=push_recv_sem,
        device_id=(sibling, col), device_id_type=MESH,
    )

    def push_arrives():
        relay.wait_recv()

        @pl.when(relays)
        def _():
            relay.start()

    means = pushed.at[pl.ds(0, elements)]
    to_left = pltpu.make_async_remote_copy(
        src_ref=means, dst_ref=beyond, send_sem=beyond_sem.at[0], recv_sem=beyond_sem.at[1],
        device_id=(sec, left), device_id_type=MESH,
    )

    @pl.when(jnp.logical_not(is_cloud))
    def _():
        pl.semaphore_wait(barrier, n_sec + 1)
        for section in (2, 1, 3):
            push(section).start()

    def give(other, chip):
        return pltpu.make_async_remote_copy(
            src_ref=tend_send.at[other], dst_ref=tends.at[sec - 1, col],
            send_sem=tend_send_sem.at[chip], recv_sem=tend_recv_sem.at[sec - 1],
            device_id=(2 * chip + 1, other), device_id_type=MESH,
        )

    for fetch in fetches[3:7]:
        fetch.wait()

    place = iota((3 * elements, elements), 0)
    place = jnp.where(
        place < elements, place, jnp.where(place < 2 * elements, place + elements, place - elements)
    )
    near = jnp.where(place == elements + iota((3 * elements, elements), 1), -4.0, 0.0)
    relative = jnp.bitwise_and(nbr_ref[...] - (col - 1) * elements, total - 1)
    for k in range(4):
        near = near + jnp.where(relative[k : k + 1, :] == place, 1.0, 0.0)
    near_t = near.astype(BF16)

    cs = cs_ref[...]
    lane = jnp.bitwise_and(iota((rows, width), 1), levels_h - 1)
    upper = jnp.where(lane == levels_h - 1, cs, pltpu.roll(cs, width - 1, axis=1))
    lower = jnp.where(lane == 0, cs, pltpu.roll(cs, 1, axis=1))
    base = cs + VMIX * (upper + lower - 2.0 * cs)
    rate = rate_ref[...]

    square[...] = jnp.zeros_like(square)
    square[0:levels_c, 0:levels_h] = map_ref[...]
    square[levels_h : levels_h + levels_c, levels_h : 2 * levels_h] = map_ref[...]

    @pl.when(is_cloud)
    def _():
        chosen = iota((slots, rows), 0) + (sec - 1) * slots == slot.astype(I32)
        chosen32 = jnp.where(chosen, 1.0, 0.0)
        chosen16 = chosen32.astype(BF16)
        counts_out = jnp.sum(chosen32 * cnt_ref[...].astype(F32), axis=1, keepdims=True)
        repeat = jnp.where(
            iota((elements, rows), 0) == lax.shift_right_logical(iota((elements, rows), 1), 2), 1.0, 0.0
        ).astype(BF16)
        by_element = dot(chosen16, repeat, NT).astype(BF16)
        reach = dot(by_element, near_t, NT).astype(BF16)
        known = pick(chosen16, base) + rate * pick(reach[:, 2 * elements :], own)
        reach = reach[:, :elements]
        mapped = dot3(rate * own, square[...], NT)

        push_arrives()
        sent = known + rate * pick(reach, given[0:elements])
        slot_left = jnp.concatenate([given[elements + 4 : elements + 5], given[elements + 5 : elements + 6]], axis=1)
        chosen_left = jnp.where(
            iota((slots, rows), 0) + (sec - 1) * slots == slot_left.astype(I32), 1.0, 0.0
        ).astype(BF16)
        nbr_left = given[elements : elements + 4, 0:elements].astype(I32)
        here = iota((elements, elements), 0) + col * elements
        near_left = jnp.zeros((elements, elements), F32)
        for k in range(4):
            near_left = near_left + jnp.where(nbr_left[k : k + 1, :] == here, 1.0, 0.0)
        reach_left = dot(dot(chosen_left, repeat, NT).astype(BF16), near_left.astype(BF16), NT)
        extra = pick(reach_left.astype(BF16), mapped)
        target = dot3(sent, square[...], NT)
        target = jnp.where(iota((slots, width), 1) == levels_c, counts_out, target)
        disp_send[:, :, 0:width] = target.reshape(n_col, cap, width)
        disp_send[:, :, width:] = extra.reshape(n_col, cap, width)

        pl.semaphore_wait(barrier, n_col + 1)
        def send(other):
            pltpu.make_async_remote_copy(
                src_ref=disp_send.at[other], dst_ref=disp_recv.at[col],
                send_sem=disp_send_sem, recv_sem=disp_recv_sem,
                device_id=(sec, other), device_id_type=MESH,
            ).start()

        for_others(col, send)
        pltpu.make_async_copy(disp_send.at[col], disp_recv.at[col], disp_recv_sem).start()
        to_left.start()

        fetches[7].wait()
        for f in range(2):
            parts[f, 8 * levels_c :] = jnp.zeros((8 * (levels_h - levels_c), slots), F32)

        def widen(z, carry):
            water = block[0, 1, z].astype(F32)
            for f, x in ((1, water), (0, block[0, 0, z].astype(F32) + LATENT * water)):
                plain[f][z] = x
                parts[f, pl.ds(8 * z, 8), :] = (x[0:8] + x[8:16]) + (x[16:24] + x[24:32])
            return carry

        lax.fori_loop(0, levels_c, widen, 0, unroll=UNROLL)

        def over_columns(f):
            return sum(parts[f, pl.ds(k, levels_h, stride=8), :] for k in range(8))

        def strided(ref, z):
            return tuple(ref[z, pl.ds(k, 8, stride=4), :] for k in range(4))

        def packed(ref, z):
            return tuple(ref[z, pl.ds(8 * k, 8), :] for k in range(4))

        def put_strided(ref, z, tiles):
            for k in range(4):
                ref[z, pl.ds(k, 8, stride=4), :] = tiles[k]

        def put_packed(ref, z, tiles):
            for k in range(4):
                ref[z, pl.ds(8 * k, 8), :] = tiles[k]

        def stencil(here, below, above, by_x, by_z):
            west = (pltpu.roll(here[3], 1, axis=0),) + here[:3]
            east = here[1:] + (pltpu.roll(here[0], 7, axis=0),)
            return tuple(
                here[k] + (by_x * (east[k] + west[k]) + by_z * (above[k] + below[k]))
                for k in range(4)
            )

        for f in range(2):

            def first(z, carry, f=f):
                below, here = carry
                above = strided(plain[f], jnp.minimum(z + 1, levels_c - 1))
                put_packed(
                    (energy_a, water_a)[f], z, stencil(here, below, above, HORIZ / CENTRE, VERTIC / CENTRE)
                )
                return here, above

            edge = strided(plain[f], 0)
            lax.fori_loop(0, levels_c, first, (edge, edge), unroll=UNROLL)

        columns_inv = 1.0 / across
        start = [over_columns(f) * columns_inv for f in range(2)]
        level = iota((levels_h, slots), 0)
        wet = jnp.concatenate([sat_ref[...], jnp.zeros((1, 128 - levels_c), F32)], axis=1)
        wet = jnp.transpose(jnp.broadcast_to(wet, (128, 128)))[:levels_h]

        def smoothed(x):
            up = jnp.where(level == levels_c - 1, x, pltpu.roll(x, levels_h - 1, axis=0))
            low = jnp.where(level == 0, x, pltpu.roll(x, 1, axis=0))
            return (1.0 - 2.0 * VERTIC) * x + VERTIC * (up + low)

        untouched = [start[0]]
        for _ in range(MAX_SUB):
            untouched.append(smoothed(untouched[-1]))

        pltpu.make_async_copy(disp_recv, disp_recv, disp_recv_sem).wait()
        later = disp_recv[:, :, width:].reshape(slots, width)
        arrived = jnp.transpose(
            disp_recv[:, :, 0:width].reshape(slots, width) + pltpu.roll(later, slots - cap, axis=0)
        )
        counts = arrived[levels_c : levels_c + 1, :]
        counts8 = jnp.broadcast_to(counts, (8, slots))
        goal = [arrived[f * levels_h : (f + 1) * levels_h] for f in range(2)]
        goal[0] = goal[0] + LATENT * goal[1]
        mean = list(start)
        offset = [jnp.zeros((levels_h, slots), F32)] * 2

        for n in range(MAX_SUB):
            scale = CENTRE ** (n + 1)
            keep = counts > float(n)
            d = [RELAX * (goal[f] - mean[f]) for f in range(2)]
            shifted = [smoothed(offset[f] + d[f]) for f in range(2)]
            limit = (0.5 / scale) * (wet - shifted[1])
            limits[...] = limit if n == 0 else jnp.where(keep, limit, 0.0)

            def condense(water, z, by_half):
                bound = jnp.broadcast_to(limits[pl.ds(z, 1), :], (8, slots))
                new = [jnp.minimum(water[k], by_half * water[k] + bound) for k in range(4)]
                parts[1, pl.ds(8 * z, 8), :] = (new[0] + new[1]) + (new[2] + new[3])
                return new

            if n == 0:

                def finish(z, carry):
                    put_packed(water_b, z, condense(packed(water_a, z), z, 0.5))
                    return carry

                lax.fori_loop(0, levels_c, finish, 0, unroll=UNROLL)
            else:
                going = jnp.where(counts8 > float(n), 1.0, 0.0)
                by_x, by_z, by_half = going * (HORIZ / CENTRE), going * (VERTIC / CENTRE), 1.0 - going * 0.5
                old, fresh = (water_b, water_a) if n % 2 else (water_a, water_b)

                def sweep(z, carry, n=n, old=old, fresh=fresh, by_x=by_x, by_z=by_z, by_half=by_half):
                    below, here = carry
                    above = packed(old, jnp.minimum(z + 1, levels_c - 1))
                    new = condense(stencil(here, below, above, by_x, by_z), z, by_half)
                    if n == MAX_SUB - 1:
                        put_strided(plain_water, z, new)
                    else:
                        put_packed(fresh, z, new)
                    return here, above

                edge = packed(old, 0)
                lax.fori_loop(0, levels_c, sweep, (edge, edge), unroll=UNROLL)

            dried = over_columns(1) * (columns_inv * scale) + shifted[1]
            mean[0] = jnp.where(keep, untouched[n + 1] + shifted[0], mean[0])
            mean[1] = jnp.where(keep, dried, mean[1])
            offset = [jnp.where(keep, shifted[f], offset[f]) for f in range(2)]

        gain = [jnp.where(level < levels_c, mean[f] - start[f], 0.0) for f in range(2)]
        change = jnp.concatenate([gain[0] - LATENT * gain[1], gain[1]], axis=0)
        tendency = dot3(jnp.transpose(change), square[...])
        tend_send[...] = tendency.reshape(n_col, cap, width)

        for chip in range(2):
            for_others(col, lambda other, chip=chip: give(other, chip).start())

            @pl.when(sec != 2 * chip + 1)
            def _():
                give(col, chip).start()

        @pl.when(core == 1)
        def _():
            pltpu.make_async_copy(tend_send.at[col], tends.at[sec - 1, col], tend_recv_sem.at[sec - 1]).start()

        for n in range(1, MAX_SUB):
            going = jnp.where(counts8 > float(n), 1.0, 0.0)
            by_x, by_z = going * (HORIZ / CENTRE), going * (VERTIC / CENTRE)

            old, fresh = (energy_a, energy_b) if n % 2 else (energy_b, energy_a)

            def follow(z, carry, n=n, old=old, fresh=fresh, by_x=by_x, by_z=by_z):
                below, here = carry
                above = packed(old, jnp.minimum(z + 1, levels_c - 1))
                new = stencil(here, below, above, by_x, by_z)
                if n == MAX_SUB - 1:
                    put_strided(plain_energy, z, new)
                else:
                    put_packed(fresh, z, new)
                return here, above

            edge = packed(old, 0)
            lax.fori_loop(0, levels_c, follow, (edge, edge), unroll=UNROLL)

        power = jnp.full((1, slots), CENTRE, F32)
        for n in range(1, MAX_SUB):
            power = jnp.where(counts > float(n), CENTRE ** (n + 1), power)
        used = jnp.broadcast_to(counts, (across, slots)) > 0.0
        power = jnp.broadcast_to(power, (across, slots))
        for f in range(2):
            offsets[f] = offset[f]

        def narrow(z, carry):
            x = [
                power * plain[f][z] + jnp.broadcast_to(offsets[f, pl.ds(z, 1), :], power.shape)
                for f in range(2)
            ]
            x[0] = x[0] - LATENT * x[1]
            for f in range(2):
                block[0, f, z] = jnp.where(used, x[f], block[0, f, z].astype(F32)).astype(BF16)
            return carry

        lax.fori_loop(0, levels_c, narrow, 0, unroll=UNROLL)

    @pl.when(jnp.logical_not(is_cloud))
    def _():
        push_arrives()
        to_left.start()
        fetches[7].wait()

    near_e = jnp.transpose(
        jnp.concatenate([near, jnp.zeros((3 * elements, 128 - elements), F32)], axis=1)
    )[:elements].astype(BF16)
    to_left.wait_recv()
    around = jnp.concatenate([given[0:elements], beyond[...], own], axis=0)
    spread = rate * pick(near_e, around)
    adv_ref[...] = base
    for k in range(4):
        adv_ref[pl.ds(k, elements, stride=4), :] += spread
    slot_column = jnp.transpose(jnp.broadcast_to(slot, (128, rows)))[:, 0:1]
    member = jnp.where(
        slot_column == iota((rows, (n_sec - 1) * slots), 1).astype(F32), 1.0, 0.0
    ).astype(BF16)

    def heard(source):
        pltpu.make_async_copy(tends.at[source], tends.at[source], tend_recv_sem.at[source]).wait()

    def passing(source):
        return pltpu.make_async_remote_copy(
            src_ref=tends.at[source], dst_ref=tends.at[source],
            send_sem=core_send_sem.at[source], recv_sem=core_recv_sem.at[source],
            device_id=(sibling, col), device_id_type=MESH,
        )

    @pl.when(core == 1)
    def _():
        for source in range(n_sec - 1):
            heard(source)
            passing(source).start()
        adv_ref[...] += pick(member, tends[...].reshape((n_sec - 1) * slots, width))

    @pl.when(core == 0)
    def _():
        for source in range(n_sec - 1):
            passing(source).wait_recv()
            found = tends[source].reshape(slots, width)
            adv_ref[...] += pick(member[:, source * slots : (source + 1) * slots], found)

    summed = adv_ref[...]
    out_ref[...] = jnp.where(
        iota((rows, width), 1) >= levels_h, jnp.maximum(summed, 0.0), summed
    )

    @pl.when(jnp.logical_not(is_cloud))
    def _():
        for section in (2, 1, 3):
            push(section).wait_send()

    @pl.when(relays)
    def _():
        relay.wait_send()

    to_left.wait_send()

    @pl.when(core == 1)
    def _():
        for source in range(n_sec - 1):
            passing(source).wait_send()

    @pl.when(is_cloud)
    def _():
        others = pl.ds(0, n_col - 1)
        pltpu.make_async_copy(disp_send.at[others], disp_send.at[others], disp_send_sem).wait()
        for chip in range(2):
            pltpu.make_async_copy(tend_send.at[others], tend_send.at[others], tend_send_sem.at[chip]).wait()

            @pl.when(sec != 2 * chip + 1)
            def _():
                give(col, chip).wait_send()


def write(columns, cloud, columns_out, cloud_out, sem):
    copies = [
        pltpu.make_async_copy(cloud, cloud_out, sem.at[0]),
        pltpu.make_async_copy(columns, columns_out, sem.at[1]),
    ]
    for copy in copies:
        copy.start()
    for copy in copies:
        copy.wait()


def body(
    column_state, mixing_rate, neighbours, assignment, substeps, cloud_state, level_map, saturation
):
    n_sec, n_col = lax.axis_size("sec"), lax.axis_size("col")
    rows, width = column_state.shape
    elements = rows // 4
    _, fields, levels_c, across, slots = cloud_state.shape
    cap, levels_h = slots // n_col, level_map.shape[1]
    vmem = pl.BlockSpec(memory_space=pltpu.VMEM)
    hbm = pl.BlockSpec(memory_space=pltpu.HBM)
    message = (n_col, cap, width)
    dma = pltpu.SemaphoreType.DMA
    results = (
        jax.ShapeDtypeStruct(column_state.shape, F32),
        jax.ShapeDtypeStruct(cloud_state.shape, BF16),
    )
    operands = (
        column_state,
        mixing_rate.reshape(1, width),
        neighbours.T,
        assignment.reshape(1, rows),
        substeps.reshape(1, rows),
        cloud_state,
        level_map,
        saturation.reshape(1, levels_c),
    )
    columns, cloud = pl.pallas_call(
        functools.partial(kernel, (n_sec, n_col)),
        out_shape=tuple(pltpu.VMEM(r.shape, r.dtype) for r in results),
        in_specs=[hbm] * 8,
        out_specs=(vmem, vmem),
        scratch_shapes=[
            pltpu.VMEM((rows, width), F32),
            pltpu.VMEM((1, width), F32),
            pltpu.VMEM((4, elements), I32),
            pltpu.VMEM((1, rows), I32),
            pltpu.VMEM((1, rows), I32),
            pltpu.VMEM((levels_c, levels_h), F32),
            pltpu.VMEM((1, levels_c), F32),
            *[pltpu.VMEM((levels_c, across, slots), F32)] * 6,
            pltpu.VMEM((fields, 8 * levels_h, slots), F32),
            pltpu.VMEM((levels_h, slots), F32),
            pltpu.VMEM((fields, levels_h, slots), F32),
            pltpu.VMEM((fields * levels_h, fields * levels_h), F32),
            pltpu.VMEM((elements + 8, width), F32),
            pltpu.VMEM((elements + 8, width), F32),
            pltpu.VMEM((elements, width), F32),
            pltpu.VMEM((n_col, cap, 2 * width), F32),
            pltpu.VMEM((n_col, cap, 2 * width), F32),
            pltpu.VMEM(message, F32),
            pltpu.VMEM((n_sec - 1,) + message, F32),
            pltpu.VMEM((rows, width), F32),
            dma((8,)),
            dma((3,)),
            dma,
            dma,
            dma((2,)),
            dma,
            dma,
            dma((2,)),
            dma((n_sec - 1,)),
            dma((n_sec - 1,)),
            dma((n_sec - 1,)),
        ],
        compiler_params=pltpu.CompilerParams(
            collective_id=0, has_side_effects=True, vmem_limit_bytes=48 * 1024 * 1024
        ),
    )(*(pltpu.with_memory_space_constraint(x, pltpu.HBM) for x in operands))
    anywhere = pl.BlockSpec(memory_space=pl.ANY)
    return pl.pallas_call(
        write,
        out_shape=results,
        in_specs=[anywhere, anywhere],
        out_specs=(anywhere, anywhere),
        scratch_shapes=[dma((2,))],
        compiler_params=pltpu.CompilerParams(vmem_limit_bytes=1024 * 1024),
    )(columns, cloud)


def solution(mesh):
    in_specs = (
        P("col", None),
        P(),
        P("col", None),
        P("col", None),
        P("col"),
        P("sec", None, None, None, "col"),
        P(),
        P(),
    )
    out_specs = (P("col", None), P("sec", None, None, None, "col"))
    return jax.shard_map(body, mesh=mesh, in_specs=in_specs, out_specs=out_specs, check_vma=False)
```
